32 devices in a mesh: grp: 4 (over y, x), dev: 8 (over z, core).
Axes of the slice: x: 2, y: 2, z: 4, core: 2. Of those that a mesh axis runs over, the one named last changes fastest.
Arguments:
- integral_slabs: bfloat16 [8, 512, 512], P('dev'), may hold values from -6 to 6
- slab_owner: int32 [8], replicated, may hold values from 0 to 7, each once
- pair_orbs: int32 [256, 2], P(('grp', 'dev')), may hold values from 0 to 7, all different within a row; in each aligned block of 8 rows (0 to 7, 8 to 15, ...) at most 2 rows name the same one
- domain_bases: bfloat16 [256, 512, 128], P(('grp', 'dev')), may hold values from -0.25 to 0.25
- amplitudes: bfloat16 [256, 128, 128], P(('grp', 'dev')), may hold values from -6 to 6
- coupled: int32 [256, 32], P(('grp', 'dev')), may hold values from 0 to 31
- coupled_len: int32 [256], P(('grp', 'dev')), may hold values from 1 to 32, as said below
Outputs:
- residual: float32 [256, 128, 128], P(('grp', 'dev'))
The draws below stay inside these ranges and needn't reach their ends.
Inputs may be any that keep to these rules, and one draw needn't show every extreme that they name: `slab_owner`: a permutation of the positions. `pair_orbs`: the two orbitals of a pair differ; among the pairs of one device no orbital is named more than 2 times. `coupled_len`: pair 0 uses all 32 slots.
All inputs are finite; a program needn't handle non-finite values.
Results may differ from the reference program's by a relative error of at most 0.005.
Values may be sent and summed in bfloat16 or wider, within the bound.
No kernel may reach another device: no remote copies, remote signals or barrier semaphores. Data moves between devices by JAX's collectives and lax.ppermute only.
A program may use at most 128 MiB of HBM per device.

```python
import math
import jax
import jax.numpy as jnp
import numpy as np
from jax import lax

NAUX = 512
NORB = 512
NPNO = 128
P_DEV = 8
NCPL = 32
NOCC = 8
NPAIR = 256
CAP = 2
N_GRP = 4
N_DEV = 8


def draw_coupled_len(key, part):
    listed = jax.random.randint(key, (NPAIR,), 1, NCPL + 1)
    return listed.at[0].set(NCPL).astype(jnp.int32)


def with_ends(drawn, key, low, high):
    longest = drawn.shape.index(max(drawn.shape))
    spots = []
    for shift in (0, 1):
        where = [jax.random.randint(jax.random.fold_in(key, axis), (), 0, length) for axis, length in enumerate(drawn.shape)]
        where[longest] = (where[longest] + shift) % drawn.shape[longest]
        spots.append(tuple(where))
    return drawn.at[spots[0]].set(low).at[spots[1]].set(high)


def shard_levels(rng, extent, cuts, least, high):
    def one(dim, blocks):
        draws = jax.random.uniform(jax.random.fold_in(jax.random.fold_in(rng, 6), dim), (blocks,), jnp.float32, least / len(cuts), high / len(cuts))
        return jnp.repeat(jnp.exp(draws), extent[dim] // blocks).reshape((-1,) + (1,) * (len(extent) - dim - 1))

    gain = one(*cuts[0])
    for cut in cuts[1:]:
        gain = gain * one(*cut)
    return gain


def shared_out(own_key, own, number, rows, count, top, bound, skew):
    ranking = jax.random.permutation(own_key, count)
    crowded, common = shares(count, rows * top, bound, skew, True), shares(count, rows * top, bound, skew, False)
    places = jnp.arange(count)

    def named(tallies, rotation):
        used = int((tallies > 0).sum())
        fixed = max(1, used // 4)
        shifted = fixed + (places - fixed + rotation * (used - fixed)) % max(1, count - fixed)
        return jnp.zeros((count,), jnp.int32).at[ranking[jnp.where(places < fixed, places, shifted)]].set(jnp.asarray(tallies, jnp.int32))

    tallies = jnp.where(number % 4 == 0, named(crowded, number // 4), named(common, number - number // 4 - 1))
    mixed = jax.random.permutation(jax.random.fold_in(own, 3), count)
    source_of, receiver = mixed[0:count // 2 * 2:2], mixed[1:count // 2 * 2:2]
    margin = jnp.minimum(tallies[source_of] - 1, bound - tallies[receiver]) // 2
    margin = jnp.where((source_of == ranking[0]) | (receiver == ranking[0]) | (tallies[receiver] == 0), 0, jnp.maximum(margin, 0))
    shifted = jax.random.randint(jax.random.fold_in(own, 4), (count // 2,), 0, 1 << 20) % (margin + 1)
    tallies = tallies.at[source_of].add(-shifted).at[receiver].add(shifted)
    labels = jnp.searchsorted(jnp.cumsum(tallies), jnp.arange(rows * top), side="right").astype(jnp.int32)
    listing = labels.reshape(top, rows).T
    listing = listing[jax.random.permutation(jax.random.fold_in(own, 1), rows)]
    rotation = jax.random.randint(jax.random.fold_in(own, 2), (rows, 1), 0, top)
    return jnp.take_along_axis(listing, (jnp.arange(top)[None, :] + rotation) % top, axis=1)


def shares(number_of, total, bound, skew, full):
    portions = [(1 << 20) // math.isqrt(standing ** skew) + 1 for standing in range(1, number_of + 1)]
    largest = bound if full else min(bound, max(-(-total // number_of), total * portions[0] // sum(portions)))
    least = 1 if total - largest >= number_of - 1 else 0
    holding, surplus = [largest] + [least] * (number_of - 1), total - largest - least * (number_of - 1)
    while surplus > 0:
        movable = [i for i in range(1, number_of) if holding[i] < largest] or [i for i in range(1, number_of) if holding[i] < bound]
        mass, left = sum([portions[i] for i in movable]), surplus
        for i in movable:
            more = min(bound - holding[i], max(1, left * portions[i] // mass), surplus)
            holding[i] = holding[i] + more
            surplus = surplus - more
    return np.array(holding)


def centred(stream_key, shape, spread, bound, shards=(), kind=jnp.bfloat16):
    values = spread * jax.random.normal(stream_key, shape, jnp.float32)
    if shards:
        values = values * shard_levels(stream_key, shape, shards, -0.22, 0.18)
    return jnp.clip(values, -bound, bound).astype(kind)


def setup_inputs(seed: int = 0) -> dict:
    keys = jax.random.split(jax.random.key(seed), 8)
    integral_slabs = centred(keys[0], (NOCC, NAUX, NORB), 1.0, 6.0, ((0, 8),))
    slab_owner = jax.random.permutation(keys[1], NOCC).astype(jnp.int32)
    pair_orbs_keys = jax.random.split(jax.random.fold_in(keys[2], 1), NPAIR // P_DEV)
    pair_orbs_turns = jax.random.permutation(jax.random.fold_in(keys[2], 3), NPAIR // P_DEV)
    pair_orbs = jax.vmap(lambda own, number: shared_out(jax.random.fold_in(keys[2], 2), own, number, P_DEV, NOCC, 2, CAP, 0))(pair_orbs_keys, pair_orbs_turns).reshape((NPAIR, 2))
    domain_bases = centred(keys[3], (NPAIR, NORB, NPNO), NORB ** -0.5, 0.25, ((0, 32),))
    amplitudes = centred(keys[4], (NPAIR, NPNO, NPNO), 1.0, 6.0, ((0, 32),))
    coupled = with_ends(jax.random.randint(keys[5], (NPAIR, NCPL), 0, N_GRP * P_DEV), jax.random.fold_in(keys[5], 1), 0, (N_GRP * P_DEV) - 1).astype(jnp.int32)
    coupled_len = draw_coupled_len(jax.random.fold_in(keys[7], 71), 0)
    return {"integral_slabs": integral_slabs, "slab_owner": slab_owner, "pair_orbs": pair_orbs, "domain_bases": domain_bases, "amplitudes": amplitudes, "coupled": coupled, "coupled_len": coupled_len}


def reference(integral_slabs, slab_owner, pair_orbs, domain_bases, amplitudes, coupled, coupled_len):
    pair_total = domain_bases.shape[0]
    pair_ids = jnp.arange(pair_total, dtype=jnp.int32)
    owner_device = pair_ids // P_DEV % N_DEV
    global_pairs = ((coupled // P_DEV * N_DEV + owner_device[:, None]) * P_DEV + coupled % P_DEV).astype(jnp.int32)
    inverse_root = 1.0 / math.sqrt(NAUX)

    def one_pair(pair_index):
        domain_basis = domain_bases[pair_index]
        first_slab = integral_slabs[slab_owner[pair_orbs[pair_index, 0]]]
        second_slab = integral_slabs[slab_owner[pair_orbs[pair_index, 1]]]
        half_left = jnp.dot(first_slab, domain_basis, preferred_element_type=jnp.float32).astype(jnp.bfloat16)
        half_right = jnp.dot(second_slab, domain_basis, preferred_element_type=jnp.float32).astype(jnp.bfloat16)
        exchange = jnp.dot(half_left.T, half_right, preferred_element_type=jnp.float32) * inverse_root
        chosen = global_pairs[pair_index]
        chosen_bases = domain_bases[chosen].astype(jnp.float32)
        chosen_amps = amplitudes[chosen].astype(jnp.float32)
        intersection = jnp.einsum('ra,krb->kab', domain_basis.astype(jnp.float32), chosen_bases).astype(jnp.bfloat16)
        projected = jnp.einsum('kab,kbc->kac', intersection.astype(jnp.float32), chosen_amps).astype(jnp.bfloat16)
        coupled_terms = jnp.einsum('kac,kdc->kad', projected.astype(jnp.float32), intersection.astype(jnp.float32))
        weights = (jnp.arange(NCPL) < coupled_len[pair_index]).astype(jnp.float32)
        coupled_sum = jnp.einsum('k,kad->ad', weights, coupled_terms)
        return exchange + NORB / NPNO * coupled_sum
    return lax.map(one_pair, pair_ids)
```

```python
import functools
import math

import jax
import jax.numpy as jnp
from jax import lax
from jax.experimental import pallas as pl
from jax.experimental.pallas import tpu as pltpu
from jax.sharding import PartitionSpec as P

VMEM_LIMIT = 48 * 1024 * 1024


def coupled_kernel(start_ref, weight_ref, own_ref, cand_ref, acc_ref, out_ref, inter_ref, proj_ref):
    pairs, pno, _ = out_ref.shape
    orbs = own_ref.shape[1]
    cands = cand_ref.shape[0]
    first = start_ref[0]
    empty = jnp.zeros((pno, pno), jnp.bfloat16)
    for j in range(0, cands, 2):
        bases = jnp.concatenate([cand_ref[j, :orbs, :], cand_ref[j + 1, :orbs, :]], axis=1)
        inter = jnp.dot(own_ref[...], bases, preferred_element_type=jnp.float32).astype(jnp.bfloat16)
        inter_ref[:, j * pno : (j + 2) * pno] = inter
        amps = jnp.concatenate(
            [
                jnp.concatenate([cand_ref[j, orbs:, :], empty], axis=1),
                jnp.concatenate([empty, cand_ref[j + 1, orbs:, :]], axis=1),
            ],
            axis=0,
        )
        proj = jnp.dot(inter, amps, preferred_element_type=jnp.float32)
        for p in range(pairs):
            for c in range(2):
                block = proj[p * pno : (p + 1) * pno, c * pno : (c + 1) * pno]
                proj_ref[p * pno : (p + 1) * pno, (j + c) * pno : (j + c + 1) * pno] = (
                    block * weight_ref[p, first + j + c]
                ).astype(jnp.bfloat16)
    for p in range(pairs):
        rows = slice(p * pno, (p + 1) * pno)
        out_ref[p] = acc_ref[p] + lax.dot_general(
            proj_ref[rows, :], inter_ref[rows, :], (((1,), (1,)), ((), ())), preferred_element_type=jnp.float32
        )


def add_coupled(start, weights, own_t, cands, acc):
    pairs, pno, _ = acc.shape
    rows, orbs = own_t.shape
    count = cands.shape[0]
    smem = pl.BlockSpec(memory_space=pltpu.SMEM)
    vmem = pl.BlockSpec(memory_space=pltpu.VMEM)
    flops = 2 * rows * count * pno * (orbs + 2 * pno)
    return pl.pallas_call(
        coupled_kernel,
        out_shape=jax.ShapeDtypeStruct(acc.shape, jnp.float32),
        in_specs=[smem, smem, vmem, vmem, vmem],
        out_specs=vmem,
        scratch_shapes=[pltpu.VMEM((rows, count * pno), jnp.bfloat16)] * 2,
        compiler_params=pltpu.CompilerParams(vmem_limit_bytes=VMEM_LIMIT),
        cost_estimate=pl.CostEstimate(
            flops=flops,
            bytes_accessed=own_t.size * 2 + cands.size * 2 + acc.size * 8,
            transcendentals=0,
        ),
        name="coupled",
    )(start, weights, own_t, cands, acc)


def exchange_kernel(scale, place_ref, slab_ref, base_ref, acc_ref, out_ref):
    def one_pair(p, carry):
        basis = base_ref[p]
        left = jnp.dot(slab_ref[place_ref[p, 0]], basis, preferred_element_type=jnp.float32).astype(jnp.bfloat16)
        right = jnp.dot(slab_ref[place_ref[p, 1]], basis, preferred_element_type=jnp.float32).astype(jnp.bfloat16)
        product = lax.dot_general(left, right, (((0,), (0,)), ((), ())), preferred_element_type=jnp.float32)
        out_ref[p] = acc_ref[p] + product * scale
        return carry

    lax.fori_loop(0, out_ref.shape[0], one_pair, 0)


def add_exchange(places, slabs, bases, acc):
    aux = slabs.shape[1]
    smem = pl.BlockSpec(memory_space=pltpu.SMEM)
    vmem = pl.BlockSpec(memory_space=pltpu.VMEM)
    return pl.pallas_call(
        functools.partial(exchange_kernel, 1.0 / math.sqrt(aux)),
        out_shape=jax.ShapeDtypeStruct(acc.shape, jnp.float32),
        in_specs=[smem, vmem, vmem, vmem],
        out_specs=vmem,
        compiler_params=pltpu.CompilerParams(vmem_limit_bytes=VMEM_LIMIT),
        cost_estimate=pl.CostEstimate(
            flops=4 * bases.size * aux + 2 * acc.size * aux,
            bytes_accessed=slabs.size * 2 + bases.size * 2 + acc.size * 8,
            transcendentals=0,
        ),
        name="exchange",
    )(places, slabs, bases, acc)


def gather_slabs(own, n_dev):
    chips = n_dev // 2
    if chips != 4:
        return lax.all_gather(own, "dev", axis=0, tiled=False)

    def hop(value, moves):
        pairs = [(a * 2 + core, b * 2 + core) for a, b in moves for core in range(2)]
        return lax.ppermute(value, "dev", pairs)

    me = lax.axis_index("dev")
    chip, core = me // 2, me % 2
    up1 = hop(own, [(0, 1), (1, 2), (2, 3)])
    down1 = hop(own, [(1, 0), (2, 1), (3, 2)])
    up2 = hop(up1, [(1, 2), (2, 3)])
    down2 = hop(down1, [(2, 1), (1, 0)])
    far2 = jnp.where(chip >= 2, up2, down2)
    far3 = hop(far2, [(2, 3), (1, 0)])
    before = jnp.where(chip == 0, far3, up1)
    after = jnp.where(chip == chips - 1, far3, down1)
    mine = jnp.stack([own, after, far2, before])
    other = lax.ppermute(mine, "dev", [(d, d ^ 1) for d in range(n_dev)])
    order = (jnp.arange(chips) - chip) % chips
    mine, other = mine[order], other[order]
    even = jnp.where(core == 0, mine, other)
    odd = jnp.where(core == 0, other, mine)
    return jnp.stack([even, odd], axis=1).reshape((n_dev,) + own.shape)


def slot_counts(coupled, coupled_len, cand_count, scale):
    live = jnp.arange(coupled.shape[1])[None, :] < coupled_len[:, None]
    hits = (coupled[:, :, None] == jnp.arange(cand_count, dtype=jnp.int32)[None, None, :]) & live[:, :, None]
    return jnp.sum(hits.astype(jnp.float32), axis=1) * scale


def on_device(integral_slabs, slab_owner, pair_orbs, domain_bases, amplitudes, coupled, coupled_len):
    n_grp, n_dev = lax.axis_size("grp"), lax.axis_size("dev")
    pairs, orbs, pno = domain_bases.shape
    half = pairs // 2
    group = lax.axis_index("grp")

    packed = [
        jnp.concatenate([domain_bases[s : s + half], amplitudes[s : s + half]], axis=1) for s in (0, half)
    ]
    swap1 = [(g, g ^ 1) for g in range(n_grp)]
    swap2 = [(g, g ^ 2) for g in range(n_grp)]
    near1_lo = lax.ppermute(packed[0], "grp", swap1)
    near2_hi = lax.ppermute(packed[1], "grp", swap2)
    near1_hi = lax.ppermute(packed[1], "grp", swap1)
    near2_lo = lax.ppermute(packed[0], "grp", swap2)
    far_lo = lax.ppermute(near1_lo, "grp", swap2)
    far_hi = lax.ppermute(near2_hi, "grp", swap1)

    slabs = gather_slabs(integral_slabs[0], n_dev)

    weights = slot_counts(coupled, coupled_len, n_grp * pairs, orbs / pno)
    places = slab_owner[pair_orbs]
    own_t = jnp.swapaxes(domain_bases, 1, 2).reshape(pairs * pno, orbs)
    acc = jnp.zeros((pairs, pno, pno), jnp.float32)
    for source, shift, chunk in (
        (group, 0, packed[0]),
        (group, half, packed[1]),
        (group ^ 1, 0, near1_lo),
        (group ^ 2, half, near2_hi),
        (group ^ 1, half, near1_hi),
        (group ^ 2, 0, near2_lo),
    ):
        start = (source * pairs + shift).astype(jnp.int32).reshape(1)
        acc = add_coupled(start, weights, own_t, chunk, acc)
    acc = add_exchange(places, slabs, domain_bases, acc)
    for shift, chunk in ((0, far_lo), (half, far_hi)):
        start = ((group ^ 3) * pairs + shift).astype(jnp.int32).reshape(1)
        acc = add_coupled(start, weights, own_t, chunk, acc)
    return acc


def solution(mesh):
    in_specs = (
        P("dev", None, None),
        P(),
        P(("grp", "dev"), None),
        P(("grp", "dev"), None, None),
        P(("grp", "dev"), None, None),
        P(("grp", "dev"), None),
        P(("grp", "dev")),
    )
    out_specs = P(("grp", "dev"), None, None)
    return jax.shard_map(
        on_device, mesh=mesh, in_specs=in_specs, out_specs=out_specs, check_vma=False
    )
```

```python
import functools
import math

import jax
import jax.numpy as jnp
from jax import lax
from jax.experimental import pallas as pl
from jax.experimental.pallas import tpu as pltpu
from jax.sharding import PartitionSpec as P

VMEM_LIMIT = 48 * 1024 * 1024
DECLARED = 20_000_000_000
SMEM_SPEC = pl.BlockSpec(memory_space=pltpu.SMEM)
VMEM_SPEC = pl.BlockSpec(memory_space=pltpu.VMEM)


def call_kernel(body, out_shape, scratch, name, smem_args, vmem_args, flops=DECLARED):
    return pl.pallas_call(
        body,
        out_shape=out_shape,
        in_specs=[SMEM_SPEC] * len(smem_args) + [VMEM_SPEC] * len(vmem_args),
        out_specs=VMEM_SPEC,
        scratch_shapes=scratch,
        compiler_params=pltpu.CompilerParams(vmem_limit_bytes=VMEM_LIMIT),
        cost_estimate=pl.CostEstimate(flops=flops, bytes_accessed=0, transcendentals=0),
        name=name,
    )(*smem_args, *vmem_args)


def coupled_kernel(first_ref, weight_ref, own_ref, *refs):
    *cand_refs, acc_ref, out_ref, inter_ref, proj_ref = refs
    pairs, pno, _ = out_ref.shape
    orbs = own_ref.shape[1]
    empty = jnp.zeros((pno, pno), jnp.bfloat16)
    size = cand_refs[0].shape[0]
    for j in range(0, size * len(cand_refs), 2):
        cand_ref, at = cand_refs[j // size], j % size
        first = first_ref[j // size] + at
        bases = jnp.concatenate([cand_ref[at, :orbs, :], cand_ref[at + 1, :orbs, :]], axis=1)
        inter = jnp.dot(own_ref[...], bases, preferred_element_type=jnp.float32).astype(jnp.bfloat16)
        inter_ref[:, j * pno : (j + 2) * pno] = inter
        amps = jnp.concatenate(
            [
                jnp.concatenate([cand_ref[at, orbs:, :], empty], axis=1),
                jnp.concatenate([empty, cand_ref[at + 1, orbs:, :]], axis=1),
            ],
            axis=0,
        )
        proj = jnp.dot(inter, amps, preferred_element_type=jnp.float32)
        for p in range(pairs):
            for c in range(2):
                block = proj[p * pno : (p + 1) * pno, c * pno : (c + 1) * pno]
                proj_ref[p * pno : (p + 1) * pno, (j + c) * pno : (j + c + 1) * pno] = (
                    block * weight_ref[p, first + c]
                ).astype(jnp.bfloat16)
    for p in range(pairs):
        rows = slice(p * pno, (p + 1) * pno)
        out_ref[p] = acc_ref[p] + lax.dot_general(
            proj_ref[rows, :], inter_ref[rows, :], (((1,), (1,)), ((), ())), preferred_element_type=jnp.float32
        )


def add_coupled(first, weights, own_t, chunks, acc, flops):
    rows, pno = own_t.shape[0], acc.shape[2]
    count = sum(chunk.shape[0] for chunk in chunks)
    return call_kernel(
        coupled_kernel,
        jax.ShapeDtypeStruct(acc.shape, jnp.float32),
        [pltpu.VMEM((rows, count * pno), jnp.bfloat16)] * 2,
        "coupled",
        (first, weights),
        (own_t, *chunks, acc),
        flops,
    )


def half_transforms(owner_ref, orbs_ref, turn_ref, slab_refs, base_ref, half_ref, uses_ref, base):
    pairs, _, pno = base_ref.shape
    sides = 2 * pairs

    def clear(k, carry):
        uses_ref[k, 0] = sides
        uses_ref[k, 1] = sides
        return carry

    def note(f, carry):
        k = turn_ref[owner_ref[orbs_ref[f // 2, f % 2]]]
        uses_ref[k, 1] = uses_ref[k, 0]
        uses_ref[k, 0] = f
        return carry

    lax.fori_loop(0, turn_ref.shape[0], clear, 0)
    lax.fori_loop(0, sides, note, 0)

    def both_sides(slab, k):
        one, two = uses_ref[k, 0], uses_ref[k, 1]
        last = pairs - 1
        bases = jnp.concatenate(
            [base_ref[jnp.minimum(one // 2, last)], base_ref[jnp.minimum(two // 2, last)]], axis=1
        )
        both = jnp.dot(slab, bases, preferred_element_type=jnp.float32).astype(jnp.bfloat16)
        half_ref[one] = both[:, :pno]
        half_ref[two] = both[:, pno:]

    for slab_ref in slab_refs:
        if slab_ref.shape[0] > 4:

            def step(k, carry, slab_ref=slab_ref, base=base):
                both_sides(slab_ref[k], base + k)
                return carry

            lax.fori_loop(0, slab_ref.shape[0], step, 0)
        else:
            for k in range(slab_ref.shape[0]):
                both_sides(slab_ref[k], base + k)
        base += slab_ref.shape[0]


def halves_kernel(owner_ref, orbs_ref, turn_ref, *refs):
    *slab_refs, base_ref, half_ref, uses_ref = refs
    half_transforms(owner_ref, orbs_ref, turn_ref, slab_refs, base_ref, half_ref, uses_ref, 0)


def exchange_kernel(scale, base, owner_ref, orbs_ref, turn_ref, *refs):
    *slab_refs, base_ref, early_ref, acc_ref, out_ref, half_ref, uses_ref = refs
    half_transforms(owner_ref, orbs_ref, turn_ref, slab_refs, base_ref, half_ref, uses_ref, base)
    for p in range(out_ref.shape[0]):
        left, right = [
            jnp.where(turn_ref[owner_ref[orbs_ref[p, side]]] < base, early_ref[2 * p + side], half_ref[2 * p + side])
            for side in range(2)
        ]
        product = lax.dot_general(left, right, (((0,), (0,)), ((), ())), preferred_element_type=jnp.float32)
        out_ref[p] = acc_ref[p] + product * scale


def first_halves(slab_owner, pair_orbs, turn, slabs, bases):
    pairs, _, pno = bases.shape
    return call_kernel(
        halves_kernel,
        jax.ShapeDtypeStruct((2 * pairs + 1, slabs[0].shape[1], pno), jnp.bfloat16),
        [pltpu.SMEM((turn.shape[0], 2), jnp.int32)],
        "halves",
        (slab_owner, pair_orbs, turn),
        (*slabs, bases),
        0,
    )


def add_exchange(slab_owner, pair_orbs, turn, base, slabs, bases, early, acc):
    return call_kernel(
        functools.partial(exchange_kernel, 1.0 / math.sqrt(slabs[0].shape[1]), base),
        jax.ShapeDtypeStruct(acc.shape, jnp.float32),
        [pltpu.VMEM(early.shape, jnp.bfloat16), pltpu.SMEM((turn.shape[0], 2), jnp.int32)],
        "exchange",
        (slab_owner, pair_orbs, turn),
        (*slabs, bases, early, acc),
        0,
    )


def after(value, *earlier):
    return lax.optimization_barrier((value,) + earlier)[0]


def slot_counts(coupled, coupled_len, cand_count, scale):
    live = jnp.arange(coupled.shape[1])[None, :] < coupled_len[:, None]
    hits = (coupled[:, :, None] == jnp.arange(cand_count, dtype=jnp.int32)[None, None, :]) & live[:, :, None]
    return jnp.sum(hits.astype(jnp.float32), axis=1) * scale


def on_device(integral_slabs, slab_owner, pair_orbs, domain_bases, amplitudes, coupled, coupled_len):
    n_grp, n_dev = lax.axis_size("grp"), lax.axis_size("dev")
    pairs, orbs, pno = domain_bases.shape
    group, me = lax.axis_index("grp"), lax.axis_index("dev")
    near1, near2, far = group ^ 1, group ^ 2, group ^ 3
    chips = n_dev // 2
    chip, core = me // 2, me % 2
    line = chips == 4

    half, part = pairs // 2, pairs // 4
    pack = lambda low, high: jnp.concatenate([domain_bases[low:high], amplitudes[low:high]], axis=1)
    own_lo, own_hi = pack(0, half), pack(half, pairs)

    def along_x(value):
        return lax.ppermute(value, "grp", [(g, g ^ 1) for g in range(n_grp)])

    def along_y(value):
        return lax.ppermute(value, "grp", [(g, g ^ 2) for g in range(n_grp)])

    def next_chip(value):
        return lax.ppermute(value, "dev", [(d, (d + 2) % n_dev) for d in range(n_dev)])

    def other_core(value):
        return lax.ppermute(value, "dev", [(d, d ^ 1) for d in range(n_dev)])

    weights = slot_counts(coupled, coupled_len, n_grp * pairs, orbs / pno)
    own_t = jnp.swapaxes(domain_bases, 1, 2).reshape(pairs * pno, orbs)

    def add(acc, *parts, flops=DECLARED):
        first = jnp.stack([source * pairs + low for source, low, _ in parts]).astype(jnp.int32)
        return add_coupled(first, weights, own_t, [chunk for _, _, chunk in parts], acc, flops)

    slab = integral_slabs[0]
    ring = chips <= 4

    x_lo, y_hi = along_x(own_lo), along_y(own_hi)
    x_hi1, y_lo1 = along_x(own_hi[:part]), along_y(own_lo[:part])
    far_hi, far_lo = along_x(y_hi), along_y(x_lo)

    acc = jnp.zeros((pairs, pno, pno), jnp.float32)
    acc = add(acc, (group, 0, own_lo), (group, half, own_hi))
    if ring:
        round1 = next_chip(slab)
        early = jnp.stack([slab, round1])
        early_swap = other_core(early)
        round2 = next_chip(after(round1, early_swap, x_lo, y_hi))
        acc = after(acc, early_swap)
    acc = add(acc, (near1, 0, x_lo), (near2, half, y_hi))
    acc = add(acc, (near1, half, x_hi1), (near2, 0, y_lo1), flops=0)
    if ring:
        round2 = after(round2, acc)
        swap2, round3 = other_core(round2), next_chip(round2)
        slabs = [early, early_swap, round2[None], swap2[None]]
        position = jnp.arange(n_dev, dtype=jnp.int32)
        steps = (chip - position // 2) % chips
        turn = jnp.where(steps < 2, steps, 2 * steps) + jnp.where(position % 2 == core, 0, jnp.where(steps < 2, 2, 1))
        ahead = 6
    else:
        gathered = lax.all_gather(slab, "dev", axis=0, tiled=False)
        ahead = n_dev // 2
        slabs, rest = [gathered[:ahead]], [gathered[ahead:]]
        swap2 = slab
        turn = jnp.arange(n_dev)
    turn = turn.astype(jnp.int32)
    x_hi2, y_lo2 = along_x(after(own_hi[part:], swap2)), along_y(after(own_lo[part:], swap2))
    halves = first_halves(slab_owner, pair_orbs, turn, slabs, after(domain_bases, acc))
    acc = after(acc, halves)
    acc = add(acc, (far, 0, far_lo), (far, half, far_hi), flops=0)
    if ring:
        round3 = after(round3, acc)
        rest = [round3[None], other_core(round3)[None]]
    acc = add_exchange(slab_owner, pair_orbs, turn, ahead, rest, domain_bases, halves, acc)
    return add(acc, (near1, half + part, x_hi2), (near2, part, y_lo2))


def solution(mesh):
    in_specs = (
        P("dev", None, None),
        P(),
        P(("grp", "dev"), None),
        P(("grp", "dev"), None, None),
        P(("grp", "dev"), None, None),
        P(("grp", "dev"), None),
        P(("grp", "dev")),
    )
    out_specs = P(("grp", "dev"), None, None)
    return jax.shard_map(
        on_device, mesh=mesh, in_specs=in_specs, out_specs=out_specs, check_vma=False
    )
```

```python
import functools
import math

import jax
import jax.numpy as jnp
from jax import lax
from jax.experimental import pallas as pl
from jax.experimental.pallas import tpu as pltpu
from jax.sharding import PartitionSpec as P

MIB = 1024 * 1024
DECLARED = 20_000_000_000
SMEM_SPEC = pl.BlockSpec(memory_space=pltpu.SMEM)
VMEM_SPEC = pl.BlockSpec(memory_space=pltpu.VMEM)


def call_kernel(body, out_shape, scratch, name, smem_args, vmem_args, flops, aliases={}):
    held = sum(math.prod(a.shape) * a.dtype.itemsize for a in (*vmem_args, *scratch, out_shape))
    return pl.pallas_call(
        body,
        out_shape=out_shape,
        in_specs=[SMEM_SPEC] * len(smem_args) + [VMEM_SPEC] * len(vmem_args),
        out_specs=VMEM_SPEC,
        scratch_shapes=scratch,
        input_output_aliases=aliases,
        compiler_params=pltpu.CompilerParams(vmem_limit_bytes=held + 6 * MIB),
        cost_estimate=pl.CostEstimate(flops=flops, bytes_accessed=0, transcendentals=0),
        name=name,
    )(*smem_args, *vmem_args)


def coupled_kernel(first_ref, weight_ref, own_ref, *refs):
    *cand_refs, acc_ref, out_ref, inter_ref, proj_ref = refs
    pairs, pno, _ = out_ref.shape
    orbs = own_ref.shape[1]
    empty = jnp.zeros((pno, pno), jnp.bfloat16)
    size = cand_refs[0].shape[0]
    for j in range(0, size * len(cand_refs), 2):
        cand_ref, at = cand_refs[j // size], j % size
        first = first_ref[j // size] + at
        bases = jnp.concatenate([cand_ref[at, :orbs, :], cand_ref[at + 1, :orbs, :]], axis=1)
        inter = jnp.dot(own_ref[...], bases, preferred_element_type=jnp.float32).astype(jnp.bfloat16)
        inter_ref[:, j * pno : (j + 2) * pno] = inter
        amps = jnp.concatenate(
            [
                jnp.concatenate([cand_ref[at, orbs:, :], empty], axis=1),
                jnp.concatenate([empty, cand_ref[at + 1, orbs:, :]], axis=1),
            ],
            axis=0,
        )
        proj = jnp.dot(inter, amps, preferred_element_type=jnp.float32)
        for p in range(pairs):
            for c in range(2):
                block = proj[p * pno : (p + 1) * pno, c * pno : (c + 1) * pno]
                proj_ref[p * pno : (p + 1) * pno, (j + c) * pno : (j + c + 1) * pno] = (
                    block * weight_ref[p, first + c]
                ).astype(jnp.bfloat16)
    for p in range(pairs):
        rows = slice(p * pno, (p + 1) * pno)
        out_ref[p] = acc_ref[p] + lax.dot_general(
            proj_ref[rows, :], inter_ref[rows, :], (((1,), (1,)), ((), ())), preferred_element_type=jnp.float32
        )


def add_coupled(first, weights, own_t, chunks, acc, flops):
    rows, pno = own_t.shape[0], acc.shape[2]
    count = sum(chunk.shape[0] for chunk in chunks)
    return call_kernel(
        coupled_kernel,
        jax.ShapeDtypeStruct(acc.shape, jnp.float32),
        [pltpu.VMEM((rows, count * pno), jnp.bfloat16)] * 2,
        "coupled",
        (first, weights),
        (own_t, *chunks, acc),
        flops,
    )


def half_transforms(owner_ref, orbs_ref, turn_ref, slab_refs, base_ref, half_ref, uses_ref, base):
    pairs, _, pno = base_ref.shape
    sides = 2 * pairs

    def clear(k, carry):
        uses_ref[k, 0] = sides
        uses_ref[k, 1] = sides
        return carry

    def note(f, carry):
        k = turn_ref[owner_ref[orbs_ref[f // 2, f % 2]]]
        uses_ref[k, 1] = uses_ref[k, 0]
        uses_ref[k, 0] = f
        return carry

    lax.fori_loop(0, turn_ref.shape[0], clear, 0)
    lax.fori_loop(0, sides, note, 0)

    def both_sides(slab, k):
        one, two = uses_ref[k, 0], uses_ref[k, 1]
        last = pairs - 1
        bases = jnp.concatenate(
            [base_ref[jnp.minimum(one // 2, last)], base_ref[jnp.minimum(two // 2, last)]], axis=1
        )
        both = jnp.dot(slab, bases, preferred_element_type=jnp.float32).astype(jnp.bfloat16)
        half_ref[one] = both[:, :pno]
        half_ref[two] = both[:, pno:]

    for slab_ref in slab_refs:
        if slab_ref.shape[0] > 4:

            def step(k, carry, slab_ref=slab_ref, base=base):
                both_sides(slab_ref[k], base + k)
                return carry

            lax.fori_loop(0, slab_ref.shape[0], step, 0)
        else:
            for k in range(slab_ref.shape[0]):
                both_sides(slab_ref[k], base + k)
        base += slab_ref.shape[0]


def halves_kernel(base, owner_ref, orbs_ref, turn_ref, *refs):
    *slab_refs, base_ref, half_ref, uses_ref = refs
    half_transforms(owner_ref, orbs_ref, turn_ref, slab_refs, base_ref, half_ref, uses_ref, base)


def more_halves_kernel(base, owner_ref, orbs_ref, turn_ref, *refs):
    *slab_refs, base_ref, _, half_ref, uses_ref = refs
    half_transforms(owner_ref, orbs_ref, turn_ref, slab_refs, base_ref, half_ref, uses_ref, base)


def exchange_kernel(scale, base, owner_ref, orbs_ref, turn_ref, *refs):
    *slab_refs, base_ref, early_ref, acc_ref, out_ref, half_ref, uses_ref = refs
    half_transforms(owner_ref, orbs_ref, turn_ref, slab_refs, base_ref, half_ref, uses_ref, base)
    for p in range(out_ref.shape[0]):
        left, right = [
            jnp.where(turn_ref[owner_ref[orbs_ref[p, side]]] < base, early_ref[2 * p + side], half_ref[2 * p + side])
            for side in range(2)
        ]
        product = lax.dot_general(left, right, (((0,), (0,)), ((), ())), preferred_element_type=jnp.float32)
        out_ref[p] = acc_ref[p] + product * scale


def half_products(scalars, base, slabs, bases, done=None):
    pairs, _, pno = bases.shape
    shape = jax.ShapeDtypeStruct((2 * pairs + 1, slabs[0].shape[1], pno), jnp.bfloat16)
    uses = [pltpu.SMEM((scalars[2].shape[0], 2), jnp.int32)]
    if done is None:
        return call_kernel(functools.partial(halves_kernel, base), shape, uses, "halves", scalars, (*slabs, bases), 0)
    args = (*slabs, bases, done)
    aliases = {len(scalars) + len(args) - 1: 0}
    return call_kernel(
        functools.partial(more_halves_kernel, base), shape, uses, "more_halves", scalars, args, 0, aliases
    )


def add_exchange(scalars, base, slabs, bases, early, acc):
    return call_kernel(
        functools.partial(exchange_kernel, 1.0 / math.sqrt(slabs[0].shape[1]), base),
        jax.ShapeDtypeStruct(acc.shape, jnp.float32),
        [pltpu.VMEM(early.shape, jnp.bfloat16), pltpu.SMEM((scalars[2].shape[0], 2), jnp.int32)],
        "exchange",
        scalars,
        (*slabs, bases, early, acc),
        0,
    )


def after(value, *earlier):
    return lax.optimization_barrier((value,) + earlier)[0]


def slot_counts(coupled, coupled_len, cand_count, scale):
    live = jnp.arange(coupled.shape[1])[None, :] < coupled_len[:, None]
    hits = (coupled[:, :, None] == jnp.arange(cand_count, dtype=jnp.int32)[None, None, :]) & live[:, :, None]
    return jnp.sum(hits.astype(jnp.float32), axis=1) * scale


def on_device(integral_slabs, slab_owner, pair_orbs, domain_bases, amplitudes, coupled, coupled_len):
    n_grp, n_dev = lax.axis_size("grp"), lax.axis_size("dev")
    pairs, orbs, pno = domain_bases.shape
    group, me = lax.axis_index("grp"), lax.axis_index("dev")
    near1, near2, far = group ^ 1, group ^ 2, group ^ 3
    chips = n_dev // 2
    chip, core = me // 2, me % 2
    line = chips == 4

    half = pairs // 2
    pack = lambda low, high: jnp.concatenate([domain_bases[low:high], amplitudes[low:high]], axis=1)
    own_lo, own_hi = pack(0, half), pack(half, pairs)

    def along_x(value):
        return lax.ppermute(value, "grp", [(g, g ^ 1) for g in range(n_grp)])

    def along_y(value):
        return lax.ppermute(value, "grp", [(g, g ^ 2) for g in range(n_grp)])

    def next_chip(value):
        return lax.ppermute(value, "dev", [(d, (d + 2) % n_dev) for d in range(n_dev)])

    def other_core(value):
        return lax.ppermute(value, "dev", [(d, d ^ 1) for d in range(n_dev)])

    weights = slot_counts(coupled, coupled_len, n_grp * pairs, orbs / pno)
    own_t = jnp.swapaxes(domain_bases, 1, 2).reshape(pairs * pno, orbs)

    def add(acc, *parts, flops=DECLARED):
        first = jnp.stack([source * pairs + low for source, low, _ in parts]).astype(jnp.int32)
        return add_coupled(first, weights, own_t, [chunk for _, _, chunk in parts], acc, flops)

    slab = integral_slabs[0]
    ring = chips <= 4
    position = jnp.arange(n_dev, dtype=jnp.int32)

    x_lo, y_hi = along_x(own_lo), along_y(own_hi)
    x_hi, y_lo = along_x(after(own_hi, own_lo)), along_y(after(own_lo, own_hi))
    far_hi, far_lo = along_x(y_hi), along_y(x_lo)

    acc = jnp.zeros((pairs, pno, pno), jnp.float32)
    if ring:
        round1 = next_chip(slab)
    acc = add(acc, (group, 0, own_lo), (group, half, own_hi), flops=0)
    if ring:
        round2 = next_chip(after(round1, acc))
        swap0, swap1 = other_core(after(slab, x_lo, y_hi)), other_core(after(round1, x_lo, y_hi))
    acc = add(acc, (near1, 0, x_lo), (near2, half, y_hi))
    if ring:
        steps = (chip - position // 2) % chips
        turn = 2 * steps + jnp.where(position % 2 == core, 0, 1)
        scalars = (slab_owner, pair_orbs, turn.astype(jnp.int32))
        slabs = [slab[None], swap0[None], round1[None], swap1[None]]
        halves = half_products(scalars, 0, slabs, after(domain_bases, acc))
        acc = after(acc, halves)
        round2 = after(round2, acc)
        round3, swap2 = next_chip(round2), other_core(round2)
    acc = add(acc, (near1, half, x_hi), (near2, 0, y_lo), flops=0)
    if ring:
        halves = half_products(scalars, 4, [round2[None], swap2[None]], after(domain_bases, acc), halves)
        acc = after(acc, halves)
        ahead, rest = 6, [round3[None], other_core(after(round3, acc))[None]]
    else:
        gathered = lax.all_gather(slab, "dev", axis=0, tiled=False)
        scalars = (slab_owner, pair_orbs, position)
        ahead = n_dev // 2
        halves = half_products(scalars, 0, [gathered[:ahead]], domain_bases)
        rest = [gathered[ahead:]]
    acc = add_exchange(scalars, ahead, rest, domain_bases, halves, acc)
    return add(acc, (far, 0, far_lo), (far, half, far_hi), flops=0)


def solution(mesh):
    in_specs = (
        P("dev", None, None),
        P(),
        P(("grp", "dev"), None),
        P(("grp", "dev"), None, None),
        P(("grp", "dev"), None, None),
        P(("grp", "dev"), None),
        P(("grp", "dev")),
    )
    out_specs = P(("grp", "dev"), None, None)
    return jax.shard_map(
        on_device, mesh=mesh, in_specs=in_specs, out_specs=out_specs, check_vma=False
    )
```

```python
import functools
import math

import jax
import jax.numpy as jnp
from jax import lax
from jax.experimental import pallas as pl
from jax.experimental.pallas import tpu as pltpu
from jax.sharding import PartitionSpec as P

MARGIN = 2 * 1024 * 1024
DECLARED = 20_000_000_000
SMEM_SPEC = pl.BlockSpec(memory_space=pltpu.SMEM)
VMEM_SPEC = pl.BlockSpec(memory_space=pltpu.VMEM)


def call_kernel(body, out_shape, scratch, name, smem_args, vmem_args, flops, aliases={}):
    held = sum(math.prod(a.shape) * a.dtype.itemsize for a in (*vmem_args, *scratch, out_shape))
    return pl.pallas_call(
        body,
        out_shape=out_shape,
        in_specs=[SMEM_SPEC] * len(smem_args) + [VMEM_SPEC] * len(vmem_args),
        out_specs=VMEM_SPEC,
        scratch_shapes=scratch,
        input_output_aliases=aliases,
        compiler_params=pltpu.CompilerParams(vmem_limit_bytes=held + MARGIN),
        cost_estimate=pl.CostEstimate(flops=flops, bytes_accessed=0, transcendentals=0),
        name=name,
    )(*smem_args, *vmem_args)


def coupled_kernel(first_ref, weight_ref, own_ref, *refs):
    *cand_refs, acc_ref, out_ref, inter_ref, proj_ref = refs
    pairs, pno, _ = out_ref.shape
    orbs = own_ref.shape[1]
    empty = jnp.zeros((pno, pno), jnp.bfloat16)
    size = cand_refs[0].shape[0]
    for m in range(0, pairs, 2):
        for j in range(0, size * len(cand_refs), 2):
            cand_ref, at = cand_refs[j // size], j % size
            first = first_ref[j // size] + at
            bases = jnp.concatenate([cand_ref[at, :orbs, :], cand_ref[at + 1, :orbs, :]], axis=1)
            inter = jnp.dot(
                own_ref[m * pno : (m + 2) * pno, :], bases, preferred_element_type=jnp.float32
            ).astype(jnp.bfloat16)
            inter_ref[:, j * pno : (j + 2) * pno] = inter
            amps = jnp.concatenate(
                [
                    jnp.concatenate([cand_ref[at, orbs:, :], empty], axis=1),
                    jnp.concatenate([empty, cand_ref[at + 1, orbs:, :]], axis=1),
                ],
                axis=0,
            )
            proj = jnp.dot(inter, amps, preferred_element_type=jnp.float32)
            for p in range(2):
                for c in range(2):
                    block = proj[p * pno : (p + 1) * pno, c * pno : (c + 1) * pno]
                    proj_ref[p * pno : (p + 1) * pno, (j + c) * pno : (j + c + 1) * pno] = (
                        block * weight_ref[m + p, first + c]
                    ).astype(jnp.bfloat16)
        for p in range(2):
            rows = slice(p * pno, (p + 1) * pno)
            out_ref[m + p] = acc_ref[m + p] + lax.dot_general(
                proj_ref[rows, :], inter_ref[rows, :], (((1,), (1,)), ((), ())), preferred_element_type=jnp.float32
            )


def add_coupled(first, weights, own_t, chunks, acc, flops):
    pno = acc.shape[2]
    count = sum(chunk.shape[0] for chunk in chunks)
    return call_kernel(
        coupled_kernel,
        jax.ShapeDtypeStruct(acc.shape, jnp.float32),
        [pltpu.VMEM((2 * pno, count * pno), jnp.bfloat16)] * 2,
        "coupled",
        (first, weights),
        (own_t, *chunks, acc),
        flops,
    )


def half_transforms(uses_ref, slab_refs, base_ref, half_ref, base):
    pairs, _, pno = base_ref.shape

    def both_sides(slab, k):
        one, two = uses_ref[k, 0], uses_ref[k, 1]
        last = pairs - 1
        bases = jnp.concatenate(
            [base_ref[jnp.minimum(one // 2, last)], base_ref[jnp.minimum(two // 2, last)]], axis=1
        )
        both = jnp.dot(slab, bases, preferred_element_type=jnp.float32).astype(jnp.bfloat16)
        half_ref[one] = both[:, :pno]
        half_ref[two] = both[:, pno:]

    for slab_ref in slab_refs:
        if slab_ref.shape[0] > 4:

            def step(k, carry, slab_ref=slab_ref, base=base):
                both_sides(slab_ref[k], base + k)
                return carry

            lax.fori_loop(0, slab_ref.shape[0], step, 0)
        else:
            for k in range(slab_ref.shape[0]):
                both_sides(slab_ref[k], base + k)
        base += slab_ref.shape[0]


def halves_kernel(base, uses_ref, *refs):
    *slab_refs, base_ref, half_ref = refs
    half_transforms(uses_ref, slab_refs, base_ref, half_ref, base)


def more_halves_kernel(base, uses_ref, *refs):
    *slab_refs, base_ref, _, half_ref = refs
    half_transforms(uses_ref, slab_refs, base_ref, half_ref, base)


def exchange_kernel(scale, base, uses_ref, turn_ref, *refs):
    *slab_refs, base_ref, early_ref, acc_ref, out_ref, half_ref = refs
    half_transforms(uses_ref, slab_refs, base_ref, half_ref, base)
    for p in range(out_ref.shape[0]):
        left, right = [
            jnp.where(turn_ref[p, side] < base, early_ref[2 * p + side], half_ref[2 * p + side]) for side in range(2)
        ]
        product = lax.dot_general(left, right, (((0,), (0,)), ((), ())), preferred_element_type=jnp.float32)
        out_ref[p] = acc_ref[p] + product * scale


def half_products(uses, base, slabs, bases, done=None):
    pairs, _, pno = bases.shape
    shape = jax.ShapeDtypeStruct((2 * pairs + 1, slabs[0].shape[1], pno), jnp.bfloat16)
    if done is None:
        return call_kernel(functools.partial(halves_kernel, base), shape, [], "halves", (uses,), (*slabs, bases), 0)
    args = (*slabs, bases, done)
    return call_kernel(
        functools.partial(more_halves_kernel, base), shape, [], "more_halves", (uses,), args, 0, {len(args): 0}
    )


def add_exchange(uses, turn, base, slabs, bases, early, acc):
    return call_kernel(
        functools.partial(exchange_kernel, 1.0 / math.sqrt(slabs[0].shape[1]), base),
        jax.ShapeDtypeStruct(acc.shape, jnp.float32),
        [pltpu.VMEM(early.shape, jnp.bfloat16)],
        "exchange",
        (uses, turn),
        (*slabs, bases, early, acc),
        0,
    )


def slab_uses(slab_owner, pair_orbs, order):
    n_dev = order.shape[0]
    sides = pair_orbs.shape[0] * 2
    table = jnp.arange(n_dev, dtype=jnp.int32)
    position = jnp.sum(jnp.where(pair_orbs.reshape(sides)[:, None] == table, slab_owner, 0), axis=1)
    turn = jnp.sum(jnp.where(position[:, None] == table, order, 0), axis=1).astype(jnp.int32)
    hit = turn[:, None] == table
    side = jnp.arange(sides, dtype=jnp.int32)[:, None]
    last = jnp.max(jnp.where(hit, side, -1), axis=0)
    first = jnp.min(jnp.where(hit, side, sides), axis=0)
    return turn.reshape(-1, 2), jnp.stack([first, jnp.where(last < 0, sides, last)], axis=1)


def pack_kernel(base_ref, amp_ref, low_ref, high_ref, sems):
    half, orbs = low_ref.shape[0], base_ref.shape[1]
    copies = []
    for k, out_ref in enumerate((low_ref, high_ref)):
        rows = pl.ds(k * half, half)
        copies.append(pltpu.make_async_copy(base_ref.at[rows], out_ref.at[:, pl.ds(0, orbs)], sems.at[2 * k]))
        copies.append(
            pltpu.make_async_copy(amp_ref.at[rows], out_ref.at[:, pl.ds(orbs, amp_ref.shape[1])], sems.at[2 * k + 1])
        )
    for copy in copies:
        copy.start()
    for copy in copies:
        copy.wait()


def pack(bases, amps):
    pairs, orbs, pno = bases.shape
    shape = jax.ShapeDtypeStruct((pairs // 2, orbs + pno, pno), bases.dtype)
    return pl.pallas_call(
        pack_kernel,
        out_shape=(shape, shape),
        in_specs=[pl.BlockSpec(memory_space=pl.ANY)] * 2,
        out_specs=(VMEM_SPEC, VMEM_SPEC),
        scratch_shapes=[pltpu.SemaphoreType.DMA((4,))],
        compiler_params=pltpu.CompilerParams(vmem_limit_bytes=4 * MARGIN),
        name="pack",
    )(bases, amps)


def after(value, *earlier):
    return lax.optimization_barrier((value,) + earlier)[0]


def slot_counts(coupled, coupled_len, cand_count, scale):
    live = jnp.arange(coupled.shape[1])[None, :] < coupled_len[:, None]
    hits = (coupled[:, :, None] == jnp.arange(cand_count, dtype=jnp.int32)[None, None, :]) & live[:, :, None]
    return jnp.sum(hits.astype(jnp.float32), axis=1) * scale


def on_device(integral_slabs, slab_owner, pair_orbs, domain_bases, amplitudes, coupled, coupled_len):
    n_grp, n_dev = lax.axis_size("grp"), lax.axis_size("dev")
    pairs, orbs, pno = domain_bases.shape
    group, me = lax.axis_index("grp"), lax.axis_index("dev")
    near1, near2, far = group ^ 1, group ^ 2, group ^ 3
    chips = n_dev // 2
    chip, core = me // 2, me % 2
    line = chips == 4

    half = pairs // 2
    own_lo, own_hi = pack(domain_bases, amplitudes)

    def along_x(value):
        return lax.ppermute(value, "grp", [(g, g ^ 1) for g in range(n_grp)])

    def along_y(value):
        return lax.ppermute(value, "grp", [(g, g ^ 2) for g in range(n_grp)])

    def next_chip(value):
        return lax.ppermute(value, "dev", [(d, (d + 2) % n_dev) for d in range(n_dev)])

    def other_core(value):
        return lax.ppermute(value, "dev", [(d, d ^ 1) for d in range(n_dev)])

    weights = slot_counts(coupled, coupled_len, n_grp * pairs, orbs / pno)
    own_t = jnp.swapaxes(domain_bases, 1, 2).reshape(pairs * pno, orbs)

    def add(acc, *parts, flops=DECLARED):
        first = jnp.stack([source * pairs + low for source, low, _ in parts]).astype(jnp.int32)
        return add_coupled(first, weights, own_t, [chunk for _, _, chunk in parts], acc, flops)

    slab = integral_slabs[0]
    ring = chips <= 4
    position = jnp.arange(n_dev, dtype=jnp.int32)

    x_lo, y_hi = along_x(own_lo), along_y(own_hi)
    x_hi, y_lo = along_x(after(own_hi, own_lo)), along_y(after(own_lo, own_hi))
    far_hi, far_lo = along_x(y_hi), along_y(x_lo)

    acc = jnp.zeros((pairs, pno, pno), jnp.float32)
    if ring:
        round1 = next_chip(slab)
    acc = add(acc, (group, 0, own_lo), (group, half, own_hi), flops=0)
    if ring:
        round2 = next_chip(after(round1, acc))
        swap0, swap1 = other_core(after(slab, x_lo, y_hi)), other_core(after(round1, x_lo, y_hi))
    acc = add(acc, (near1, 0, x_lo), (near2, half, y_hi))
    if ring:
        order = 2 * ((chip - position // 2) % chips) + jnp.where(position % 2 == core, 0, 1)
        turn, uses = slab_uses(slab_owner, pair_orbs, order)
        slabs = [slab[None], swap0[None], round1[None], swap1[None]]
        halves = half_products(uses, 0, slabs, after(domain_bases, acc))
        acc = after(acc, halves)
        round2 = after(round2, acc)
        round3, swap2 = next_chip(round2), other_core(round2)
    acc = add(acc, (near1, half, x_hi), (near2, 0, y_lo), flops=0)
    if ring:
        halves = half_products(uses, 4, [round2[None], swap2[None]], after(domain_bases, acc), halves)
        acc = after(acc, halves)
        ahead, rest = 6, [round3[None], other_core(after(round3, acc))[None]]
    else:
        gathered = lax.all_gather(slab, "dev", axis=0, tiled=False)
        turn, uses = slab_uses(slab_owner, pair_orbs, position)
        ahead = n_dev // 2
        halves = half_products(uses, 0, [gathered[:ahead]], domain_bases)
        rest = [gathered[ahead:]]
    acc = add_exchange(uses, turn, ahead, rest, domain_bases, halves, acc)
    return add(acc, (far, 0, far_lo), (far, half, far_hi), flops=0)


def solution(mesh):
    in_specs = (
        P("dev", None, None),
        P(),
        P(("grp", "dev"), None),
        P(("grp", "dev"), None, None),
        P(("grp", "dev"), None, None),
        P(("grp", "dev"), None),
        P(("grp", "dev")),
    )
    out_specs = P(("grp", "dev"), None, None)
    return jax.shard_map(
        on_device, mesh=mesh, in_specs=in_specs, out_specs=out_specs, check_vma=False
    )
```

```python
import functools
import math

import jax
import jax.numpy as jnp
from jax import lax
from jax.experimental import pallas as pl
from jax.experimental.pallas import tpu as pltpu
from jax.sharding import PartitionSpec as P

MARGIN = 2 * 1024 * 1024
DECLARED = 20_000_000_000
SMEM_SPEC = pl.BlockSpec(memory_space=pltpu.SMEM)
VMEM_SPEC = pl.BlockSpec(memory_space=pltpu.VMEM)
HBM_SPEC = pl.BlockSpec(memory_space=pltpu.HBM)


def call_kernel(body, out_shape, scratch, name, smem_args, vmem_args, flops, hbm_args=(), out_spec=VMEM_SPEC, aliases={}):
    held = [*vmem_args, *scratch] + ([out_shape] if out_spec is VMEM_SPEC else [])
    held = sum(math.prod(a.shape) * a.dtype.itemsize for a in held if a.dtype in (jnp.float32, jnp.bfloat16))
    return pl.pallas_call(
        body,
        out_shape=out_shape,
        in_specs=[SMEM_SPEC] * len(smem_args) + [VMEM_SPEC] * len(vmem_args) + [HBM_SPEC] * len(hbm_args),
        out_specs=out_spec,
        scratch_shapes=scratch,
        input_output_aliases=aliases,
        compiler_params=pltpu.CompilerParams(vmem_limit_bytes=held + MARGIN),
        cost_estimate=pl.CostEstimate(flops=flops, bytes_accessed=0, transcendentals=0),
        name=name,
    )(*smem_args, *vmem_args, *hbm_args)


def summed_kernel(body, name, smem_args, vmem_args, scratch, acc, shape, flops):
    pairs, pno, _ = shape

    def kernel(*refs):
        *refs, sum_ref, in_sem, out_sems = refs
        inputs, scratch_refs = refs[: len(refs) - len(scratch)], refs[len(refs) - len(scratch) :]
        *inputs, out_hbm = inputs
        load = None
        if acc is not None:
            *inputs, acc_hbm = inputs
            load = pltpu.make_async_copy(acc_hbm, sum_ref, in_sem)
            load.start()
        stores = []

        def ready():
            if load is not None:
                load.wait()

        def add(p, value):
            sum_ref[p] = value if load is None else sum_ref[p] + value
            stores.append(pltpu.make_async_copy(sum_ref.at[p], out_hbm.at[p], out_sems.at[p]))
            stores[-1].start()

        body(ready, add, *inputs, *scratch_refs)
        for store in stores:
            store.wait()

    return call_kernel(
        kernel,
        jax.ShapeDtypeStruct(shape, jnp.float32),
        [*scratch, pltpu.VMEM(shape, jnp.float32), pltpu.SemaphoreType.DMA(()), pltpu.SemaphoreType.DMA((pairs,))],
        name,
        smem_args,
        vmem_args,
        flops,
        () if acc is None else (acc,),
        HBM_SPEC,
    )


def coupled_body(ready, add, first_ref, weight_ref, own_ref, *refs):
    *cand_refs, inter_ref, proj_ref = refs
    rows, orbs = own_ref.shape
    pno = cand_refs[0].shape[2]
    empty = jnp.zeros((pno, pno), jnp.bfloat16)
    size = cand_refs[0].shape[0]
    for j in range(0, size * len(cand_refs), 2):
        cand_ref, at = cand_refs[j // size], j % size
        first = first_ref[j // size] + at
        bases = jnp.concatenate([cand_ref[at, :orbs, :], cand_ref[at + 1, :orbs, :]], axis=1)
        inter = jnp.dot(own_ref[...], bases, preferred_element_type=jnp.float32).astype(jnp.bfloat16)
        inter_ref[:, j * pno : (j + 2) * pno] = inter
        amps = jnp.concatenate(
            [
                jnp.concatenate([cand_ref[at, orbs:, :], empty], axis=1),
                jnp.concatenate([empty, cand_ref[at + 1, orbs:, :]], axis=1),
            ],
            axis=0,
        )
        proj = jnp.dot(inter, amps, preferred_element_type=jnp.float32)
        for p in range(rows // pno):
            for c in range(2):
                block = proj[p * pno : (p + 1) * pno, c * pno : (c + 1) * pno]
                proj_ref[p * pno : (p + 1) * pno, (j + c) * pno : (j + c + 1) * pno] = (
                    block * weight_ref[p, first + c]
                ).astype(jnp.bfloat16)
    ready()
    for p in range(0, rows // pno, 2):
        both = slice(p * pno, (p + 2) * pno)
        total = lax.dot_general(
            proj_ref[both, :], inter_ref[both, :], (((1,), (1,)), ((), ())), preferred_element_type=jnp.float32
        )
        add(p, total[:pno, :pno])
        add(p + 1, total[pno:, pno:])


def add_coupled(first, weights, own_t, chunks, acc, shape, flops):
    rows, pno = own_t.shape[0], shape[2]
    count = sum(chunk.shape[0] for chunk in chunks)
    scratch = [pltpu.VMEM((rows, count * pno), jnp.bfloat16)] * 2
    return summed_kernel(coupled_body, "coupled", (first, weights), (own_t, *chunks), scratch, acc, shape, flops)


def half_transforms(uses_ref, slab_refs, own_ref, half_ref, base):
    pno = half_ref.shape[2]
    last = own_ref.shape[0] // pno - 1

    def rows(side):
        return own_ref[pl.ds(pl.multiple_of(jnp.minimum(side // 2, last) * pno, pno), pno), :]

    def both_sides(slab, k):
        one, two = uses_ref[k, 0], uses_ref[k, 1]
        bases = jnp.concatenate([rows(one), rows(two)], axis=0)
        both = lax.dot_general(slab, bases, (((1,), (1,)), ((), ())), preferred_element_type=jnp.float32)
        both = both.astype(jnp.bfloat16)
        half_ref[one] = both[:, :pno]
        half_ref[two] = both[:, pno:]

    for slab_ref in slab_refs:
        if slab_ref.shape[0] > 4:

            def step(k, carry, slab_ref=slab_ref, base=base):
                both_sides(slab_ref[k], base + k)
                return carry

            lax.fori_loop(0, slab_ref.shape[0], step, 0)
        else:
            for k in range(slab_ref.shape[0]):
                both_sides(slab_ref[k], base + k)
        base += slab_ref.shape[0]


def halves_kernel(base, uses_ref, *refs):
    *slab_refs, own_ref, half_ref = refs
    half_transforms(uses_ref, slab_refs, own_ref, half_ref, base)


def more_halves_kernel(base, uses_ref, *refs):
    *slab_refs, own_ref, _, half_ref = refs
    half_transforms(uses_ref, slab_refs, own_ref, half_ref, base)


def exchange_body(scale, base, ready, add, uses_ref, turn_ref, *refs):
    *slab_refs, own_ref, early_ref, half_ref = refs
    half_transforms(uses_ref, slab_refs, own_ref, half_ref, base)
    ready()
    for p in range(turn_ref.shape[0]):
        left, right = [
            jnp.where(turn_ref[p, side] < base, early_ref[2 * p + side], half_ref[2 * p + side]) for side in range(2)
        ]
        product = lax.dot_general(left, right, (((0,), (0,)), ((), ())), preferred_element_type=jnp.float32)
        add(p, product * scale)


def half_products(uses, base, slabs, own_t, pno, done=None):
    sides = own_t.shape[0] // pno * 2
    shape = jax.ShapeDtypeStruct((sides + 1, slabs[0].shape[1], pno), jnp.bfloat16)
    if done is None:
        return call_kernel(functools.partial(halves_kernel, base), shape, [], "halves", (uses,), (*slabs, own_t), 0)
    args = (*slabs, own_t, done)
    return call_kernel(
        functools.partial(more_halves_kernel, base), shape, [], "more_halves", (uses,), args, 0, aliases={len(args): 0}
    )


def add_exchange(uses, turn, base, slabs, own_t, early, acc):
    body = functools.partial(exchange_body, 1.0 / math.sqrt(slabs[0].shape[1]), base)
    scratch = [pltpu.VMEM(early.shape, jnp.bfloat16)]
    return summed_kernel(body, "exchange", (uses, turn), (*slabs, own_t, early), scratch, acc, acc.shape, 0)


def slab_uses(slab_owner, pair_orbs, order):
    n_dev = order.shape[0]
    sides = pair_orbs.shape[0] * 2
    table = jnp.arange(n_dev, dtype=jnp.int32)
    position = jnp.sum(jnp.where(pair_orbs.reshape(sides)[:, None] == table, slab_owner, 0), axis=1)
    turn = jnp.sum(jnp.where(position[:, None] == table, order, 0), axis=1).astype(jnp.int32)
    hit = turn[:, None] == table
    side = jnp.arange(sides, dtype=jnp.int32)[:, None]
    last = jnp.max(jnp.where(hit, side, -1), axis=0)
    first = jnp.min(jnp.where(hit, side, sides), axis=0)
    return turn.reshape(-1, 2), jnp.stack([first, jnp.where(last < 0, sides, last)], axis=1)


def pack_kernel(base_ref, amp_ref, low_ref, high_ref, sems):
    half, orbs = low_ref.shape[0], base_ref.shape[1]
    copies = []
    for k, out_ref in enumerate((low_ref, high_ref)):
        rows = pl.ds(k * half, half)
        copies.append(pltpu.make_async_copy(base_ref.at[rows], out_ref.at[:, pl.ds(0, orbs)], sems.at[2 * k]))
        copies.append(
            pltpu.make_async_copy(amp_ref.at[rows], out_ref.at[:, pl.ds(orbs, amp_ref.shape[1])], sems.at[2 * k + 1])
        )
    for copy in copies:
        copy.start()
    for copy in copies:
        copy.wait()


def pack(bases, amps):
    pairs, orbs, pno = bases.shape
    shape = jax.ShapeDtypeStruct((pairs // 2, orbs + pno, pno), bases.dtype)
    return pl.pallas_call(
        pack_kernel,
        out_shape=(shape, shape),
        in_specs=[HBM_SPEC] * 2,
        out_specs=(VMEM_SPEC, VMEM_SPEC),
        scratch_shapes=[pltpu.SemaphoreType.DMA((4,))],
        compiler_params=pltpu.CompilerParams(vmem_limit_bytes=4 * MARGIN),
        name="pack",
    )(bases, amps)


def after(value, *earlier):
    return lax.optimization_barrier((value,) + earlier)[0]


def slot_counts(coupled, coupled_len, cand_count, scale):
    live = jnp.arange(coupled.shape[1])[None, :] < coupled_len[:, None]
    hits = (coupled[:, :, None] == jnp.arange(cand_count, dtype=jnp.int32)[None, None, :]) & live[:, :, None]
    return jnp.sum(hits.astype(jnp.float32), axis=1) * scale


def on_device(integral_slabs, slab_owner, pair_orbs, domain_bases, amplitudes, coupled, coupled_len):
    n_grp, n_dev = lax.axis_size("grp"), lax.axis_size("dev")
    pairs, orbs, pno = domain_bases.shape
    group, me = lax.axis_index("grp"), lax.axis_index("dev")
    near1, near2, far = group ^ 1, group ^ 2, group ^ 3
    chips = n_dev // 2
    chip, core = me // 2, me % 2
    line = chips == 4

    half = pairs // 2
    own_lo, own_hi = pack(domain_bases, amplitudes)

    def along_x(value):
        return lax.ppermute(value, "grp", [(g, g ^ 1) for g in range(n_grp)])

    def along_y(value):
        return lax.ppermute(value, "grp", [(g, g ^ 2) for g in range(n_grp)])

    def next_chip(value):
        return lax.ppermute(value, "dev", [(d, (d + 2) % n_dev) for d in range(n_dev)])

    def other_core(value):
        return lax.ppermute(value, "dev", [(d, d ^ 1) for d in range(n_dev)])

    weights = slot_counts(coupled, coupled_len, n_grp * pairs, orbs / pno)
    own_t = jnp.swapaxes(domain_bases, 1, 2).reshape(pairs * pno, orbs)

    def add(acc, *parts, flops=DECLARED, own_t=own_t):
        first = jnp.stack([source * pairs + low for source, low, _ in parts]).astype(jnp.int32)
        return add_coupled(first, weights, own_t, [chunk for _, _, chunk in parts], acc, (pairs, pno, pno), flops)

    slab = integral_slabs[0]
    ring = chips <= 4
    position = jnp.arange(n_dev, dtype=jnp.int32)

    x_lo, y_hi = along_x(own_lo), along_y(own_hi)
    x_hi, y_lo = along_x(after(own_hi, own_lo)), along_y(after(own_lo, own_hi))
    far_hi, far_lo = along_x(y_hi), along_y(x_lo)

    if ring:
        round1 = next_chip(slab)
    acc = add(None, (group, 0, own_lo), (group, half, own_hi), own_t=after(own_t, round1) if ring else own_t)
    if ring:
        round2 = next_chip(round1)
        swap0, swap1 = other_core(after(slab, x_lo, y_hi)), other_core(after(round1, x_lo, y_hi))
    acc = add(acc, (near1, 0, x_lo), (near2, half, y_hi))
    if ring:
        order = 2 * ((chip - position // 2) % chips) + jnp.where(position % 2 == core, 0, 1)
        turn, uses = slab_uses(slab_owner, pair_orbs, order)
        slabs = [slab[None], swap0[None], round1[None], swap1[None]]
        halves = half_products(uses, 0, slabs, after(own_t, acc), pno)
        acc = after(acc, halves)
        round2 = after(round2, acc)
        round3, swap2 = next_chip(round2), other_core(round2)
    acc = add(acc, (near1, half, x_hi), (near2, 0, y_lo), flops=0)
    if ring:
        halves = half_products(uses, 4, [round2[None], swap2[None]], after(own_t, acc), pno, halves)
        acc = after(acc, halves)
        ahead, rest = 6, [round3[None], other_core(after(round3, acc))[None]]
    else:
        gathered = lax.all_gather(slab, "dev", axis=0, tiled=False)
        turn, uses = slab_uses(slab_owner, pair_orbs, position)
        ahead = n_dev // 2
        halves = half_products(uses, 0, [gathered[:ahead]], own_t, pno)
        rest = [gathered[ahead:]]
    acc = add_exchange(uses, turn, ahead, rest, own_t, halves, acc)
    return add(acc, (far, 0, far_lo), (far, half, far_hi), flops=0)


def solution(mesh):
    in_specs = (
        P("dev", None, None),
        P(),
        P(("grp", "dev"), None),
        P(("grp", "dev"), None, None),
        P(("grp", "dev"), None, None),
        P(("grp", "dev"), None),
        P(("grp", "dev")),
    )
    out_specs = P(("grp", "dev"), None, None)
    return jax.shard_map(
        on_device, mesh=mesh, in_specs=in_specs, out_specs=out_specs, check_vma=False
    )
```

```python
import functools
import math

import jax
import jax.numpy as jnp
from jax import lax
from jax.experimental import pallas as pl
from jax.experimental.pallas import tpu as pltpu
from jax.sharding import PartitionSpec as P

MARGIN = 2 * 1024 * 1024
DECLARED = 20_000_000_000
SMEM_SPEC = pl.BlockSpec(memory_space=pltpu.SMEM)
VMEM_SPEC = pl.BlockSpec(memory_space=pltpu.VMEM)
HBM_SPEC = pl.BlockSpec(memory_space=pltpu.HBM)


def call_kernel(body, out_shape, scratch, name, smem_args, vmem_args, flops, hbm_args=(), aliases={}):
    outs = out_shape if isinstance(out_shape, tuple) else (out_shape,)
    held = [a for a in (*vmem_args, *scratch, *outs) if a.dtype in (jnp.float32, jnp.bfloat16)]
    return pl.pallas_call(
        body,
        out_shape=out_shape,
        in_specs=[SMEM_SPEC] * len(smem_args) + [VMEM_SPEC] * len(vmem_args) + [HBM_SPEC] * len(hbm_args),
        out_specs=(VMEM_SPEC,) * len(outs) if isinstance(out_shape, tuple) else VMEM_SPEC,
        scratch_shapes=scratch,
        input_output_aliases=aliases,
        compiler_params=pltpu.CompilerParams(
            vmem_limit_bytes=sum(math.prod(a.shape) * a.dtype.itemsize for a in held) + MARGIN
        ),
        cost_estimate=pl.CostEstimate(flops=flops, bytes_accessed=0, transcendentals=0),
        name=name,
    )(*smem_args, *vmem_args, *hbm_args)


def coupled_sums(left_ref, bases, amps, weight, count, inter_ref, proj_ref):
    rows, pno = left_ref.shape[0], amps(0).shape[0]
    empty = jnp.zeros((pno, pno), jnp.bfloat16)
    for j in range(0, count, 2):
        pair = jnp.concatenate([bases(j), bases(j + 1)], axis=1)
        inter = jnp.dot(left_ref[...], pair, preferred_element_type=jnp.float32).astype(jnp.bfloat16)
        inter_ref[:, j * pno : (j + 2) * pno] = inter
        diagonal = jnp.concatenate(
            [jnp.concatenate([amps(j), empty], axis=1), jnp.concatenate([empty, amps(j + 1)], axis=1)], axis=0
        )
        proj = jnp.dot(inter, diagonal, preferred_element_type=jnp.float32)
        for p in range(rows // pno):
            for c in range(2):
                block = proj[p * pno : (p + 1) * pno, c * pno : (c + 1) * pno]
                proj_ref[p * pno : (p + 1) * pno, (j + c) * pno : (j + c + 1) * pno] = (
                    block * weight(p, j + c)
                ).astype(jnp.bfloat16)

    def total(p):
        at = slice(p * pno, (p + 1) * pno)
        return lax.dot_general(
            proj_ref[at, :], inter_ref[at, :], (((1,), (1,)), ((), ())), preferred_element_type=jnp.float32
        )

    return total


def own_kernel(weight_ref, left_ref, low_ref, high_ref, out_ref, inter_ref, proj_ref):
    pairs, pno, _ = out_ref.shape
    orbs, half = left_ref.shape[1], pairs // 2
    packs = [(low_ref, k) for k in range(half)] + [(high_ref, k) for k in range(half)]
    total = coupled_sums(
        left_ref,
        lambda c: packs[c][0][packs[c][1], :orbs, :],
        lambda c: packs[c][0][packs[c][1], orbs : orbs + pno, :],
        lambda p, c: weight_ref[p, c],
        pairs,
        inter_ref,
        proj_ref,
    )
    for p in range(pairs):
        out_ref[p] = total(p)


def both_kernel(mine_at, theirs_at, weight_ref, left_ref, low_ref, high_ref, acc_ref, *refs):
    in_low, in_high, out_ref, back_ref, held_ref, turned_ref, inter_ref, proj_ref, sems = refs
    pairs, pno, _ = out_ref.shape
    orbs, half = left_ref.shape[1], pairs // 2
    copies = [
        pltpu.make_async_copy((in_low, in_high)[q // half].at[q % half], held_ref.at[q], sems.at[q]) for q in range(pairs)
    ]
    for copy in copies:
        copy.start()

    def their_basis(q):
        copies[q].wait()
        return held_ref[q, :orbs, :]

    total = coupled_sums(
        left_ref,
        their_basis,
        lambda q: held_ref[q, orbs : orbs + pno, :],
        lambda p, q: weight_ref[p, mine_at + q],
        pairs,
        inter_ref,
        proj_ref,
    )
    for p in range(pairs):
        out_ref[p] = acc_ref[p] + total(p)
    for q in range(pairs):
        turned_ref[q * pno : (q + 1) * pno, :] = held_ref[q, :orbs, :].T
    counts = [held_ref[q, orbs + pno :, :].astype(jnp.float32) for q in range(pairs)]
    packs = [(low_ref, k) for k in range(half)] + [(high_ref, k) for k in range(half)]
    total = coupled_sums(
        turned_ref,
        lambda p: packs[p][0][packs[p][1], :orbs, :],
        lambda p: packs[p][0][packs[p][1], orbs : orbs + pno, :],
        lambda q, p: counts[q][0:1, theirs_at + p : theirs_at + p + 1],
        pairs,
        inter_ref,
        proj_ref,
    )
    for q in range(pairs):
        back_ref[q] = total(q).astype(jnp.bfloat16)


def coupled_scratch(rows):
    return [pltpu.VMEM((rows, rows), jnp.bfloat16)] * 2


def own_coupled(weights, own_t, packs):
    rows, pairs = own_t.shape[0], weights.shape[0]
    shape = jax.ShapeDtypeStruct((pairs, rows // pairs, rows // pairs), jnp.float32)
    return call_kernel(own_kernel, shape, coupled_scratch(rows), "own_coupled", (weights,), (own_t, *packs), DECLARED)


def both_coupled(mine_at, theirs_at, weights, own_t, packs, acc, received, flops):
    pairs = acc.shape[0]
    shapes = (jax.ShapeDtypeStruct(acc.shape, jnp.float32), jax.ShapeDtypeStruct(acc.shape, jnp.bfloat16))
    scratch = [
        pltpu.VMEM((pairs,) + received[0].shape[1:], jnp.bfloat16),
        pltpu.VMEM(own_t.shape, jnp.bfloat16),
        *coupled_scratch(own_t.shape[0]),
        pltpu.SemaphoreType.DMA((pairs,)),
    ]
    body = functools.partial(both_kernel, mine_at, theirs_at)
    return call_kernel(
        body, shapes, scratch, "both_coupled", (weights,), (own_t, *packs, acc), flops, hbm_args=tuple(received)
    )


def half_transforms(uses_ref, slab_refs, own_ref, half_ref, base):
    pno = half_ref.shape[2]
    last = own_ref.shape[0] // pno - 1

    def rows(side):
        return own_ref[pl.ds(pl.multiple_of(jnp.minimum(side // 2, last) * pno, pno), pno), :]

    def both_sides(slab, k):
        one, two = uses_ref[k, 0], uses_ref[k, 1]
        bases = jnp.concatenate([rows(one), rows(two)], axis=0)
        both = lax.dot_general(slab, bases, (((1,), (1,)), ((), ())), preferred_element_type=jnp.float32)
        both = both.astype(jnp.bfloat16)
        half_ref[one] = both[:, :pno]
        half_ref[two] = both[:, pno:]

    for slab_ref in slab_refs:
        if slab_ref.shape[0] > 4:

            def step(k, carry, slab_ref=slab_ref, base=base):
                both_sides(slab_ref[k], base + k)
                return carry

            lax.fori_loop(0, slab_ref.shape[0], step, 0)
        else:
            for k in range(slab_ref.shape[0]):
                both_sides(slab_ref[k], base + k)
        base += slab_ref.shape[0]


def halves_kernel(base, uses_ref, *refs):
    *slab_refs, own_ref, half_ref = refs
    half_transforms(uses_ref, slab_refs, own_ref, half_ref, base)


def more_halves_kernel(base, uses_ref, *refs):
    *slab_refs, own_ref, _, half_ref = refs
    half_transforms(uses_ref, slab_refs, own_ref, half_ref, base)


def exchange_kernel(scale, base, uses_ref, turn_ref, *refs):
    *slab_refs, own_ref, early_ref, acc_ref, back1_ref, back2_ref, out_ref, half_ref = refs
    half_transforms(uses_ref, slab_refs, own_ref, half_ref, base)
    for p in range(out_ref.shape[0]):
        left, right = [
            jnp.where(turn_ref[p, side] < base, early_ref[2 * p + side], half_ref[2 * p + side]) for side in range(2)
        ]
        product = lax.dot_general(left, right, (((0,), (0,)), ((), ())), preferred_element_type=jnp.float32)
        back = back1_ref[p].astype(jnp.float32) + back2_ref[p].astype(jnp.float32)
        out_ref[p] = acc_ref[p] + back + product * scale


def half_products(uses, base, slabs, own_t, pno, done=None):
    sides = own_t.shape[0] // pno * 2
    shape = jax.ShapeDtypeStruct((sides + 1, slabs[0].shape[1], pno), jnp.bfloat16)
    if done is None:
        return call_kernel(functools.partial(halves_kernel, base), shape, [], "halves", (uses,), (*slabs, own_t), 0)
    args = (*slabs, own_t, done)
    return call_kernel(
        functools.partial(more_halves_kernel, base), shape, [], "more_halves", (uses,), args, DECLARED, aliases={len(args): 0}
    )


def add_exchange(uses, turn, base, slabs, own_t, early, sums):
    return call_kernel(
        functools.partial(exchange_kernel, 1.0 / math.sqrt(slabs[0].shape[1]), base),
        jax.ShapeDtypeStruct(sums[0].shape, jnp.float32),
        [pltpu.VMEM(early.shape, jnp.bfloat16)],
        "exchange",
        (uses, turn),
        (*slabs, own_t, early, *sums),
        0,
    )


def slab_uses(slab_owner, pair_orbs, order):
    n_dev = order.shape[0]
    sides = pair_orbs.shape[0] * 2
    table = jnp.arange(n_dev, dtype=jnp.int32)
    position = jnp.sum(jnp.where(pair_orbs.reshape(sides)[:, None] == table, slab_owner, 0), axis=1)
    turn = jnp.sum(jnp.where(position[:, None] == table, order, 0), axis=1).astype(jnp.int32)
    hit = turn[:, None] == table
    side = jnp.arange(sides, dtype=jnp.int32)[:, None]
    last = jnp.max(jnp.where(hit, side, -1), axis=0)
    first = jnp.min(jnp.where(hit, side, sides), axis=0)
    return turn.reshape(-1, 2), jnp.stack([first, jnp.where(last < 0, sides, last)], axis=1)


def pack_kernel(base_ref, amp_ref, count_ref, low_ref, high_ref, sems):
    half = low_ref.shape[0]
    copies = []
    for k, out_ref in enumerate((low_ref, high_ref)):
        row = 0
        for part, ref in enumerate((base_ref, amp_ref, count_ref)):
            rows = pl.ds(row, ref.shape[1])
            row += ref.shape[1]
            copies.append(
                pltpu.make_async_copy(ref.at[pl.ds(k * half, half)], out_ref.at[:, rows], sems.at[3 * k + part])
            )
    for copy in copies:
        copy.start()
    for copy in copies:
        copy.wait()


def pack(bases, amps, counts):
    pairs, _, pno = bases.shape
    counts = jnp.pad(counts.astype(jnp.bfloat16)[:, None, :], ((0, 0), (0, 15), (0, pno - counts.shape[1])))
    rows = bases.shape[1] + amps.shape[1] + counts.shape[1]
    shape = jax.ShapeDtypeStruct((pairs // 2, rows, pno), bases.dtype)
    return pl.pallas_call(
        pack_kernel,
        out_shape=(shape, shape),
        in_specs=[HBM_SPEC] * 3,
        out_specs=(VMEM_SPEC, VMEM_SPEC),
        scratch_shapes=[pltpu.SemaphoreType.DMA((6,))],
        compiler_params=pltpu.CompilerParams(vmem_limit_bytes=4 * MARGIN),
        name="pack",
    )(bases, amps, counts)


def after(value, *earlier):
    return lax.optimization_barrier((value,) + earlier)[0]


def slot_counts(coupled, coupled_len, cand_count, scale):
    live = jnp.arange(coupled.shape[1])[None, :] < coupled_len[:, None]
    hits = (coupled[:, :, None] == jnp.arange(cand_count, dtype=jnp.int32)[None, None, :]) & live[:, :, None]
    return jnp.sum(hits.astype(jnp.float32), axis=1) * scale


def on_device(integral_slabs, slab_owner, pair_orbs, domain_bases, amplitudes, coupled, coupled_len):
    n_grp, n_dev = lax.axis_size("grp"), lax.axis_size("dev")
    pairs, orbs, pno = domain_bases.shape
    group, me = lax.axis_index("grp"), lax.axis_index("dev")
    chips = n_dev // 2
    chip, core = me // 2, me % 2

    ring = (0, 1, 3, 2)
    following = ({g: ring[(i + 1) % 4] for i, g in enumerate(ring)}, {g: ring[i - 1] for i, g in enumerate(ring)})

    def between_groups(value, moves):
        pairs_of = [(a * n_dev + d, b * n_dev + d) for d in range(n_dev) for a, b in moves[d % 2]]
        return lax.ppermute(value, ("grp", "dev"), pairs_of)

    onward = [list(f.items()) for f in following]
    backward = [[(b, a) for a, b in moves] for moves in onward]
    across = [[(1, 3), (3, 2)], [(1, 0), (3, 1)]]
    across_back = [[(3, 0), (2, 1)], [(0, 3), (1, 2)]]

    def next_chip(value):
        return lax.ppermute(value, "dev", [(d, (d + 2) % n_dev) for d in range(n_dev)])

    def other_core(value):
        return lax.ppermute(value, "dev", [(d, d ^ 1) for d in range(n_dev)])

    place = sum(jnp.where(group == g, i, 0) for i, g in enumerate(ring))
    source = coupled // pairs
    source_place = sum(jnp.where(source == g, i, 0) for i, g in enumerate(ring))
    block = jnp.where(core == 0, source_place - place, place - source_place) % 4
    weights = slot_counts(block * pairs + coupled % pairs, coupled_len, n_grp * pairs, orbs / pno)
    own = pack(domain_bases, amplitudes, weights)
    own_t = jnp.swapaxes(domain_bases, 1, 2).reshape(pairs * pno, orbs)

    before_lo, before_hi = between_groups(own[0], onward), between_groups(own[1], onward)
    far_lo, far_hi = between_groups(before_lo, across), between_groups(before_hi, across)

    slab = integral_slabs[0]
    around = chips <= 4
    position = jnp.arange(n_dev, dtype=jnp.int32)
    if around:
        round1 = next_chip(slab)
        round2 = next_chip(round1)
        order = 2 * ((chip - position // 2) % chips) + jnp.where(position % 2 == core, 0, 1)
        turn, uses = slab_uses(slab_owner, pair_orbs, order)
        ahead = 6
    else:
        turn, uses = slab_uses(slab_owner, pair_orbs, position)
        ahead = n_dev // 2
    acc = own_coupled(weights, own_t, own)
    if around:
        swap0, swap1 = other_core(after(slab, before_lo)), other_core(after(round1, before_lo))
    acc, back = both_coupled(
        3 * pairs, pairs, weights, own_t, own, acc, (before_lo, before_hi), DECLARED
    )
    back1 = between_groups(back, backward)
    if around:
        slabs = [slab[None], swap0[None], round1[None], swap1[None]]
        halves = half_products(uses, 0, slabs, after(own_t, acc), pno)
        acc = after(acc, halves)
        round2 = after(round2, acc)
        round3, swap2 = next_chip(round2), other_core(round2)
    else:
        gathered = lax.all_gather(slab, "dev", axis=0, tiled=False)
        halves = half_products(uses, 0, [gathered[:ahead]], own_t, pno)
        rest = [gathered[ahead:]]
    acc, back = both_coupled(
        2 * pairs, 2 * pairs, weights, own_t, own, acc, (far_lo, far_hi), 0
    )
    back2 = between_groups(back, across_back)
    if around:
        round3 = after(round3, acc)
        rest = [round3[None], other_core(round3)[None]]
        halves = half_products(uses, 4, [round2[None], swap2[None]], after(own_t, acc, back1), pno, halves)
    return add_exchange(uses, turn, ahead, rest, own_t, halves, (acc, back1, back2))


def solution(mesh):
    in_specs = (
        P("dev", None, None),
        P(),
        P(("grp", "dev"), None),
        P(("grp", "dev"), None, None),
        P(("grp", "dev"), None, None),
        P(("grp", "dev"), None),
        P(("grp", "dev")),
    )
    out_specs = P(("grp", "dev"), None, None)
    return jax.shard_map(
        on_device, mesh=mesh, in_specs=in_specs, out_specs=out_specs, check_vma=False
    )
```

```python
import functools
import math

import jax
import jax.numpy as jnp
from jax import lax
from jax.experimental import pallas as pl
from jax.experimental.pallas import tpu as pltpu
from jax.sharding import PartitionSpec as P

MARGIN = 2 * 1024 * 1024
DECLARED = 20_000_000_000
OWN_COST, NEIGHBOUR_COST, ACROSS_COST = 0, DECLARED, DECLARED
SMEM_SPEC = pl.BlockSpec(memory_space=pltpu.SMEM)
VMEM_SPEC = pl.BlockSpec(memory_space=pltpu.VMEM)
HBM_SPEC = pl.BlockSpec(memory_space=pltpu.HBM)


def call_kernel(body, out_shape, scratch, name, smem_args, vmem_args, flops, hbm_args=(), aliases={}):
    outs = out_shape if isinstance(out_shape, tuple) else (out_shape,)
    held = [a for a in (*vmem_args, *scratch, *outs) if a.dtype in (jnp.float32, jnp.bfloat16)]
    return pl.pallas_call(
        body,
        out_shape=out_shape,
        in_specs=[SMEM_SPEC] * len(smem_args) + [VMEM_SPEC] * len(vmem_args) + [HBM_SPEC] * len(hbm_args),
        out_specs=(VMEM_SPEC,) * len(outs) if isinstance(out_shape, tuple) else VMEM_SPEC,
        scratch_shapes=scratch,
        input_output_aliases=aliases,
        compiler_params=pltpu.CompilerParams(
            vmem_limit_bytes=sum(math.prod(a.shape) * a.dtype.itemsize for a in held) + MARGIN
        ),
        cost_estimate=pl.CostEstimate(flops=flops, bytes_accessed=0, transcendentals=0),
        name=name,
    )(*smem_args, *vmem_args, *hbm_args)


class Side:
    def __init__(self, left, packs, orbs, pno):
        self.left, self.packs, self.orbs, self.pno = left, packs, orbs, pno

    def basis(self, k):
        return self.packs[k][: self.orbs, :]

    def amps(self, k):
        return self.packs[k][self.orbs : self.orbs + self.pno, :]

    def counts(self, k):
        return self.packs[k][self.orbs + self.pno :, :].astype(jnp.float32)


def project(side, other, at, inter_ref, proj_ref):
    pno = side.pno
    empty = jnp.zeros((pno, pno), jnp.bfloat16)
    counts = [side.counts(p) for p in range(len(side.packs))]
    for j in range(0, len(other.packs), 2):
        pair = jnp.concatenate([other.basis(j), other.basis(j + 1)], axis=1)
        inter = jnp.dot(side.left[...], pair, preferred_element_type=jnp.float32).astype(jnp.bfloat16)
        inter_ref[:, j * pno : (j + 2) * pno] = inter
        diagonal = jnp.concatenate(
            [
                jnp.concatenate([other.amps(j), empty], axis=1),
                jnp.concatenate([empty, other.amps(j + 1)], axis=1),
            ],
            axis=0,
        )
        proj = jnp.dot(inter, diagonal, preferred_element_type=jnp.float32)
        for p, count in enumerate(counts):
            for c in range(2):
                block = proj[p * pno : (p + 1) * pno, c * pno : (c + 1) * pno]
                proj_ref[p * pno : (p + 1) * pno, (j + c) * pno : (j + c + 1) * pno] = (
                    block * count[0:1, at + j + c : at + j + c + 1]
                ).astype(jnp.bfloat16)


def own_kernel(left_ref, pack_ref, out_ref, inter_ref, proj_ref):
    pairs, pno, _ = out_ref.shape
    own = Side(left_ref, [pack_ref.at[k] for k in range(pairs)], left_ref.shape[1], pno)
    project(own, own, 0, inter_ref, proj_ref)
    for p in range(pairs):
        at = slice(p * pno, (p + 1) * pno)
        out_ref[p] = lax.dot_general(
            proj_ref[at, :], inter_ref[at, :], (((1,), (1,)), ((), ())), preferred_element_type=jnp.float32
        )


def both_sums(one, two, one_at, two_at, refs):
    rows, columns, pno = len(one.packs) * one.pno, len(two.packs) * one.pno, one.pno
    one_inter, one_proj = [ref.at[:rows, :columns] for ref in refs[:2]]
    two_inter, two_proj = [ref.at[:columns, :rows] for ref in refs[2:]]
    project(one, two, one_at, one_inter, one_proj)
    project(two, one, two_at, two_inter, two_proj)

    def total(proj, inter):
        def of(k):
            at = slice(k * pno, (k + 1) * pno)
            return jnp.dot(proj[at, :], inter[:, at], preferred_element_type=jnp.float32)

        return of

    return total(one_proj, two_inter), total(two_proj, one_inter)


def turn(packs, left_ref, orbs):
    pno = packs[0].shape[1]
    for k, ref in enumerate(packs):
        left_ref[k * pno : (k + 1) * pno, :] = ref[:orbs, :].T


def neighbour_kernel(left_ref, pack_ref, acc_ref, in_ref, out_ref, back_ref, held_ref, turned_ref, *refs):
    *products, sems = refs
    pairs, pno, _ = out_ref.shape
    orbs = left_ref.shape[1]
    copies = [pltpu.make_async_copy(in_ref.at[q], held_ref.at[q], sems.at[q]) for q in range(pairs)]
    for copy in copies:
        copy.start()
    for copy in copies:
        copy.wait()
    own = Side(left_ref, [pack_ref.at[k] for k in range(pairs)], orbs, pno)
    their = Side(turned_ref, [held_ref.at[k] for k in range(pairs)], orbs, pno)
    turn(their.packs, turned_ref, orbs)
    mine, back = both_sums(own, their, 3 * pairs, pairs, products)
    for p in range(pairs):
        back_ref[p] = back(p).astype(jnp.bfloat16)
        out_ref[p] = acc_ref[p] + mine(p)


def across_kernel(upper_ref, left_ref, pack_ref, acc_ref, in_ref, out_ref, back_ref, held_ref, turned_ref, *refs):
    *products, sems = refs
    pairs, pno, _ = out_ref.shape
    orbs, half = left_ref.shape[1], pairs // 2
    copies = [pltpu.make_async_copy(in_ref.at[q], held_ref.at[q], sems.at[q]) for q in range(pairs)]
    for copy in copies:
        copy.start()
    for copy in copies:
        copy.wait()
    own_packs = [pack_ref.at[k] for k in range(pairs)]
    their_packs = [held_ref.at[k] for k in range(pairs)]

    @pl.when(upper_ref[0] == 1)
    def _():
        turn(their_packs, turned_ref, orbs)
        one = Side(left_ref.at[half * pno :, :], own_packs[half:], orbs, pno)
        two = Side(turned_ref, their_packs, orbs, pno)
        mine, back = both_sums(one, two, 2 * pairs, 2 * pairs + half, products)
        for p in range(pairs):
            back_ref[p] = back(p).astype(jnp.bfloat16)
            out_ref[p] = acc_ref[p] if p < half else acc_ref[p] + mine(p - half)

    @pl.when(upper_ref[0] == 0)
    def _():
        turn(their_packs[:half], turned_ref, orbs)
        one = Side(turned_ref.at[: half * pno, :], their_packs[:half], orbs, pno)
        two = Side(left_ref, own_packs, orbs, pno)
        back, mine = both_sums(one, two, 2 * pairs, 2 * pairs, products)
        for p in range(pairs):
            back_ref[p] = back(p).astype(jnp.bfloat16) if p < half else jnp.zeros((pno, pno), jnp.bfloat16)
            out_ref[p] = acc_ref[p] + mine(p)


def own_coupled(own_t, own, flops):
    rows, pairs = own_t.shape[0], own.shape[0]
    shape = jax.ShapeDtypeStruct((pairs, rows // pairs, rows // pairs), jnp.float32)
    scratch = [pltpu.VMEM((rows, rows), jnp.bfloat16)] * 2
    return call_kernel(own_kernel, shape, scratch, "own_coupled", (), (own_t, own), flops)


def both_coupled(body, name, scalars, own_t, own, acc, received, flops, rows):
    shapes = (jax.ShapeDtypeStruct(acc.shape, jnp.float32), jax.ShapeDtypeStruct(acc.shape, jnp.bfloat16))
    wide = own_t.shape[0]
    scratch = [
        pltpu.VMEM(received.shape, jnp.bfloat16),
        pltpu.VMEM(own_t.shape, jnp.bfloat16),
        *[pltpu.VMEM((rows, wide), jnp.bfloat16)] * 2,
        *[pltpu.VMEM((wide, rows), jnp.bfloat16)] * 2,
        pltpu.SemaphoreType.DMA((received.shape[0],)),
    ]
    return call_kernel(body, shapes, scratch, name, scalars, (own_t, own, acc), flops, hbm_args=(received,))


def half_transforms(uses_ref, slab_refs, own_ref, half_ref, base):
    pno = half_ref.shape[2]
    last = own_ref.shape[0] // pno - 1

    def rows(side):
        return own_ref[pl.ds(pl.multiple_of(jnp.minimum(side // 2, last) * pno, pno), pno), :]

    def both_sides(slab, k):
        one, two = uses_ref[k, 0], uses_ref[k, 1]
        bases = jnp.concatenate([rows(one), rows(two)], axis=0)
        both = lax.dot_general(slab, bases, (((1,), (1,)), ((), ())), preferred_element_type=jnp.float32)
        both = both.astype(jnp.bfloat16)
        half_ref[one] = both[:, :pno]
        half_ref[two] = both[:, pno:]

    for slab_ref in slab_refs:
        if slab_ref.shape[0] > 4:

            def step(k, carry, slab_ref=slab_ref, base=base):
                both_sides(slab_ref[k], base + k)
                return carry

            lax.fori_loop(0, slab_ref.shape[0], step, 0)
        else:
            for k in range(slab_ref.shape[0]):
                both_sides(slab_ref[k], base + k)
        base += slab_ref.shape[0]


def halves_kernel(base, uses_ref, *refs):
    *slab_refs, own_ref, half_ref = refs
    half_transforms(uses_ref, slab_refs, own_ref, half_ref, base)


def exchange_kernel(scale, base, uses_ref, turn_ref, *refs):
    *slab_refs, own_ref, early_ref, acc_ref, back1_ref, back2_ref, out_ref, half_ref = refs
    half_transforms(uses_ref, slab_refs, own_ref, half_ref, base)
    for p in range(out_ref.shape[0]):
        left, right = [
            jnp.where(turn_ref[p, side] < base, early_ref[2 * p + side], half_ref[2 * p + side]) for side in range(2)
        ]
        product = lax.dot_general(left, right, (((0,), (0,)), ((), ())), preferred_element_type=jnp.float32)
        back = back1_ref[p].astype(jnp.float32) + back2_ref[p].astype(jnp.float32)
        out_ref[p] = acc_ref[p] + back + product * scale


def half_products(uses, base, slabs, own_t, pno):
    sides = own_t.shape[0] // pno * 2
    shape = jax.ShapeDtypeStruct((sides + 1, slabs[0].shape[1], pno), jnp.bfloat16)
    return call_kernel(functools.partial(halves_kernel, base), shape, [], "halves", (uses,), (*slabs, own_t), 0)


def add_exchange(uses, turn, base, slabs, own_t, early, sums):
    return call_kernel(
        functools.partial(exchange_kernel, 1.0 / math.sqrt(slabs[0].shape[1]), base),
        jax.ShapeDtypeStruct(sums[0].shape, jnp.float32),
        [pltpu.VMEM(early.shape, jnp.bfloat16)],
        "exchange",
        (uses, turn),
        (*slabs, own_t, early, *sums),
        0,
    )


def slab_uses(slab_owner, pair_orbs, order):
    n_dev = order.shape[0]
    sides = pair_orbs.shape[0] * 2
    table = jnp.arange(n_dev, dtype=jnp.int32)
    position = jnp.sum(jnp.where(pair_orbs.reshape(sides)[:, None] == table, slab_owner, 0), axis=1)
    turn = jnp.sum(jnp.where(position[:, None] == table, order, 0), axis=1).astype(jnp.int32)
    hit = turn[:, None] == table
    side = jnp.arange(sides, dtype=jnp.int32)[:, None]
    last = jnp.max(jnp.where(hit, side, -1), axis=0)
    first = jnp.min(jnp.where(hit, side, sides), axis=0)
    return turn.reshape(-1, 2), jnp.stack([first, jnp.where(last < 0, sides, last)], axis=1)


def pack_kernel(base_ref, amp_ref, count_ref, out_ref, sems):
    copies, row = [], 0
    for part, ref in enumerate((base_ref, amp_ref, count_ref)):
        rows = pl.ds(row, ref.shape[1])
        row += ref.shape[1]
        copies.append(pltpu.make_async_copy(ref, out_ref.at[:, rows], sems.at[part]))
    for copy in copies:
        copy.start()
    for copy in copies:
        copy.wait()


def pack(bases, amps, counts):
    pairs, _, pno = bases.shape
    counts = jnp.pad(counts.astype(jnp.bfloat16)[:, None, :], ((0, 0), (0, 15), (0, pno - counts.shape[1])))
    rows = bases.shape[1] + amps.shape[1] + counts.shape[1]
    return pl.pallas_call(
        pack_kernel,
        out_shape=jax.ShapeDtypeStruct((pairs, rows, pno), bases.dtype),
        in_specs=[HBM_SPEC] * 3,
        out_specs=VMEM_SPEC,
        scratch_shapes=[pltpu.SemaphoreType.DMA((3,))],
        compiler_params=pltpu.CompilerParams(vmem_limit_bytes=4 * MARGIN),
        name="pack",
    )(bases, amps, counts)


def after(value, *earlier):
    return lax.optimization_barrier((value,) + earlier)[0]


def slot_counts(coupled, coupled_len, cand_count, scale):
    live = jnp.arange(coupled.shape[1])[None, :] < coupled_len[:, None]
    hits = (coupled[:, :, None] == jnp.arange(cand_count, dtype=jnp.int32)[None, None, :]) & live[:, :, None]
    return jnp.sum(hits.astype(jnp.float32), axis=1) * scale


def on_device(integral_slabs, slab_owner, pair_orbs, domain_bases, amplitudes, coupled, coupled_len):
    n_grp, n_dev = lax.axis_size("grp"), lax.axis_size("dev")
    pairs, orbs, pno = domain_bases.shape
    group, me = lax.axis_index("grp"), lax.axis_index("dev")
    chips = n_dev // 2
    chip, core = me // 2, me % 2

    ring = (0, 1, 3, 2)
    following = ({g: ring[(i + 1) % 4] for i, g in enumerate(ring)}, {g: ring[i - 1] for i, g in enumerate(ring)})

    def between_groups(value, moves):
        pairs_of = [(a * n_dev + d, b * n_dev + d) for d in range(n_dev) for a, b in moves[d % 2]]
        return lax.ppermute(value, ("grp", "dev"), pairs_of)

    onward = [list(f.items()) for f in following]
    backward = [[(b, a) for a, b in moves] for moves in onward]

    def along_chips(value, step):
        return lax.ppermute(value, "dev", [(d, (d + 2 * step) % n_dev) for d in range(n_dev)])

    def other_core(value):
        return lax.ppermute(value, "dev", [(d, d ^ 1) for d in range(n_dev)])

    place = sum(jnp.where(group == g, i, 0) for i, g in enumerate(ring))
    source = coupled // pairs
    source_place = sum(jnp.where(source == g, i, 0) for i, g in enumerate(ring))
    block = jnp.where(core == 0, source_place - place, place - source_place) % 4
    counts = slot_counts(block * pairs + coupled % pairs, coupled_len, n_grp * pairs, orbs / pno)
    own = pack(domain_bases, amplitudes, counts)
    own_t = jnp.swapaxes(domain_bases, 1, 2).reshape(pairs * pno, orbs)
    upper = jnp.where(place >= 2, 1, 0).astype(jnp.int32).reshape(1)

    before = between_groups(own, onward)
    far = between_groups(before, onward)

    slab = integral_slabs[0]
    around = chips == 4
    position = jnp.arange(n_dev, dtype=jnp.int32)
    if around:
        below, above = along_chips(slab, 1), along_chips(slab, -1)
        beyond = along_chips(below, 1)
        steps = (chip - position // 2) % chips
        late = jnp.where(steps == 2, 6, jnp.where(steps == 3, 4, 2 * steps))
        order = late + jnp.where(position % 2 == core, 0, 1)
        ahead = 6
    else:
        order, ahead = position, n_dev // 2
    turns, uses = slab_uses(slab_owner, pair_orbs, order)
    acc = own_coupled(own_t, own, OWN_COST)
    acc, back = both_coupled(
        neighbour_kernel, "neighbour", (), own_t, own, acc, before, NEIGHBOUR_COST, own_t.shape[0]
    )
    back1 = between_groups(back, backward)
    if around:
        held = [slab, below, above]
        pieces = [value[None] for value in held + [other_core(after(value, acc)) for value in held]]
        slabs = [pieces[i] for i in (0, 3, 1, 4, 2, 5)]
    else:
        gathered = lax.all_gather(slab, "dev", axis=0, tiled=False)
        slabs, rest = [gathered[:ahead]], [gathered[ahead:]]
    halves = half_products(uses, 0, slabs, after(own_t, acc), pno)
    acc = after(acc, halves, back1)
    acc, back = both_coupled(
        across_kernel, "across", (upper,), own_t, own, acc, far, ACROSS_COST, own_t.shape[0] // 2
    )
    back2 = lax.ppermute(back, "grp", [(g, g ^ 3) for g in range(n_grp)])
    if around:
        beyond = after(beyond, halves)
        rest = [beyond[None], other_core(beyond)[None]]
    return add_exchange(uses, turns, ahead, rest, own_t, halves, (acc, back1, back2))


def solution(mesh):
    in_specs = (
        P("dev", None, None),
        P(),
        P(("grp", "dev"), None),
        P(("grp", "dev"), None, None),
        P(("grp", "dev"), None, None),
        P(("grp", "dev"), None),
        P(("grp", "dev")),
    )
    out_specs = P(("grp", "dev"), None, None)
    return jax.shard_map(
        on_device, mesh=mesh, in_specs=in_specs, out_specs=out_specs, check_vma=False
    )
```

```python
import functools
import math

import jax
import jax.numpy as jnp
from jax import lax
from jax.experimental import pallas as pl
from jax.experimental.pallas import tpu as pltpu
from jax.sharding import PartitionSpec as P

MARGIN = 2 * 1024 * 1024
DECLARED = 20_000_000_000
OWN_COST, FIRST_COST, SECOND_COST, LAST_COST = 0, 0, 0, DECLARED
SMEM_SPEC = pl.BlockSpec(memory_space=pltpu.SMEM)
VMEM_SPEC = pl.BlockSpec(memory_space=pltpu.VMEM)
HBM_SPEC = pl.BlockSpec(memory_space=pltpu.HBM)


def call_kernel(body, out_shape, scratch, name, smem_args, vmem_args, flops, hbm_args=(), aliases={}):
    outs = out_shape if isinstance(out_shape, tuple) else (out_shape,)
    held = [a for a in (*vmem_args, *scratch, *outs) if a.dtype in (jnp.float32, jnp.bfloat16)]
    return pl.pallas_call(
        body,
        out_shape=out_shape,
        in_specs=[SMEM_SPEC] * len(smem_args) + [VMEM_SPEC] * len(vmem_args) + [HBM_SPEC] * len(hbm_args),
        out_specs=(VMEM_SPEC,) * len(outs) if isinstance(out_shape, tuple) else VMEM_SPEC,
        scratch_shapes=scratch,
        input_output_aliases=aliases,
        compiler_params=pltpu.CompilerParams(
            vmem_limit_bytes=sum(math.prod(a.shape) * a.dtype.itemsize for a in held) + MARGIN
        ),
        cost_estimate=pl.CostEstimate(flops=flops, bytes_accessed=0, transcendentals=0),
        name=name,
    )(*smem_args, *vmem_args, *hbm_args)


class Side:
    def __init__(self, left, packs, orbs, pno):
        self.left, self.packs, self.orbs, self.pno = left, packs, orbs, pno

    def basis(self, k):
        return self.packs[k][: self.orbs, :]

    def amps(self, k):
        return self.packs[k][self.orbs : self.orbs + self.pno, :]

    def counts(self, k):
        return self.packs[k][self.orbs + self.pno :, :].astype(jnp.float32)


def project(side, other, lanes, inter_ref, proj_ref, copies=()):
    pno = side.pno
    empty = jnp.zeros((pno, pno), jnp.bfloat16)
    counts = [side.counts(p) for p in range(len(side.packs))]
    for j in range(0, len(other.packs), 2):
        for copy in copies[j : j + 2]:
            copy.wait()
        pair = jnp.concatenate([other.basis(j), other.basis(j + 1)], axis=1)
        inter = jnp.dot(side.left[...], pair, preferred_element_type=jnp.float32).astype(jnp.bfloat16)
        inter_ref[:, j * pno : (j + 2) * pno] = inter
        diagonal = jnp.concatenate(
            [
                jnp.concatenate([other.amps(j), empty], axis=1),
                jnp.concatenate([empty, other.amps(j + 1)], axis=1),
            ],
            axis=0,
        )
        proj = jnp.dot(inter, diagonal, preferred_element_type=jnp.float32)
        for p, count in enumerate(counts):
            for c in range(2):
                block = proj[p * pno : (p + 1) * pno, c * pno : (c + 1) * pno]
                proj_ref[p * pno : (p + 1) * pno, (j + c) * pno : (j + c + 1) * pno] = (
                    block * count[0:1, lanes[j + c] : lanes[j + c] + 1]
                ).astype(jnp.bfloat16)


def fetch(sources, held_ref, sems):
    copies = [pltpu.make_async_copy(source, held_ref.at[k], sems.at[k]) for k, source in enumerate(sources)]
    for copy in copies:
        copy.start()
    return copies


def own_kernel(left_ref, low_ref, high_ref, out_ref, inter_ref, proj_ref):
    pairs, pno, _ = out_ref.shape
    packs = [ref.at[k] for ref in (low_ref, high_ref) for k in range(pairs // 2)]
    own = Side(left_ref, packs, left_ref.shape[1], pno)
    project(own, own, range(pairs), inter_ref, proj_ref)
    for p in range(pairs):
        out_ref[p] = one_sum(proj_ref, inter_ref, p, pno)


def coupled_kernel(lanes, left_ref, low_ref, high_ref, acc_ref, one_ref, two_ref, out_ref, held_ref, inter_ref, proj_ref, sems):
    pairs, pno, _ = out_ref.shape
    half, orbs = pairs // 2, left_ref.shape[1]
    copies = fetch([ref.at[k] for ref in (one_ref, two_ref) for k in range(half)], held_ref, sems)
    own = Side(left_ref, [ref.at[k] for ref in (low_ref, high_ref) for k in range(half)], orbs, pno)
    other = Side(None, [held_ref.at[k] for k in range(pairs)], orbs, pno)
    project(own, other, lanes, inter_ref, proj_ref, copies)
    for p in range(pairs):
        out_ref[p] = acc_ref[p] + one_sum(proj_ref, inter_ref, p, pno)


def one_sum(proj_ref, inter_ref, p, pno):
    at = slice(p * pno, (p + 1) * pno)
    return lax.dot_general(
        proj_ref[at, :], inter_ref[at, :], (((1,), (1,)), ((), ())), preferred_element_type=jnp.float32
    )


def both_sums(held_ref, turned_ref, copies, one_lanes, two_lanes, products, orbs):
    half, pno = held_ref.shape[0] // 2, held_ref.shape[2]
    for k, copy in enumerate(copies):
        copy.wait()
        turned_ref[k * pno : (k + 1) * pno, :] = held_ref[k, :orbs, :].T
    sides = [
        Side(
            turned_ref.at[first * pno : (first + half) * pno, :],
            [held_ref.at[first + k] for k in range(half)],
            orbs,
            pno,
        )
        for first in (0, half)
    ]
    project(sides[0], sides[1], two_lanes, products[0], products[1])
    project(sides[1], sides[0], one_lanes, products[2], products[3])

    def total(proj, inter):
        def of(k):
            at = slice(k * pno, (k + 1) * pno)
            return jnp.dot(proj[at, :], inter[:, at], preferred_element_type=jnp.float32)

        return of

    return total(products[1], products[2]), total(products[3], products[0])


def first_across_kernel(orbs, one_ref, two_ref, out_one, out_two, held_ref, turned_ref, *refs):
    *products, sems = refs
    half = out_one.shape[0]
    block = 3 * 2 * half
    copies = fetch([ref.at[k] for ref in (one_ref, two_ref) for k in range(half)], held_ref, sems)
    low, high = range(block, block + half), range(block + half, block + 2 * half)
    one, two = both_sums(held_ref, turned_ref, copies, low, high, products, orbs)
    for k in range(half):
        out_one[k] = one(k)
        out_two[k] = two(k)


def second_across_kernel(orbs, upper_ref, low1, low2, *refs):
    x_low, x_high, y_low, y_high, back_x, back_y, held_ref, turned_ref, *refs = refs
    *products, sems = refs
    half, pno = low1.shape[0], low1.shape[1]
    block = 3 * 2 * half
    none = jnp.zeros((pno, pno), jnp.bfloat16)

    @pl.when(upper_ref[0] == 0)
    def _():
        copies = fetch([ref.at[k] for ref in (x_low, y_low) for k in range(half)], held_ref, sems)
        low = range(block, block + half)
        one, two = both_sums(held_ref, turned_ref, copies, low, low, products, orbs)
        for k in range(half):
            back_x[k] = (low1[k] + one(k)).astype(jnp.bfloat16)
            back_x[half + k] = none
            back_y[k] = two(k).astype(jnp.bfloat16)
            back_y[half + k] = low2[k].astype(jnp.bfloat16)

    @pl.when(upper_ref[0] == 1)
    def _():
        copies = fetch([ref.at[k] for ref in (x_high, y_high) for k in range(half)], held_ref, sems)
        high = range(block + half, block + 2 * half)
        one, two = both_sums(held_ref, turned_ref, copies, high, high, products, orbs)
        for k in range(half):
            back_x[k] = low1[k].astype(jnp.bfloat16)
            back_x[half + k] = one(k).astype(jnp.bfloat16)
            back_y[k] = none
            back_y[half + k] = (low2[k] + two(k)).astype(jnp.bfloat16)


def own_coupled(own_t, own, flops):
    rows, pairs = own_t.shape[0], own[0].shape[0] * 2
    shape = jax.ShapeDtypeStruct((pairs, rows // pairs, rows // pairs), jnp.float32)
    scratch = [pltpu.VMEM((rows, rows), jnp.bfloat16)] * 2
    return call_kernel(own_kernel, shape, scratch, "own_coupled", (), (own_t, *own), flops)


def add_coupled(lanes, own_t, own, acc, received, flops):
    rows, pairs = own_t.shape[0], acc.shape[0]
    scratch = [
        pltpu.VMEM((pairs,) + received[0].shape[1:], jnp.bfloat16),
        *[pltpu.VMEM((rows, rows), jnp.bfloat16)] * 2,
        pltpu.SemaphoreType.DMA((pairs,)),
    ]
    shape = jax.ShapeDtypeStruct(acc.shape, jnp.float32)
    body = functools.partial(coupled_kernel, lanes)
    return call_kernel(body, shape, scratch, "coupled", (), (own_t, *own, acc), flops, hbm_args=received)


def across(body, name, scalars, partial, received, shapes, orbs, flops):
    half, rows, pno = received[0].shape
    wide = half * pno
    scratch = [
        pltpu.VMEM((2 * half, rows, pno), jnp.bfloat16),
        pltpu.VMEM((2 * wide, orbs), jnp.bfloat16),
        *[pltpu.VMEM((wide, wide), jnp.bfloat16)] * 4,
        pltpu.SemaphoreType.DMA((2 * half,)),
    ]
    return call_kernel(
        functools.partial(body, orbs), shapes, scratch, name, scalars, partial, flops, hbm_args=received
    )


def half_transforms(uses_ref, slab_refs, own_ref, half_ref, base):
    pno = half_ref.shape[2]
    last = own_ref.shape[0] // pno - 1

    def rows(side):
        return own_ref[pl.ds(pl.multiple_of(jnp.minimum(side // 2, last) * pno, pno), pno), :]

    def both_sides(slab, k):
        one, two = uses_ref[k, 0], uses_ref[k, 1]
        bases = jnp.concatenate([rows(one), rows(two)], axis=0)
        both = lax.dot_general(slab, bases, (((1,), (1,)), ((), ())), preferred_element_type=jnp.float32)
        both = both.astype(jnp.bfloat16)
        half_ref[one] = both[:, :pno]
        half_ref[two] = both[:, pno:]

    for slab_ref in slab_refs:
        if slab_ref.shape[0] > 4:

            def step(k, carry, slab_ref=slab_ref, base=base):
                both_sides(slab_ref[k], base + k)
                return carry

            lax.fori_loop(0, slab_ref.shape[0], step, 0)
        else:
            for k in range(slab_ref.shape[0]):
                both_sides(slab_ref[k], base + k)
        base += slab_ref.shape[0]


def halves_kernel(base, uses_ref, *refs):
    *slab_refs, own_ref, half_ref = refs
    half_transforms(uses_ref, slab_refs, own_ref, half_ref, base)


def more_halves_kernel(base, uses_ref, *refs):
    *slab_refs, own_ref, _, half_ref = refs
    half_transforms(uses_ref, slab_refs, own_ref, half_ref, base)


def exchange_kernel(scale, base, uses_ref, turn_ref, *refs):
    *slab_refs, own_ref, early_ref, acc_ref, back1_ref, back2_ref, out_ref, half_ref = refs
    half_transforms(uses_ref, slab_refs, own_ref, half_ref, base)
    for p in range(out_ref.shape[0]):
        left, right = [
            jnp.where(turn_ref[p, side] < base, early_ref[2 * p + side], half_ref[2 * p + side]) for side in range(2)
        ]
        product = lax.dot_general(left, right, (((0,), (0,)), ((), ())), preferred_element_type=jnp.float32)
        back = back1_ref[p].astype(jnp.float32) + back2_ref[p].astype(jnp.float32)
        out_ref[p] = acc_ref[p] + back + product * scale


def half_products(uses, base, slabs, own_t, pno, done=None):
    sides = own_t.shape[0] // pno * 2
    shape = jax.ShapeDtypeStruct((sides + 1, slabs[0].shape[1], pno), jnp.bfloat16)
    if done is None:
        return call_kernel(functools.partial(halves_kernel, base), shape, [], "halves", (uses,), (*slabs, own_t), 0)
    args = (*slabs, own_t, done)
    return call_kernel(
        functools.partial(more_halves_kernel, base), shape, [], "more_halves", (uses,), args, 0, aliases={len(args): 0}
    )


def add_exchange(uses, turn, base, slabs, own_t, early, sums):
    return call_kernel(
        functools.partial(exchange_kernel, 1.0 / math.sqrt(slabs[0].shape[1]), base),
        jax.ShapeDtypeStruct(sums[0].shape, jnp.float32),
        [pltpu.VMEM(early.shape, jnp.bfloat16)],
        "exchange",
        (uses, turn),
        (*slabs, own_t, early, *sums),
        0,
    )


def slab_uses(slab_owner, pair_orbs, order):
    n_dev = order.shape[0]
    sides = pair_orbs.shape[0] * 2
    table = jnp.arange(n_dev, dtype=jnp.int32)
    position = jnp.sum(jnp.where(pair_orbs.reshape(sides)[:, None] == table, slab_owner, 0), axis=1)
    turn = jnp.sum(jnp.where(position[:, None] == table, order, 0), axis=1).astype(jnp.int32)
    hit = turn[:, None] == table
    side = jnp.arange(sides, dtype=jnp.int32)[:, None]
    last = jnp.max(jnp.where(hit, side, -1), axis=0)
    first = jnp.min(jnp.where(hit, side, sides), axis=0)
    return turn.reshape(-1, 2), jnp.stack([first, jnp.where(last < 0, sides, last)], axis=1)


def pack_kernel(base_ref, amp_ref, count_ref, low_ref, high_ref, sems):
    half = low_ref.shape[0]
    copies = []
    for k, out_ref in enumerate((low_ref, high_ref)):
        row = 0
        for part, ref in enumerate((base_ref, amp_ref, count_ref)):
            rows = pl.ds(row, ref.shape[1])
            row += ref.shape[1]
            copies.append(
                pltpu.make_async_copy(ref.at[pl.ds(k * half, half)], out_ref.at[:, rows], sems.at[3 * k + part])
            )
    for copy in copies:
        copy.start()
    for copy in copies:
        copy.wait()


def pack(bases, amps, counts):
    pairs, _, pno = bases.shape
    counts = jnp.pad(counts.astype(jnp.bfloat16)[:, None, :], ((0, 0), (0, 15), (0, pno - counts.shape[1])))
    rows = bases.shape[1] + amps.shape[1] + counts.shape[1]
    shape = jax.ShapeDtypeStruct((pairs // 2, rows, pno), bases.dtype)
    return pl.pallas_call(
        pack_kernel,
        out_shape=(shape, shape),
        in_specs=[HBM_SPEC] * 3,
        out_specs=(VMEM_SPEC, VMEM_SPEC),
        scratch_shapes=[pltpu.SemaphoreType.DMA((6,))],
        compiler_params=pltpu.CompilerParams(vmem_limit_bytes=4 * MARGIN),
        name="pack",
    )(bases, amps, counts)


def after(value, *earlier):
    return lax.optimization_barrier((value,) + earlier)[0]


def slot_counts(coupled, coupled_len, cand_count, scale):
    live = jnp.arange(coupled.shape[1])[None, :] < coupled_len[:, None]
    hits = (coupled[:, :, None] == jnp.arange(cand_count, dtype=jnp.int32)[None, None, :]) & live[:, :, None]
    return jnp.sum(hits.astype(jnp.float32), axis=1) * scale


def on_device(integral_slabs, slab_owner, pair_orbs, domain_bases, amplitudes, coupled, coupled_len):
    n_grp, n_dev = lax.axis_size("grp"), lax.axis_size("dev")
    pairs, orbs, pno = domain_bases.shape
    group, me = lax.axis_index("grp"), lax.axis_index("dev")
    chips = n_dev // 2
    chip, core = me // 2, me % 2

    half = pairs // 2

    def along_x(value):
        return lax.ppermute(value, "grp", [(g, g ^ 1) for g in range(n_grp)])

    def along_y(value):
        return lax.ppermute(value, "grp", [(g, g ^ 2) for g in range(n_grp)])

    def next_chip(value):
        return lax.ppermute(value, "dev", [(d, (d + 2) % n_dev) for d in range(n_dev)])

    def other_core(value):
        return lax.ppermute(value, "dev", [(d, d ^ 1) for d in range(n_dev)])

    counts = slot_counts((coupled // pairs ^ group) * pairs + coupled % pairs, coupled_len, n_grp * pairs, orbs / pno)
    own = pack(domain_bases, amplitudes, counts)
    own_lo, own_hi = own
    own_t = jnp.swapaxes(domain_bases, 1, 2).reshape(pairs * pno, orbs)
    upper = jnp.where(group >= 2, 1, 0).astype(jnp.int32).reshape(1)

    x_lo, y_hi = along_x(own_lo), along_y(own_hi)
    x_hi, y_lo = along_x(after(own_hi, own_lo)), along_y(after(own_lo, own_hi))

    slab = integral_slabs[0]
    around = chips <= 4
    position = jnp.arange(n_dev, dtype=jnp.int32)
    order, ahead = position, n_dev // 2
    acc = own_coupled(own_t, own, OWN_COST)
    if around:
        order = 2 * ((chip - position // 2) % chips) + jnp.where(position % 2 == core, 0, 1)
        ahead = 6
        round1 = next_chip(slab)
        round2 = next_chip(after(round1, acc))
        swap0, swap1 = other_core(after(slab, x_lo, y_hi)), other_core(after(round1, x_lo, y_hi))
    turns, uses = slab_uses(slab_owner, pair_orbs, order)

    lanes = [*range(pairs, pairs + half), *range(2 * pairs + half, 3 * pairs)]
    acc = add_coupled(lanes, own_t, own, acc, (x_lo, y_hi), DECLARED)
    part = jax.ShapeDtypeStruct((half, pno, pno), jnp.float32)
    first = across(
        first_across_kernel, "first_across", (), (), (after(x_lo, acc), after(y_hi, acc)), (part, part), orbs, FIRST_COST
    )
    if around:
        slabs = [slab[None], swap0[None], round1[None], swap1[None]]
        halves = half_products(uses, 0, slabs, after(own_t, *first), pno)
        round2 = after(round2, halves)
        round3, swap2 = next_chip(round2), other_core(round2)
        halves = half_products(uses, 4, [round2[None], swap2[None]], own_t, pno, halves)
    else:
        gathered = lax.all_gather(slab, "dev", axis=0, tiled=False)
        halves = half_products(uses, 0, [gathered[:ahead]], own_t, pno)
        rest = [gathered[ahead:]]
    whole = jax.ShapeDtypeStruct((pairs, pno, pno), jnp.bfloat16)
    back_x, back_y = across(
        second_across_kernel,
        "second_across",
        (upper,),
        (after(first[0], halves), first[1]),
        (x_lo, x_hi, y_lo, y_hi),
        (whole, whole),
        orbs,
        SECOND_COST,
    )
    back = (along_x(back_x), along_y(back_y))
    lanes = [*range(pairs + half, 2 * pairs), *range(2 * pairs, 2 * pairs + half)]
    acc = add_coupled(lanes, own_t, own, after(acc, back_x), (x_hi, y_lo), LAST_COST)
    if around:
        round3 = after(round3, acc, *back)
        rest = [round3[None], other_core(round3)[None]]
    return add_exchange(uses, turns, ahead, rest, own_t, halves, (acc, *back))


def solution(mesh):
    in_specs = (
        P("dev", None, None),
        P(),
        P(("grp", "dev"), None),
        P(("grp", "dev"), None, None),
        P(("grp", "dev"), None, None),
        P(("grp", "dev"), None),
        P(("grp", "dev")),
    )
    out_specs = P(("grp", "dev"), None, None)
    return jax.shard_map(
        on_device, mesh=mesh, in_specs=in_specs, out_specs=out_specs, check_vma=False
    )
```

```python
import functools
import math

import jax
import jax.numpy as jnp
from jax import lax
from jax.experimental import pallas as pl
from jax.experimental.pallas import tpu as pltpu
from jax.sharding import PartitionSpec as P

MARGIN = 2 * 1024 * 1024
PACK_LIMIT = 56 * 1024 * 1024
DECLARED = 20_000_000_000
OWN_COST, FIRST_COST, SECOND_COST, LAST_COST = 0, 0, 0, DECLARED
SMEM_SPEC = pl.BlockSpec(memory_space=pltpu.SMEM)
VMEM_SPEC = pl.BlockSpec(memory_space=pltpu.VMEM)
HBM_SPEC = pl.BlockSpec(memory_space=pltpu.HBM)


def call_kernel(body, out_shape, scratch, name, smem_args, vmem_args, flops, hbm_args=(), aliases={}):
    outs = out_shape if isinstance(out_shape, tuple) else (out_shape,)
    held = [a for a in (*vmem_args, *scratch, *outs) if a.dtype in (jnp.float32, jnp.bfloat16)]
    return pl.pallas_call(
        body,
        out_shape=out_shape,
        in_specs=[SMEM_SPEC] * len(smem_args) + [VMEM_SPEC] * len(vmem_args) + [HBM_SPEC] * len(hbm_args),
        out_specs=(VMEM_SPEC,) * len(outs) if isinstance(out_shape, tuple) else VMEM_SPEC,
        scratch_shapes=scratch,
        input_output_aliases=aliases,
        compiler_params=pltpu.CompilerParams(
            vmem_limit_bytes=sum(math.prod(a.shape) * a.dtype.itemsize for a in held) + MARGIN
        ),
        cost_estimate=pl.CostEstimate(flops=flops, bytes_accessed=0, transcendentals=0),
        name=name,
    )(*smem_args, *vmem_args, *hbm_args)


class Side:
    def __init__(self, left, packs, orbs, pno):
        self.left, self.packs, self.orbs, self.pno = left, packs, orbs, pno

    def basis(self, k):
        return self.packs[k][: self.orbs, :]

    def amps(self, k):
        return self.packs[k][self.orbs : self.orbs + self.pno, :]

    def counts(self, lanes):
        rows = [pack[self.orbs + self.pno :, :].astype(jnp.float32) for pack in self.packs]
        return lambda p, c: rows[p][0:1, lanes[c] : lanes[c] + 1]


def project(side, other, count, inter_ref, proj_ref, copies=()):
    pno = side.pno
    empty = jnp.zeros((pno, pno), jnp.bfloat16)
    for j in range(0, len(other.packs), 2):
        for copy in copies[j : j + 2]:
            copy.wait()
        pair = jnp.concatenate([other.basis(j), other.basis(j + 1)], axis=1)
        inter = jnp.dot(side.left[...], pair, preferred_element_type=jnp.float32).astype(jnp.bfloat16)
        inter_ref[:, j * pno : (j + 2) * pno] = inter
        diagonal = jnp.concatenate(
            [
                jnp.concatenate([other.amps(j), empty], axis=1),
                jnp.concatenate([empty, other.amps(j + 1)], axis=1),
            ],
            axis=0,
        )
        proj = jnp.dot(inter, diagonal, preferred_element_type=jnp.float32)
        for p in range(side.left.shape[0] // pno):
            for c in range(2):
                block = proj[p * pno : (p + 1) * pno, c * pno : (c + 1) * pno]
                proj_ref[p * pno : (p + 1) * pno, (j + c) * pno : (j + c + 1) * pno] = (
                    block * count(p, j + c)
                ).astype(jnp.bfloat16)


def fetch(sources, held_ref, sems):
    copies = [pltpu.make_async_copy(source, held_ref.at[k], sems.at[k]) for k, source in enumerate(sources)]
    for copy in copies:
        copy.start()
    return copies


def coupled_kernel(lanes, begun, weight_ref, left_ref, *refs):
    *acc_ref, one_ref, two_ref, out_ref, held_ref, inter_ref, proj_ref, sems = refs
    pairs, pno, _ = out_ref.shape
    half, orbs = pairs // 2, left_ref.shape[1]
    copies = fetch([ref.at[k] for ref in (one_ref, two_ref) for k in range(half)], held_ref, sems)
    own = Side(left_ref, (), orbs, pno)
    other = Side(None, [held_ref.at[k] for k in range(pairs)], orbs, pno)
    project(own, other, lambda p, c: weight_ref[p, lanes[c]], inter_ref, proj_ref, copies)
    for p in range(pairs):
        total = one_sum(proj_ref, inter_ref, p, pno)
        out_ref[p] = acc_ref[0][p] + total if begun else total


def one_sum(proj_ref, inter_ref, p, pno):
    at = slice(p * pno, (p + 1) * pno)
    return lax.dot_general(
        proj_ref[at, :], inter_ref[at, :], (((1,), (1,)), ((), ())), preferred_element_type=jnp.float32
    )


def both_sums(held_ref, turned_ref, copies, one_lanes, two_lanes, products, orbs):
    half, pno = held_ref.shape[0] // 2, held_ref.shape[2]
    for k, copy in enumerate(copies):
        copy.wait()
        turned_ref[k * pno : (k + 1) * pno, :] = held_ref[k, :orbs, :].T
    sides = [
        Side(
            turned_ref.at[first * pno : (first + half) * pno, :],
            [held_ref.at[first + k] for k in range(half)],
            orbs,
            pno,
        )
        for first in (0, half)
    ]
    project(sides[0], sides[1], sides[0].counts(two_lanes), products[0], products[1])
    project(sides[1], sides[0], sides[1].counts(one_lanes), products[2], products[3])

    def total(proj, inter):
        def of(k):
            at = slice(k * pno, (k + 1) * pno)
            return jnp.dot(proj[at, :], inter[:, at], preferred_element_type=jnp.float32)

        return of

    return total(products[1], products[2]), total(products[3], products[0])


def first_across_kernel(orbs, one_ref, two_ref, out_one, out_two, held_ref, turned_ref, *refs):
    *products, sems = refs
    half = out_one.shape[0]
    block = 3 * 2 * half
    copies = fetch([ref.at[k] for ref in (one_ref, two_ref) for k in range(half)], held_ref, sems)
    low, high = range(block, block + half), range(block + half, block + 2 * half)
    one, two = both_sums(held_ref, turned_ref, copies, low, high, products, orbs)
    for k in range(half):
        out_one[k] = one(k)
        out_two[k] = two(k)


def second_across_kernel(orbs, upper_ref, low1, low2, *refs):
    x_low, x_high, y_low, y_high, back_x, back_y, held_ref, turned_ref, *refs = refs
    *products, sems = refs
    half, pno = low1.shape[0], low1.shape[1]
    block = 3 * 2 * half
    none = jnp.zeros((pno, pno), jnp.bfloat16)

    @pl.when(upper_ref[0] == 0)
    def _():
        copies = fetch([ref.at[k] for ref in (x_low, y_low) for k in range(half)], held_ref, sems)
        low = range(block, block + half)
        one, two = both_sums(held_ref, turned_ref, copies, low, low, products, orbs)
        for k in range(half):
            back_x[k] = (low1[k] + one(k)).astype(jnp.bfloat16)
            back_x[half + k] = none
            back_y[k] = two(k).astype(jnp.bfloat16)
            back_y[half + k] = low2[k].astype(jnp.bfloat16)

    @pl.when(upper_ref[0] == 1)
    def _():
        copies = fetch([ref.at[k] for ref in (x_high, y_high) for k in range(half)], held_ref, sems)
        high = range(block + half, block + 2 * half)
        one, two = both_sums(held_ref, turned_ref, copies, high, high, products, orbs)
        for k in range(half):
            back_x[k] = low1[k].astype(jnp.bfloat16)
            back_x[half + k] = one(k).astype(jnp.bfloat16)
            back_y[k] = none
            back_y[half + k] = (low2[k] + two(k)).astype(jnp.bfloat16)


def add_coupled(lanes, weights, own_t, acc, received, flops):
    half, pack_rows, pno = received[0].shape
    rows, pairs = own_t.shape[0], 2 * half
    scratch = [
        pltpu.VMEM((pairs, pack_rows, pno), jnp.bfloat16),
        *[pltpu.VMEM((rows, rows), jnp.bfloat16)] * 2,
        pltpu.SemaphoreType.DMA((pairs,)),
    ]
    shape = jax.ShapeDtypeStruct((pairs, pno, pno), jnp.float32)
    body = functools.partial(coupled_kernel, lanes, acc is not None)
    vmem_args = (own_t,) if acc is None else (own_t, acc)
    return call_kernel(body, shape, scratch, "coupled", (weights,), vmem_args, flops, hbm_args=received)


def across(body, name, scalars, partial, received, shapes, orbs, flops):
    half, rows, pno = received[0].shape
    wide = half * pno
    scratch = [
        pltpu.VMEM((2 * half, rows, pno), jnp.bfloat16),
        pltpu.VMEM((2 * wide, orbs), jnp.bfloat16),
        *[pltpu.VMEM((wide, wide), jnp.bfloat16)] * 4,
        pltpu.SemaphoreType.DMA((2 * half,)),
    ]
    return call_kernel(
        functools.partial(body, orbs), shapes, scratch, name, scalars, partial, flops, hbm_args=received
    )


def half_transforms(uses_ref, slab_refs, own_ref, store, base, pno):
    last = own_ref.shape[0] // pno - 1

    def rows(side):
        return own_ref[pl.ds(pl.multiple_of(jnp.minimum(side // 2, last) * pno, pno), pno), :]

    def both_sides(slab, k):
        one, two = uses_ref[k, 0], uses_ref[k, 1]
        bases = jnp.concatenate([rows(one), rows(two)], axis=0)
        both = lax.dot_general(slab, bases, (((1,), (1,)), ((), ())), preferred_element_type=jnp.float32)
        both = both.astype(jnp.bfloat16)
        store(k, 0, one, both[:, :pno])
        store(k, 1, two, both[:, pno:])

    for slab_ref in slab_refs:
        if slab_ref.shape[0] > 4:

            def step(k, carry, slab_ref=slab_ref, base=base):
                both_sides(slab_ref[k], base + k)
                return carry

            lax.fori_loop(0, slab_ref.shape[0], step, 0)
        else:
            for k in range(slab_ref.shape[0]):
                both_sides(slab_ref[k], base + k)
        base += slab_ref.shape[0]


def halves_kernel(base, uses_ref, *refs):
    *slab_refs, own_ref, half_ref = refs

    def store(k, use, side, half):
        half_ref[side] = half

    half_transforms(uses_ref, slab_refs, own_ref, store, base, half_ref.shape[2])


def more_halves_kernel(base, uses_ref, *refs):
    *slab_refs, own_ref, _, half_ref = refs
    halves_kernel(base, uses_ref, *slab_refs, own_ref, half_ref)


def exchange_kernel(scale, base, uses_ref, turn_ref, *refs):
    *slab_refs, own_ref, early_ref, acc_ref, back1_ref, back2_ref, out_ref, late_ref = refs

    def store(k, use, side, half):
        late_ref[2 * (k - base) + use] = half

    def half(p, side):
        k = turn_ref[p, side]
        late = jnp.where(uses_ref[k, 0] == 2 * p + side, 0, 1) + 2 * jnp.maximum(k - base, 0)
        return jnp.where(k < base, early_ref[2 * p + side], late_ref[late])

    half_transforms(uses_ref, slab_refs, own_ref, store, base, out_ref.shape[1])
    for p in range(out_ref.shape[0]):
        product = lax.dot_general(half(p, 0), half(p, 1), (((0,), (0,)), ((), ())), preferred_element_type=jnp.float32)
        back = back1_ref[p].astype(jnp.float32) + back2_ref[p].astype(jnp.float32)
        out_ref[p] = acc_ref[p] + back + product * scale


def half_products(uses, base, slabs, own_t, pno, done=None):
    sides = own_t.shape[0] // pno * 2
    shape = jax.ShapeDtypeStruct((sides + 1, slabs[0].shape[1], pno), jnp.bfloat16)
    if done is None:
        return call_kernel(functools.partial(halves_kernel, base), shape, [], "halves", (uses,), (*slabs, own_t), 0)
    args = (*slabs, own_t, done)
    return call_kernel(
        functools.partial(more_halves_kernel, base), shape, [], "more_halves", (uses,), args, 0, aliases={len(args): 0}
    )


def add_exchange(uses, turn, base, slabs, own_t, early, sums):
    return call_kernel(
        functools.partial(exchange_kernel, 1.0 / math.sqrt(slabs[0].shape[1]), base),
        jax.ShapeDtypeStruct(sums[0].shape, jnp.float32),
        [pltpu.VMEM((2 * sum(slab.shape[0] for slab in slabs),) + early.shape[1:], jnp.bfloat16)],
        "exchange",
        (uses, turn),
        (*slabs, own_t, early, *sums),
        0,
    )


def slab_uses(slab_owner, pair_orbs, order):
    n_dev = order.shape[0]
    sides = pair_orbs.shape[0] * 2
    table = jnp.arange(n_dev, dtype=jnp.int32)
    position = jnp.sum(jnp.where(pair_orbs.reshape(sides)[:, None] == table, slab_owner, 0), axis=1)
    turn = jnp.sum(jnp.where(position[:, None] == table, order, 0), axis=1).astype(jnp.int32)
    hit = turn[:, None] == table
    side = jnp.arange(sides, dtype=jnp.int32)[:, None]
    last = jnp.max(jnp.where(hit, side, -1), axis=0)
    first = jnp.min(jnp.where(hit, side, sides), axis=0)
    return turn.reshape(-1, 2), jnp.stack([first, jnp.where(last < 0, sides, last)], axis=1)


def pack_kernel(scale, group_ref, coupled_ref, length_ref, base_ref, amp_ref, *refs):
    low_ref, high_ref, weight_ref, count_ref, sems = refs
    pairs, orbs, pno = base_ref.shape
    half = pairs // 2
    copies = []

    def copy(ref, k, row, sem):
        rows = pl.ds(row, ref.shape[1])
        copies.append(
            pltpu.make_async_copy(ref.at[pl.ds(k * half, half)], (low_ref, high_ref)[k].at[:, rows], sems.at[sem])
        )
        copies[-1].start()

    for k in range(2):
        copy(base_ref, k, 0, 3 * k)
        copy(amp_ref, k, orbs, 3 * k + 1)
    lane = lax.broadcasted_iota(jnp.int32, (1, pno), 1)
    for p in range(pairs):
        counts = jnp.zeros((1, pno), jnp.float32)
        for s in range(coupled_ref.shape[1]):
            named = coupled_ref[p, s]
            at = (lax.div(named, pairs) ^ group_ref[0]) * pairs + lax.rem(named, pairs)
            counts += jnp.where(lane == jnp.where(s < length_ref[p], at, -1), scale, 0.0)
        weight_ref[p : p + 1, :] = counts
        count_ref[p] = jnp.broadcast_to(counts, count_ref.shape[1:]).astype(jnp.bfloat16)
    for k in range(2):
        copy(count_ref, k, orbs + amp_ref.shape[1], 3 * k + 2)
    for started in copies:
        started.wait()


def pack(group, coupled, coupled_len, bases, amps, scale):
    pairs, orbs, pno = bases.shape
    packed = jax.ShapeDtypeStruct((pairs // 2, orbs + amps.shape[1] + 16, pno), bases.dtype)
    return pl.pallas_call(
        functools.partial(pack_kernel, scale),
        out_shape=(packed, packed, jax.ShapeDtypeStruct((pairs, pno), jnp.float32)),
        in_specs=[SMEM_SPEC] * 3 + [HBM_SPEC] * 2,
        out_specs=(HBM_SPEC, HBM_SPEC, VMEM_SPEC),
        scratch_shapes=[pltpu.VMEM((pairs, 16, pno), jnp.bfloat16), pltpu.SemaphoreType.DMA((6,))],
        compiler_params=pltpu.CompilerParams(vmem_limit_bytes=PACK_LIMIT),
        name="pack",
    )(group, coupled, coupled_len, bases, amps)


def after(value, *earlier):
    return lax.optimization_barrier((value,) + earlier)[0]


def on_device(integral_slabs, slab_owner, pair_orbs, domain_bases, amplitudes, coupled, coupled_len):
    n_grp, n_dev = lax.axis_size("grp"), lax.axis_size("dev")
    pairs, orbs, pno = domain_bases.shape
    group, me = lax.axis_index("grp"), lax.axis_index("dev")
    chips = n_dev // 2
    chip, core = me // 2, me % 2

    half = pairs // 2

    def along_x(value):
        return lax.ppermute(value, "grp", [(g, g ^ 1) for g in range(n_grp)])

    def along_y(value):
        return lax.ppermute(value, "grp", [(g, g ^ 2) for g in range(n_grp)])

    def next_chip(value):
        return lax.ppermute(value, "dev", [(d, (d + 2) % n_dev) for d in range(n_dev)])

    def other_core(value):
        return lax.ppermute(value, "dev", [(d, d ^ 1) for d in range(n_dev)])

    own_lo, own_hi, weights = pack(
        group.astype(jnp.int32).reshape(1), coupled, coupled_len, domain_bases, amplitudes, orbs / pno
    )
    own_t = jnp.swapaxes(domain_bases, 1, 2).reshape(pairs * pno, orbs)
    upper = jnp.where(group >= 2, 1, 0).astype(jnp.int32).reshape(1)

    x_lo, y_hi = along_x(own_lo), along_y(own_hi)
    x_hi, y_lo = along_x(after(own_hi, own_lo)), along_y(after(own_lo, own_hi))

    slab = integral_slabs[0]
    around = chips <= 4
    position = jnp.arange(n_dev, dtype=jnp.int32)
    order, ahead = position, n_dev // 2
    acc = add_coupled(list(range(pairs)), weights, own_t, None, (own_lo, own_hi), OWN_COST)
    if around:
        order = 2 * ((chip - position // 2) % chips) + jnp.where(position % 2 == core, 0, 1)
        ahead = 6
        round1 = next_chip(slab)
        round2 = next_chip(after(round1, acc))
        swap0, swap1 = other_core(after(slab, x_lo, y_hi)), other_core(after(round1, x_lo, y_hi))
    turns, uses = slab_uses(slab_owner, pair_orbs, order)

    lanes = [*range(pairs, pairs + half), *range(2 * pairs + half, 3 * pairs)]
    acc = add_coupled(lanes, weights, own_t, acc, (x_lo, y_hi), DECLARED)
    part = jax.ShapeDtypeStruct((half, pno, pno), jnp.float32)
    first = across(
        first_across_kernel, "first_across", (), (), (after(x_lo, acc), after(y_hi, acc)), (part, part), orbs, FIRST_COST
    )
    if around:
        slabs = [slab[None], swap0[None], round1[None], swap1[None]]
        halves = half_products(uses, 0, slabs, after(own_t, *first), pno)
        round2 = after(round2, halves)
        round3, swap2 = next_chip(round2), other_core(round2)
        halves = half_products(uses, 4, [round2[None], swap2[None]], own_t, pno, halves)
    else:
        gathered = lax.all_gather(slab, "dev", axis=0, tiled=False)
        halves = half_products(uses, 0, [gathered[:ahead]], own_t, pno)
        rest = [gathered[ahead:]]
    whole = jax.ShapeDtypeStruct((pairs, pno, pno), jnp.bfloat16)
    back_x, back_y = across(
        second_across_kernel,
        "second_across",
        (upper,),
        (after(first[0], halves), first[1]),
        (x_lo, x_hi, y_lo, y_hi),
        (whole, whole),
        orbs,
        SECOND_COST,
    )
    back = (along_x(back_x), along_y(back_y))
    lanes = [*range(pairs + half, 2 * pairs), *range(2 * pairs, 2 * pairs + half)]
    acc = add_coupled(lanes, weights, own_t, after(acc, back_x), (x_hi, y_lo), LAST_COST)
    if around:
        round3 = after(round3, acc, *back)
        rest = [round3[None], other_core(round3)[None]]
    return add_exchange(uses, turns, ahead, rest, own_t, halves, (acc, *back))


def solution(mesh):
    in_specs = (
        P("dev", None, None),
        P(),
        P(("grp", "dev"), None),
        P(("grp", "dev"), None, None),
        P(("grp", "dev"), None, None),
        P(("grp", "dev"), None),
        P(("grp", "dev")),
    )
    out_specs = P(("grp", "dev"), None, None)
    return jax.shard_map(
        on_device, mesh=mesh, in_specs=in_specs, out_specs=out_specs, check_vma=False
    )
```

```python
import functools
import math

import jax
import jax.numpy as jnp
from jax import lax
from jax.experimental import pallas as pl
from jax.experimental.pallas import tpu as pltpu
from jax.sharding import PartitionSpec as P

MARGIN = 0
PACK_LIMIT = 56 * 1024 * 1024
DECLARED = 20_000_000_000
OWN_COST, FIRST_COST, SECOND_COST, LAST_COST = 0, 0, 0, DECLARED
SMEM_SPEC = pl.BlockSpec(memory_space=pltpu.SMEM)
VMEM_SPEC = pl.BlockSpec(memory_space=pltpu.VMEM)
HBM_SPEC = pl.BlockSpec(memory_space=pltpu.HBM)


def call_kernel(body, out_shape, scratch, name, smem_args, vmem_args, flops, hbm_args=(), aliases={}):
    outs = out_shape if isinstance(out_shape, tuple) else (out_shape,)
    held = [a for a in (*vmem_args, *scratch, *outs) if a.dtype in (jnp.float32, jnp.bfloat16)]
    return pl.pallas_call(
        body,
        out_shape=out_shape,
        in_specs=[SMEM_SPEC] * len(smem_args) + [VMEM_SPEC] * len(vmem_args) + [HBM_SPEC] * len(hbm_args),
        out_specs=(VMEM_SPEC,) * len(outs) if isinstance(out_shape, tuple) else VMEM_SPEC,
        scratch_shapes=scratch,
        input_output_aliases=aliases,
        compiler_params=pltpu.CompilerParams(
            vmem_limit_bytes=sum(math.prod(a.shape) * a.dtype.itemsize for a in held) + MARGIN
        ),
        cost_estimate=pl.CostEstimate(flops=flops, bytes_accessed=0, transcendentals=0),
        name=name,
    )(*smem_args, *vmem_args, *hbm_args)


class Side:
    def __init__(self, left, packs, orbs, pno):
        self.left, self.packs, self.orbs, self.pno = left, packs, orbs, pno

    def basis(self, k):
        return self.packs[k][: self.orbs, :]

    def amps(self, k):
        return self.packs[k][self.orbs : self.orbs + self.pno, :]

    def counts(self, lanes):
        rows = [pack[self.orbs + self.pno :, :].astype(jnp.float32) for pack in self.packs]
        return lambda p, c: rows[p][0:1, lanes[c] : lanes[c] + 1]


def project(side, other, count, inter_ref, proj_ref, copies=()):
    pno = side.pno
    empty = jnp.zeros((pno, pno), jnp.bfloat16)
    for j in range(0, len(other.packs), 2):
        for copy in copies[j : j + 2]:
            copy.wait()
        pair = jnp.concatenate([other.basis(j), other.basis(j + 1)], axis=1)
        inter = jnp.dot(side.left[...], pair, preferred_element_type=jnp.float32).astype(jnp.bfloat16)
        inter_ref[:, j * pno : (j + 2) * pno] = inter
        diagonal = jnp.concatenate(
            [
                jnp.concatenate([other.amps(j), empty], axis=1),
                jnp.concatenate([empty, other.amps(j + 1)], axis=1),
            ],
            axis=0,
        )
        proj = jnp.dot(inter, diagonal, preferred_element_type=jnp.float32)
        for p in range(side.left.shape[0] // pno):
            for c in range(2):
                block = proj[p * pno : (p + 1) * pno, c * pno : (c + 1) * pno]
                proj_ref[p * pno : (p + 1) * pno, (j + c) * pno : (j + c + 1) * pno] = (
                    block * count(p, j + c)
                ).astype(jnp.bfloat16)


def coupled_kernel(lanes, begun, weight_ref, left_ref, *refs):
    *acc_ref, one_ref, two_ref, out_ref, inter_ref, proj_ref = refs
    pairs, pno, _ = out_ref.shape
    half, orbs = pairs // 2, left_ref.shape[1]
    own = Side(left_ref, (), orbs, pno)
    other = Side(None, [ref.at[k] for ref in (one_ref, two_ref) for k in range(half)], orbs, pno)
    project(own, other, lambda p, c: weight_ref[p, lanes[c]], inter_ref, proj_ref)
    for p in range(pairs):
        total = one_sum(proj_ref, inter_ref, p, pno)
        out_ref[p] = acc_ref[0][p] + total if begun else total


def one_sum(proj_ref, inter_ref, p, pno):
    at = slice(p * pno, (p + 1) * pno)
    return lax.dot_general(
        proj_ref[at, :], inter_ref[at, :], (((1,), (1,)), ((), ())), preferred_element_type=jnp.float32
    )


def both_sums(one_ref, two_ref, turned_ref, one_lanes, two_lanes, products, orbs):
    half, _, pno = one_ref.shape
    sides = []
    for first, ref in ((0, one_ref), (half, two_ref)):
        for k in range(half):
            turned_ref[(first + k) * pno : (first + k + 1) * pno, :] = ref[k, :orbs, :].T
        left = turned_ref.at[first * pno : (first + half) * pno, :]
        sides.append(Side(left, [ref.at[k] for k in range(half)], orbs, pno))
    project(sides[0], sides[1], sides[0].counts(two_lanes), products[0], products[1])
    project(sides[1], sides[0], sides[1].counts(one_lanes), products[2], products[3])

    def total(proj, inter):
        def of(k):
            at = slice(k * pno, (k + 1) * pno)
            return jnp.dot(proj[at, :], inter[:, at], preferred_element_type=jnp.float32)

        return of

    return total(products[1], products[2]), total(products[3], products[0])


def first_across_kernel(orbs, x_low, y_high, out_one, out_two, turned_ref, *products):
    half = out_one.shape[0]
    block = 3 * 2 * half
    low, high = range(block, block + half), range(block + half, block + 2 * half)
    one, two = both_sums(x_low, y_high, turned_ref, low, high, products, orbs)
    for k in range(half):
        out_one[k] = one(k)
        out_two[k] = two(k)


def second_across_kernel(orbs, upper_ref, low1, low2, *refs):
    x_low, x_high, y_low, y_high, back_x, back_y, turned_ref, *products = refs
    half, pno = low1.shape[0], low1.shape[1]
    block = 3 * 2 * half
    none = jnp.zeros((pno, pno), jnp.bfloat16)

    @pl.when(upper_ref[0] == 0)
    def _():
        low = range(block, block + half)
        one, two = both_sums(x_low, y_low, turned_ref, low, low, products, orbs)
        for k in range(half):
            back_x[k] = (low1[k] + one(k)).astype(jnp.bfloat16)
            back_x[half + k] = none
            back_y[k] = two(k).astype(jnp.bfloat16)
            back_y[half + k] = low2[k].astype(jnp.bfloat16)

    @pl.when(upper_ref[0] == 1)
    def _():
        high = range(block + half, block + 2 * half)
        one, two = both_sums(x_high, y_high, turned_ref, high, high, products, orbs)
        for k in range(half):
            back_x[k] = low1[k].astype(jnp.bfloat16)
            back_x[half + k] = one(k).astype(jnp.bfloat16)
            back_y[k] = none
            back_y[half + k] = (low2[k] + two(k)).astype(jnp.bfloat16)


def add_coupled(lanes, weights, own_t, acc, received, flops):
    half, _, pno = received[0].shape
    rows, pairs = own_t.shape[0], 2 * half
    shape = jax.ShapeDtypeStruct((pairs, pno, pno), jnp.float32)
    body = functools.partial(coupled_kernel, lanes, acc is not None)
    vmem_args = (own_t, *received) if acc is None else (own_t, acc, *received)
    return call_kernel(body, shape, [pltpu.VMEM((rows, rows), jnp.bfloat16)] * 2, "coupled", (weights,), vmem_args, flops)


def across(body, name, scalars, vmem_args, half, shapes, orbs, flops):
    wide = half * shapes[0].shape[2]
    scratch = [pltpu.VMEM((2 * wide, orbs), jnp.bfloat16), *[pltpu.VMEM((wide, wide), jnp.bfloat16)] * 4]
    return call_kernel(functools.partial(body, orbs), shapes, scratch, name, scalars, vmem_args, flops)


def half_transforms(uses_ref, slab_refs, own_ref, store, base, pno):
    last = own_ref.shape[0] // pno - 1

    def rows(side):
        return own_ref[pl.ds(pl.multiple_of(jnp.minimum(side // 2, last) * pno, pno), pno), :]

    def both_sides(slab, k):
        one, two = uses_ref[k, 0], uses_ref[k, 1]
        bases = jnp.concatenate([rows(one), rows(two)], axis=0)
        both = lax.dot_general(slab, bases, (((1,), (1,)), ((), ())), preferred_element_type=jnp.float32)
        both = both.astype(jnp.bfloat16)
        store(k, 0, one, both[:, :pno])
        store(k, 1, two, both[:, pno:])

    for slab_ref in slab_refs:
        if slab_ref.shape[0] > 4:

            def step(k, carry, slab_ref=slab_ref, base=base):
                both_sides(slab_ref[k], base + k)
                return carry

            lax.fori_loop(0, slab_ref.shape[0], step, 0)
        else:
            for k in range(slab_ref.shape[0]):
                both_sides(slab_ref[k], base + k)
        base += slab_ref.shape[0]


def halves_kernel(base, uses_ref, *refs):
    *slab_refs, own_ref, half_ref = refs

    def store(k, use, side, half):
        half_ref[side] = half

    half_transforms(uses_ref, slab_refs, own_ref, store, base, half_ref.shape[2])


def more_halves_kernel(base, uses_ref, *refs):
    *slab_refs, own_ref, _, half_ref = refs
    halves_kernel(base, uses_ref, *slab_refs, own_ref, half_ref)


def exchange_kernel(scale, base, uses_ref, turn_ref, *refs):
    *slab_refs, own_ref, early_ref, acc_ref, back1_ref, back2_ref, out_ref, late_ref = refs

    def store(k, use, side, half):
        late_ref[2 * (k - base) + use] = half

    def half(p, side):
        k = turn_ref[p, side]
        late = jnp.where(uses_ref[k, 0] == 2 * p + side, 0, 1) + 2 * jnp.maximum(k - base, 0)
        return jnp.where(k < base, early_ref[2 * p + side], late_ref[late])

    half_transforms(uses_ref, slab_refs, own_ref, store, base, out_ref.shape[1])
    for p in range(out_ref.shape[0]):
        product = lax.dot_general(half(p, 0), half(p, 1), (((0,), (0,)), ((), ())), preferred_element_type=jnp.float32)
        back = back1_ref[p].astype(jnp.float32) + back2_ref[p].astype(jnp.float32)
        out_ref[p] = acc_ref[p] + back + product * scale


def half_products(uses, base, slabs, own_t, pno, done=None):
    sides = own_t.shape[0] // pno * 2
    shape = jax.ShapeDtypeStruct((sides + 1, slabs[0].shape[1], pno), jnp.bfloat16)
    if done is None:
        return call_kernel(functools.partial(halves_kernel, base), shape, [], "halves", (uses,), (*slabs, own_t), 0)
    args = (*slabs, own_t, done)
    return call_kernel(
        functools.partial(more_halves_kernel, base), shape, [], "more_halves", (uses,), args, 0, aliases={len(args): 0}
    )


def add_exchange(uses, turn, base, slabs, own_t, early, sums):
    return call_kernel(
        functools.partial(exchange_kernel, 1.0 / math.sqrt(slabs[0].shape[1]), base),
        jax.ShapeDtypeStruct(sums[0].shape, jnp.float32),
        [pltpu.VMEM((2 * sum(slab.shape[0] for slab in slabs),) + early.shape[1:], jnp.bfloat16)],
        "exchange",
        (uses, turn),
        (*slabs, own_t, early, *sums),
        0,
    )


def slab_uses(slab_owner, pair_orbs, order):
    n_dev = order.shape[0]
    sides = pair_orbs.shape[0] * 2
    table = jnp.arange(n_dev, dtype=jnp.int32)
    position = jnp.sum(jnp.where(pair_orbs.reshape(sides)[:, None] == table, slab_owner, 0), axis=1)
    turn = jnp.sum(jnp.where(position[:, None] == table, order, 0), axis=1).astype(jnp.int32)
    hit = turn[:, None] == table
    side = jnp.arange(sides, dtype=jnp.int32)[:, None]
    last = jnp.max(jnp.where(hit, side, -1), axis=0)
    first = jnp.min(jnp.where(hit, side, sides), axis=0)
    return turn.reshape(-1, 2), jnp.stack([first, jnp.where(last < 0, sides, last)], axis=1)


def pack_kernel(scale, group_ref, coupled_ref, length_ref, base_ref, amp_ref, *refs):
    low_ref, high_ref, weight_ref, held_ref, sems = refs
    pairs, orbs, pno = base_ref.shape
    half = pairs // 2
    copies = []

    def copy(ref, k, row, sem):
        rows = pl.ds(row, ref.shape[1])
        copies.append(pltpu.make_async_copy(ref.at[pl.ds(k * half, half)], held_ref.at[k, :, rows], sems.at[sem]))
        copies[-1].start()

    for k in range(2):
        copy(base_ref, k, 0, 2 * k)
        copy(amp_ref, k, orbs, 2 * k + 1)
    lane = lax.broadcasted_iota(jnp.int32, (1, pno), 1)
    for p in range(pairs):
        counts = jnp.zeros((1, pno), jnp.float32)
        for s in range(coupled_ref.shape[1]):
            named = coupled_ref[p, s]
            at = (lax.div(named, pairs) ^ group_ref[0]) * pairs + lax.rem(named, pairs)
            counts += jnp.where(lane == jnp.where(s < length_ref[p], at, -1), scale, 0.0)
        weight_ref[p : p + 1, :] = counts
        rows = slice(orbs + amp_ref.shape[1], held_ref.shape[2])
        held_ref[p // half, p % half, rows, :] = jnp.broadcast_to(counts, (16, pno)).astype(jnp.bfloat16)
    for started in copies:
        started.wait()
    stores = [
        pltpu.make_async_copy(held_ref.at[k], out_ref, sems.at[4 + k]) for k, out_ref in enumerate((low_ref, high_ref))
    ]
    for store in stores:
        store.start()
    for store in stores:
        store.wait()


def pack(group, coupled, coupled_len, bases, amps, scale):
    pairs, orbs, pno = bases.shape
    packed = jax.ShapeDtypeStruct((pairs // 2, orbs + amps.shape[1] + 16, pno), bases.dtype)
    return pl.pallas_call(
        functools.partial(pack_kernel, scale),
        out_shape=(packed, packed, jax.ShapeDtypeStruct((pairs, pno), jnp.float32)),
        in_specs=[SMEM_SPEC] * 3 + [HBM_SPEC] * 2,
        out_specs=(HBM_SPEC, HBM_SPEC, VMEM_SPEC),
        scratch_shapes=[pltpu.VMEM((2,) + packed.shape, bases.dtype), pltpu.SemaphoreType.DMA((6,))],
        compiler_params=pltpu.CompilerParams(vmem_limit_bytes=PACK_LIMIT),
        name="pack",
    )(group, coupled, coupled_len, bases, amps)


def after(value, *earlier):
    return lax.optimization_barrier((value,) + earlier)[0]


def on_device(integral_slabs, slab_owner, pair_orbs, domain_bases, amplitudes, coupled, coupled_len):
    n_grp, n_dev = lax.axis_size("grp"), lax.axis_size("dev")
    pairs, orbs, pno = domain_bases.shape
    group, me = lax.axis_index("grp"), lax.axis_index("dev")
    chips = n_dev // 2
    chip, core = me // 2, me % 2

    half = pairs // 2

    def along_x(value):
        return lax.ppermute(value, "grp", [(g, g ^ 1) for g in range(n_grp)])

    def along_y(value):
        return lax.ppermute(value, "grp", [(g, g ^ 2) for g in range(n_grp)])

    def next_chip(value):
        return lax.ppermute(value, "dev", [(d, (d + 2) % n_dev) for d in range(n_dev)])

    def other_core(value):
        return lax.ppermute(value, "dev", [(d, d ^ 1) for d in range(n_dev)])

    own_lo, own_hi, weights = pack(
        group.astype(jnp.int32).reshape(1), coupled, coupled_len, domain_bases, amplitudes, orbs / pno
    )
    own_t = jnp.swapaxes(domain_bases, 1, 2).reshape(pairs * pno, orbs)
    upper = jnp.where(group >= 2, 1, 0).astype(jnp.int32).reshape(1)

    x_lo, y_hi = along_x(own_lo), along_y(own_hi)
    x_hi, y_lo = along_x(after(own_hi, own_lo)), along_y(after(own_lo, own_hi))

    slab = integral_slabs[0]
    around = chips <= 4
    position = jnp.arange(n_dev, dtype=jnp.int32)
    order, ahead = position, n_dev // 2
    acc = add_coupled(list(range(pairs)), weights, own_t, None, (own_lo, own_hi), OWN_COST)
    if around:
        order = 2 * ((chip - position // 2) % chips) + jnp.where(position % 2 == core, 0, 1)
        ahead = 6
        round1 = next_chip(slab)
        round2 = next_chip(after(round1, acc))
        swap0, swap1 = other_core(after(slab, x_lo, y_hi)), other_core(after(round1, x_lo, y_hi))
    turns, uses = slab_uses(slab_owner, pair_orbs, order)

    lanes = [*range(pairs, pairs + half), *range(2 * pairs + half, 3 * pairs)]
    acc = add_coupled(lanes, weights, own_t, acc, (x_lo, y_hi), DECLARED)
    part = jax.ShapeDtypeStruct((half, pno, pno), jnp.float32)
    first = across(
        first_across_kernel, "first_across", (), (after(x_lo, acc), after(y_hi, acc)), half, (part, part), orbs, FIRST_COST
    )
    if around:
        slabs = [slab[None], swap0[None], round1[None], swap1[None]]
        halves = half_products(uses, 0, slabs, after(own_t, *first), pno)
        round2 = after(round2, halves)
        round3, swap2 = next_chip(round2), other_core(round2)
        halves = half_products(uses, 4, [round2[None], swap2[None]], own_t, pno, halves)
    else:
        gathered = lax.all_gather(slab, "dev", axis=0, tiled=False)
        halves = half_products(uses, 0, [gathered[:ahead]], own_t, pno)
        rest = [gathered[ahead:]]
    whole = jax.ShapeDtypeStruct((pairs, pno, pno), jnp.bfloat16)
    back_x, back_y = across(
        second_across_kernel,
        "second_across",
        (upper,),
        (after(first[0], halves), first[1], x_lo, x_hi, y_lo, y_hi),
        half,
        (whole, whole),
        orbs,
        SECOND_COST,
    )
    back = (along_x(back_x), along_y(back_y))
    lanes = [*range(pairs + half, 2 * pairs), *range(2 * pairs, 2 * pairs + half)]
    acc = add_coupled(lanes, weights, own_t, after(acc, back_x), (x_hi, y_lo), LAST_COST)
    if around:
        round3 = after(round3, acc, *back)
        rest = [round3[None], other_core(round3)[None]]
    return add_exchange(uses, turns, ahead, rest, own_t, halves, (acc, *back))


def solution(mesh):
    in_specs = (
        P("dev", None, None),
        P(),
        P(("grp", "dev"), None),
        P(("grp", "dev"), None, None),
        P(("grp", "dev"), None, None),
        P(("grp", "dev"), None),
        P(("grp", "dev")),
    )
    out_specs = P(("grp", "dev"), None, None)
    return jax.shard_map(
        on_device, mesh=mesh, in_specs=in_specs, out_specs=out_specs, check_vma=False
    )
```

```python
import functools
import math

import jax
import jax.numpy as jnp
from jax import lax
from jax.experimental import pallas as pl
from jax.experimental.pallas import tpu as pltpu
from jax.sharding import PartitionSpec as P

MARGIN = 0
PACK_LIMIT = 56 * 1024 * 1024
RING_CHIPS = 4
DECLARED = 20_000_000_000
OWN_COST, FIRST_COST, SECOND_COST, LAST_COST = DECLARED, 0, 0, DECLARED
SMEM_SPEC = pl.BlockSpec(memory_space=pltpu.SMEM)
VMEM_SPEC = pl.BlockSpec(memory_space=pltpu.VMEM)
HBM_SPEC = pl.BlockSpec(memory_space=pltpu.HBM)


def call_kernel(body, out_shape, scratch, name, smem_args, vmem_args, flops, hbm_args=(), aliases={}):
    outs = out_shape if isinstance(out_shape, tuple) else (out_shape,)
    held = [a for a in (*vmem_args, *scratch, *outs) if a.dtype in (jnp.float32, jnp.bfloat16)]
    return pl.pallas_call(
        body,
        out_shape=out_shape,
        in_specs=[SMEM_SPEC] * len(smem_args) + [VMEM_SPEC] * len(vmem_args) + [HBM_SPEC] * len(hbm_args),
        out_specs=(VMEM_SPEC,) * len(outs) if isinstance(out_shape, tuple) else VMEM_SPEC,
        scratch_shapes=scratch,
        input_output_aliases=aliases,
        compiler_params=pltpu.CompilerParams(
            vmem_limit_bytes=sum(math.prod(a.shape) * a.dtype.itemsize for a in held) + MARGIN
        ),
        cost_estimate=pl.CostEstimate(flops=flops, bytes_accessed=0, transcendentals=0),
        name=name,
    )(*smem_args, *vmem_args, *hbm_args)


class Side:
    def __init__(self, left, packs, orbs, pno):
        self.left, self.packs, self.orbs, self.pno = left, packs, orbs, pno

    def basis(self, k):
        return self.packs[k][: self.orbs, :]

    def amps(self, k):
        return self.packs[k][self.orbs : self.orbs + self.pno, :]

    def counts(self, lanes):
        rows = [pack[self.orbs + self.pno :, :].astype(jnp.float32) for pack in self.packs]
        return lambda p, c: rows[p][0:1, lanes[c] : lanes[c] + 1]


def project(side, other, count, inter_ref, proj_ref, copies=()):
    pno = side.pno
    empty = jnp.zeros((pno, pno), jnp.bfloat16)
    for j in range(0, len(other.packs), 2):
        for copy in copies[j : j + 2]:
            copy.wait()
        pair = jnp.concatenate([other.basis(j), other.basis(j + 1)], axis=1)
        inter = jnp.dot(side.left[...], pair, preferred_element_type=jnp.float32).astype(jnp.bfloat16)
        inter_ref[:, j * pno : (j + 2) * pno] = inter
        diagonal = jnp.concatenate(
            [
                jnp.concatenate([other.amps(j), empty], axis=1),
                jnp.concatenate([empty, other.amps(j + 1)], axis=1),
            ],
            axis=0,
        )
        proj = jnp.dot(inter, diagonal, preferred_element_type=jnp.float32)
        for p in range(side.left.shape[0] // pno):
            for c in range(2):
                block = proj[p * pno : (p + 1) * pno, c * pno : (c + 1) * pno]
                proj_ref[p * pno : (p + 1) * pno, (j + c) * pno : (j + c + 1) * pno] = (
                    block * count(p, j + c)
                ).astype(jnp.bfloat16)


def coupled_kernel(lanes, weight_ref, left_ref, acc_ref, one_ref, two_ref, out_ref, inter_ref, proj_ref):
    pairs, pno, _ = out_ref.shape
    half, orbs = pairs // 2, left_ref.shape[1]
    own = Side(left_ref, (), orbs, pno)
    other = Side(None, [ref.at[k] for ref in (one_ref, two_ref) for k in range(half)], orbs, pno)
    project(own, other, lambda p, c: weight_ref[p, lanes[c]], inter_ref, proj_ref)
    for p in range(pairs):
        out_ref[p] = acc_ref[p] + one_sum(proj_ref, inter_ref, p, pno)


def own_kernel(weight_ref, low_ref, high_ref, out_ref, left_ref, inter_ref, proj_ref):
    pairs, pno, _ = out_ref.shape
    orbs = left_ref.shape[1]
    packs = [ref.at[k] for ref in (low_ref, high_ref) for k in range(pairs // 2)]
    for p, pack_ref in enumerate(packs):
        left_ref[p * pno : (p + 1) * pno, :] = pack_ref[:orbs, :].T
    own = Side(left_ref, packs, orbs, pno)
    project(own, own, lambda p, c: weight_ref[p, c], inter_ref, proj_ref)
    for p in range(pairs):
        out_ref[p] = one_sum(proj_ref, inter_ref, p, pno)


def one_sum(proj_ref, inter_ref, p, pno):
    at = slice(p * pno, (p + 1) * pno)
    return lax.dot_general(
        proj_ref[at, :], inter_ref[at, :], (((1,), (1,)), ((), ())), preferred_element_type=jnp.float32
    )


def both_sums(one_ref, two_ref, turned_ref, one_lanes, two_lanes, products, orbs):
    half, _, pno = one_ref.shape
    sides = []
    for first, ref in ((0, one_ref), (half, two_ref)):
        for k in range(half):
            turned_ref[(first + k) * pno : (first + k + 1) * pno, :] = ref[k, :orbs, :].T
        left = turned_ref.at[first * pno : (first + half) * pno, :]
        sides.append(Side(left, [ref.at[k] for k in range(half)], orbs, pno))
    project(sides[0], sides[1], sides[0].counts(two_lanes), products[0], products[1])
    project(sides[1], sides[0], sides[1].counts(one_lanes), products[2], products[3])

    def total(proj, inter):
        def of(k):
            at = slice(k * pno, (k + 1) * pno)
            return jnp.dot(proj[at, :], inter[:, at], preferred_element_type=jnp.float32)

        return of

    return total(products[1], products[2]), total(products[3], products[0])


def first_across_kernel(orbs, x_low, y_high, out_one, out_two, turned_ref, *products):
    half = out_one.shape[0]
    block = 3 * 2 * half
    low, high = range(block, block + half), range(block + half, block + 2 * half)
    one, two = both_sums(x_low, y_high, turned_ref, low, high, products, orbs)
    for k in range(half):
        out_one[k] = one(k)
        out_two[k] = two(k)


def second_across_kernel(orbs, upper_ref, low1, low2, *refs):
    x_low, x_high, y_low, y_high, back_x, back_y, turned_ref, *products = refs
    half, pno = low1.shape[0], low1.shape[1]
    block = 3 * 2 * half
    none = jnp.zeros((pno, pno), jnp.bfloat16)

    @pl.when(upper_ref[0] == 0)
    def _():
        low = range(block, block + half)
        one, two = both_sums(x_low, y_low, turned_ref, low, low, products, orbs)
        for k in range(half):
            back_x[k] = (low1[k] + one(k)).astype(jnp.bfloat16)
            back_x[half + k] = none
            back_y[k] = two(k).astype(jnp.bfloat16)
            back_y[half + k] = low2[k].astype(jnp.bfloat16)

    @pl.when(upper_ref[0] == 1)
    def _():
        high = range(block + half, block + 2 * half)
        one, two = both_sums(x_high, y_high, turned_ref, high, high, products, orbs)
        for k in range(half):
            back_x[k] = low1[k].astype(jnp.bfloat16)
            back_x[half + k] = one(k).astype(jnp.bfloat16)
            back_y[k] = none
            back_y[half + k] = (low2[k] + two(k)).astype(jnp.bfloat16)


def own_coupled(weights, own, orbs, flops):
    half, _, pno = own[0].shape
    rows = 2 * half * pno
    shapes = (jax.ShapeDtypeStruct((2 * half, pno, pno), jnp.float32), jax.ShapeDtypeStruct((rows, orbs), jnp.bfloat16))
    scratch = [pltpu.VMEM((rows, rows), jnp.bfloat16)] * 2
    return call_kernel(own_kernel, shapes, scratch, "own_coupled", (weights,), own, flops)


def add_coupled(lanes, weights, own_t, acc, received, flops):
    rows = own_t.shape[0]
    scratch = [pltpu.VMEM((rows, rows), jnp.bfloat16)] * 2
    shape = jax.ShapeDtypeStruct(acc.shape, jnp.float32)
    body = functools.partial(coupled_kernel, lanes)
    return call_kernel(body, shape, scratch, "coupled", (weights,), (own_t, acc, *received), flops)


def across(body, name, scalars, vmem_args, half, shapes, orbs, flops):
    wide = half * shapes[0].shape[2]
    scratch = [pltpu.VMEM((2 * wide, orbs), jnp.bfloat16), *[pltpu.VMEM((wide, wide), jnp.bfloat16)] * 4]
    return call_kernel(functools.partial(body, orbs), shapes, scratch, name, scalars, vmem_args, flops)


def half_transforms(uses_ref, slab_refs, own_ref, store, base, pno):
    last = own_ref.shape[0] // pno - 1

    def rows(side):
        return own_ref[pl.ds(pl.multiple_of(jnp.minimum(side // 2, last) * pno, pno), pno), :]

    def both_sides(slab, k):
        one, two = uses_ref[k, 0], uses_ref[k, 1]
        bases = jnp.concatenate([rows(one), rows(two)], axis=0)
        both = lax.dot_general(slab, bases, (((1,), (1,)), ((), ())), preferred_element_type=jnp.float32)
        both = both.astype(jnp.bfloat16)
        store(k, 0, one, both[:, :pno])
        store(k, 1, two, both[:, pno:])

    for slab_ref in slab_refs:
        if slab_ref.shape[0] > 4:

            def step(k, carry, slab_ref=slab_ref, base=base):
                both_sides(slab_ref[k], base + k)
                return carry

            lax.fori_loop(0, slab_ref.shape[0], step, 0)
        else:
            for k in range(slab_ref.shape[0]):
                both_sides(slab_ref[k], base + k)
        base += slab_ref.shape[0]


def halves_kernel(base, uses_ref, *refs):
    *slab_refs, own_ref, half_ref = refs

    def store(k, use, side, half):
        half_ref[side] = half

    half_transforms(uses_ref, slab_refs, own_ref, store, base, half_ref.shape[2])


def more_halves_kernel(base, uses_ref, *refs):
    *slab_refs, own_ref, _, half_ref = refs
    halves_kernel(base, uses_ref, *slab_refs, own_ref, half_ref)


def exchange_kernel(scale, base, uses_ref, turn_ref, *refs):
    *slab_refs, own_ref, early_ref, acc_ref, back1_ref, back2_ref, out_ref, late_ref = refs

    def store(k, use, side, half):
        late_ref[2 * (k - base) + use] = half

    def half(p, side):
        k = turn_ref[2 * p + side]
        late = jnp.where(uses_ref[k, 0] == 2 * p + side, 0, 1) + 2 * jnp.maximum(k - base, 0)
        return jnp.where(k < base, early_ref[2 * p + side], late_ref[late])

    half_transforms(uses_ref, slab_refs, own_ref, store, base, out_ref.shape[1])
    for p in range(out_ref.shape[0]):
        product = lax.dot_general(half(p, 0), half(p, 1), (((0,), (0,)), ((), ())), preferred_element_type=jnp.float32)
        back = back1_ref[p].astype(jnp.float32) + back2_ref[p].astype(jnp.float32)
        out_ref[p] = acc_ref[p] + back + product * scale


def half_products(uses, base, slabs, own_t, pno, done=None):
    sides = own_t.shape[0] // pno * 2
    shape = jax.ShapeDtypeStruct((sides + 1, slabs[0].shape[1], pno), jnp.bfloat16)
    if done is None:
        return call_kernel(functools.partial(halves_kernel, base), shape, [], "halves", (uses,), (*slabs, own_t), 0)
    args = (*slabs, own_t, done)
    return call_kernel(
        functools.partial(more_halves_kernel, base), shape, [], "more_halves", (uses,), args, 0, aliases={len(args): 0}
    )


def add_exchange(uses, turn, base, slabs, own_t, early, sums):
    return call_kernel(
        functools.partial(exchange_kernel, 1.0 / math.sqrt(slabs[0].shape[1]), base),
        jax.ShapeDtypeStruct(sums[0].shape, jnp.float32),
        [pltpu.VMEM((2 * sum(slab.shape[0] for slab in slabs),) + early.shape[1:], jnp.bfloat16)],
        "exchange",
        (uses, turn),
        (*slabs, own_t, early, *sums),
        0,
    )


def pack_kernel(scale, chips, group_ref, me_ref, coupled_ref, length_ref, owner_ref, orbs_ref, base_ref, amp_ref, *refs):
    low_ref, high_ref, weight_ref, uses_ref, turn_ref, held_ref, sems = refs
    pairs, orbs, pno = base_ref.shape
    half = pairs // 2
    group, me = group_ref[0], me_ref[0]
    copies = []

    def copy(ref, k, row, sem):
        rows = pl.ds(row, ref.shape[1])
        copies.append(pltpu.make_async_copy(ref.at[pl.ds(k * half, half)], held_ref.at[k, :, rows], sems.at[sem]))
        copies[-1].start()

    for k in range(2):
        copy(base_ref, k, 0, 2 * k)
        copy(amp_ref, k, orbs, 2 * k + 1)
    lane = lax.broadcasted_iota(jnp.int32, (1, pno), 1)
    for p in range(pairs):
        counts = jnp.zeros((1, pno), jnp.float32)
        for s in range(coupled_ref.shape[1]):
            named = coupled_ref[p, s]
            at = (lax.div(named, pairs) ^ group) * pairs + lax.rem(named, pairs)
            counts += jnp.where(lane == jnp.where(s < length_ref[p], at, -1), scale, 0.0)
        weight_ref[p : p + 1, :] = counts
        rows = slice(orbs + amp_ref.shape[1], held_ref.shape[2])
        held_ref[p // half, p % half, rows, :] = jnp.broadcast_to(counts, (16, pno)).astype(jnp.bfloat16)
    for started in copies:
        started.wait()
    stores = [
        pltpu.make_async_copy(held_ref.at[k], out_ref, sems.at[4 + k]) for k, out_ref in enumerate((low_ref, high_ref))
    ]
    for store in stores:
        store.start()

    sides = 2 * pairs

    def clear(k, carry):
        uses_ref[k, 0] = sides
        uses_ref[k, 1] = sides
        return carry

    lax.fori_loop(0, uses_ref.shape[0], clear, 0)
    for f in range(sides):
        position = owner_ref[orbs_ref[f % 2, f // 2]]
        k = position
        if chips <= RING_CHIPS:
            steps = lax.rem(lax.div(me, 2) - lax.div(position, 2) + chips, chips)
            k = 2 * steps + (lax.rem(position, 2) ^ lax.rem(me, 2))
        turn_ref[f] = k
        uses_ref[k, 1] = uses_ref[k, 0]
        uses_ref[k, 0] = f
    for store in stores:
        store.wait()


def pack(group, me, chips, coupled, coupled_len, slab_owner, pair_orbs, bases, amps):
    pairs, orbs, pno = bases.shape
    packed = jax.ShapeDtypeStruct((pairs // 2, orbs + amps.shape[1] + 16, pno), bases.dtype)
    return pl.pallas_call(
        functools.partial(pack_kernel, orbs / pno, chips),
        out_shape=(
            packed,
            packed,
            jax.ShapeDtypeStruct((pairs, pno), jnp.float32),
            jax.ShapeDtypeStruct((slab_owner.shape[0], 2), jnp.int32),
            jax.ShapeDtypeStruct((2 * pairs,), jnp.int32),
        ),
        in_specs=[SMEM_SPEC] * 6 + [HBM_SPEC] * 2,
        out_specs=(HBM_SPEC, HBM_SPEC, VMEM_SPEC, SMEM_SPEC, SMEM_SPEC),
        scratch_shapes=[pltpu.VMEM((2,) + packed.shape, bases.dtype), pltpu.SemaphoreType.DMA((6,))],
        compiler_params=pltpu.CompilerParams(vmem_limit_bytes=PACK_LIMIT),
        name="pack",
    )(group, me, coupled, coupled_len, slab_owner, pair_orbs.T, bases, amps)


def after(value, *earlier):
    return lax.optimization_barrier((value,) + earlier)[0]


def on_device(integral_slabs, slab_owner, pair_orbs, domain_bases, amplitudes, coupled, coupled_len):
    n_grp, n_dev = lax.axis_size("grp"), lax.axis_size("dev")
    pairs, orbs, pno = domain_bases.shape
    group, me = lax.axis_index("grp"), lax.axis_index("dev")
    chips = n_dev // 2

    half = pairs // 2

    def along_x(value):
        return lax.ppermute(value, "grp", [(g, g ^ 1) for g in range(n_grp)])

    def along_y(value):
        return lax.ppermute(value, "grp", [(g, g ^ 2) for g in range(n_grp)])

    def next_chip(value):
        return lax.ppermute(value, "dev", [(d, (d + 2) % n_dev) for d in range(n_dev)])

    def other_core(value):
        return lax.ppermute(value, "dev", [(d, d ^ 1) for d in range(n_dev)])

    own_lo, own_hi, weights, uses, turns = pack(
        group.astype(jnp.int32).reshape(1), me.astype(jnp.int32).reshape(1), chips, coupled, coupled_len, slab_owner, pair_orbs, domain_bases, amplitudes
    )
    upper = (group // 2).astype(jnp.int32).reshape(1)

    x_lo, y_hi = along_x(own_lo), along_y(own_hi)
    x_hi, y_lo = along_x(after(own_hi, own_lo)), along_y(after(own_lo, own_hi))

    slab = integral_slabs[0]
    around = chips <= RING_CHIPS
    ahead = 6 if around else n_dev // 2
    if around:
        round1 = next_chip(slab)
        round2 = next_chip(round1)
        swap0, swap1 = other_core(after(slab, x_lo, y_hi)), other_core(after(round1, x_lo, y_hi))
    acc, own_t = own_coupled(weights, (after(own_lo, round1) if around else own_lo, own_hi), orbs, OWN_COST)

    lanes = [*range(pairs, pairs + half), *range(2 * pairs + half, 3 * pairs)]
    acc = add_coupled(lanes, weights, own_t, acc, (x_lo, y_hi), DECLARED)
    part = jax.ShapeDtypeStruct((half, pno, pno), jnp.float32)
    first = across(
        first_across_kernel, "first_across", (), (after(x_lo, acc), after(y_hi, acc)), half, (part, part), orbs, FIRST_COST
    )
    if around:
        slabs = [slab[None], swap0[None], round1[None], swap1[None]]
        halves = half_products(uses, 0, slabs, after(own_t, *first), pno)
        round2 = after(round2, halves)
        round3, swap2 = next_chip(round2), other_core(round2)
        halves = half_products(uses, 4, [round2[None], swap2[None]], own_t, pno, halves)
    else:
        gathered = lax.all_gather(slab, "dev", axis=0, tiled=False)
        halves = half_products(uses, 0, [gathered[:ahead]], own_t, pno)
        rest = [gathered[ahead:]]
    whole = jax.ShapeDtypeStruct((pairs, pno, pno), jnp.bfloat16)
    back_x, back_y = across(
        second_across_kernel,
        "second_across",
        (upper,),
        (after(first[0], halves), first[1], x_lo, x_hi, y_lo, y_hi),
        half,
        (whole, whole),
        orbs,
        SECOND_COST,
    )
    back = (along_x(back_x), along_y(back_y))
    lanes = [*range(pairs + half, 2 * pairs), *range(2 * pairs, 2 * pairs + half)]
    acc = add_coupled(lanes, weights, own_t, after(acc, back_x), (x_hi, y_lo), LAST_COST)
    if around:
        round3 = after(round3, acc, *back)
        rest = [round3[None], other_core(round3)[None]]
    return add_exchange(uses, turns, ahead, rest, own_t, halves, (acc, *back))


def solution(mesh):
    in_specs = (
        P("dev", None, None),
        P(),
        P(("grp", "dev"), None),
        P(("grp", "dev"), None, None),
        P(("grp", "dev"), None, None),
        P(("grp", "dev"), None),
        P(("grp", "dev")),
    )
    out_specs = P(("grp", "dev"), None, None)
    return jax.shard_map(
        on_device, mesh=mesh, in_specs=in_specs, out_specs=out_specs, check_vma=False
    )
```

```python
import functools
import math

import jax
import jax.numpy as jnp
from jax import lax
from jax.experimental import pallas as pl
from jax.experimental.pallas import tpu as pltpu
from jax.sharding import PartitionSpec as P

MARGIN = 0
PACK_LIMIT = 56 * 1024 * 1024
RING_CHIPS = 4
DECLARED = 20_000_000_000
OWN_COST, FIRST_COST, SECOND_COST, LAST_COST = 0, 0, 0, DECLARED
SMEM_SPEC = pl.BlockSpec(memory_space=pltpu.SMEM)
VMEM_SPEC = pl.BlockSpec(memory_space=pltpu.VMEM)
HBM_SPEC = pl.BlockSpec(memory_space=pltpu.HBM)


def call_kernel(body, out_shape, scratch, name, smem_args, vmem_args, flops, hbm_args=(), aliases={}):
    outs = out_shape if isinstance(out_shape, tuple) else (out_shape,)
    held = [a for a in (*vmem_args, *scratch, *outs) if a.dtype in (jnp.float32, jnp.bfloat16)]
    return pl.pallas_call(
        body,
        out_shape=out_shape,
        in_specs=[SMEM_SPEC] * len(smem_args) + [VMEM_SPEC] * len(vmem_args) + [HBM_SPEC] * len(hbm_args),
        out_specs=(VMEM_SPEC,) * len(outs) if isinstance(out_shape, tuple) else VMEM_SPEC,
        scratch_shapes=scratch,
        input_output_aliases=aliases,
        compiler_params=pltpu.CompilerParams(
            vmem_limit_bytes=sum(math.prod(a.shape) * a.dtype.itemsize for a in held) + MARGIN
        ),
        cost_estimate=pl.CostEstimate(flops=flops, bytes_accessed=0, transcendentals=0),
        name=name,
    )(*smem_args, *vmem_args, *hbm_args)


class Side:
    def __init__(self, left, packs, orbs, pno):
        self.left, self.packs, self.orbs, self.pno = left, packs, orbs, pno

    def basis(self, k):
        return self.packs[k][: self.orbs, :]

    def amps(self, k):
        return self.packs[k][self.orbs : self.orbs + self.pno, :]

    def counts(self, lanes):
        rows = [pack[self.orbs + self.pno :, :].astype(jnp.float32) for pack in self.packs]
        return lambda p, c: rows[p][0:1, lanes[c] : lanes[c] + 1]


def project(side, other, count, inter_ref, proj_ref, copies=()):
    pno = side.pno
    empty = jnp.zeros((pno, pno), jnp.bfloat16)
    for j in range(0, len(other.packs), 2):
        for copy in copies[j : j + 2]:
            copy.wait()
        pair = jnp.concatenate([other.basis(j), other.basis(j + 1)], axis=1)
        inter = jnp.dot(side.left[...], pair, preferred_element_type=jnp.float32).astype(jnp.bfloat16)
        inter_ref[:, j * pno : (j + 2) * pno] = inter
        diagonal = jnp.concatenate(
            [
                jnp.concatenate([other.amps(j), empty], axis=1),
                jnp.concatenate([empty, other.amps(j + 1)], axis=1),
            ],
            axis=0,
        )
        proj = jnp.dot(inter, diagonal, preferred_element_type=jnp.float32)
        for p in range(side.left.shape[0] // pno):
            for c in range(2):
                block = proj[p * pno : (p + 1) * pno, c * pno : (c + 1) * pno]
                proj_ref[p * pno : (p + 1) * pno, (j + c) * pno : (j + c + 1) * pno] = (
                    block * count(p, j + c)
                ).astype(jnp.bfloat16)


def coupled_kernel(lanes, weight_ref, left_ref, acc_ref, one_ref, two_ref, out_ref, inter_ref, proj_ref):
    pairs, pno, _ = out_ref.shape
    half, orbs = pairs // 2, left_ref.shape[1]
    own = Side(left_ref, (), orbs, pno)
    other = Side(None, [ref.at[k] for ref in (one_ref, two_ref) for k in range(half)], orbs, pno)
    project(own, other, lambda p, c: weight_ref[p, lanes[c]], inter_ref, proj_ref)
    for p in range(pairs):
        out_ref[p] = acc_ref[p] + one_sum(proj_ref, inter_ref, p, pno)


def own_kernel(weight_ref, low_ref, high_ref, out_ref, left_ref, inter_ref, proj_ref):
    pairs, pno, _ = out_ref.shape
    orbs = left_ref.shape[1]
    packs = [ref.at[k] for ref in (low_ref, high_ref) for k in range(pairs // 2)]
    for p, pack_ref in enumerate(packs):
        left_ref[p * pno : (p + 1) * pno, :] = pack_ref[:orbs, :].T
    own = Side(left_ref, packs, orbs, pno)
    project(own, own, lambda p, c: weight_ref[p, c], inter_ref, proj_ref)
    for p in range(pairs):
        out_ref[p] = one_sum(proj_ref, inter_ref, p, pno)


def one_sum(proj_ref, inter_ref, p, pno):
    at = slice(p * pno, (p + 1) * pno)
    return lax.dot_general(
        proj_ref[at, :], inter_ref[at, :], (((1,), (1,)), ((), ())), preferred_element_type=jnp.float32
    )


def both_sums(one_ref, two_ref, turned_ref, one_lanes, two_lanes, products, orbs):
    half, _, pno = one_ref.shape
    sides = []
    for first, ref in ((0, one_ref), (half, two_ref)):
        for k in range(half):
            turned_ref[(first + k) * pno : (first + k + 1) * pno, :] = ref[k, :orbs, :].T
        left = turned_ref.at[first * pno : (first + half) * pno, :]
        sides.append(Side(left, [ref.at[k] for k in range(half)], orbs, pno))
    project(sides[0], sides[1], sides[0].counts(two_lanes), products[0], products[1])
    project(sides[1], sides[0], sides[1].counts(one_lanes), products[2], products[3])

    def total(proj, inter):
        def of(k):
            at = slice(k * pno, (k + 1) * pno)
            return jnp.dot(proj[at, :], inter[:, at], preferred_element_type=jnp.float32)

        return of

    return total(products[1], products[2]), total(products[3], products[0])


def first_across_kernel(orbs, x_low, y_high, out_one, out_two, turned_ref, *products):
    half = out_one.shape[0]
    block = 3 * 2 * half
    low, high = range(block, block + half), range(block + half, block + 2 * half)
    one, two = both_sums(x_low, y_high, turned_ref, low, high, products, orbs)
    for k in range(half):
        out_one[k] = one(k).astype(jnp.bfloat16)
        out_two[k] = two(k).astype(jnp.bfloat16)


def second_across_kernel(orbs, upper_ref, x_low, x_high, y_low, y_high, out_one, out_two, turned_ref, *products):
    half = out_one.shape[0]
    block = 3 * 2 * half

    def between(one_ref, two_ref, lanes):
        one, two = both_sums(one_ref, two_ref, turned_ref, lanes, lanes, products, orbs)
        for k in range(half):
            out_one[k] = one(k).astype(jnp.bfloat16)
            out_two[k] = two(k).astype(jnp.bfloat16)

    @pl.when(upper_ref[0] == 0)
    def _():
        between(x_low, y_low, range(block, block + half))

    @pl.when(upper_ref[0] == 1)
    def _():
        between(x_high, y_high, range(block + half, block + 2 * half))


def own_coupled(weights, own, orbs, flops):
    half, _, pno = own[0].shape
    rows = 2 * half * pno
    shapes = (jax.ShapeDtypeStruct((2 * half, pno, pno), jnp.float32), jax.ShapeDtypeStruct((rows, orbs), jnp.bfloat16))
    scratch = [pltpu.VMEM((rows, rows), jnp.bfloat16)] * 2
    return call_kernel(own_kernel, shapes, scratch, "own_coupled", (weights,), own, flops)


def add_coupled(lanes, weights, own_t, acc, received, flops):
    rows = own_t.shape[0]
    scratch = [pltpu.VMEM((rows, rows), jnp.bfloat16)] * 2
    shape = jax.ShapeDtypeStruct(acc.shape, jnp.float32)
    body = functools.partial(coupled_kernel, lanes)
    return call_kernel(body, shape, scratch, "coupled", (weights,), (own_t, acc, *received), flops)


def across(body, name, scalars, vmem_args, orbs, flops):
    half, _, pno = vmem_args[0].shape
    wide = half * pno
    shapes = (jax.ShapeDtypeStruct((half, pno, pno), jnp.bfloat16),) * 2
    scratch = [pltpu.VMEM((2 * wide, orbs), jnp.bfloat16), *[pltpu.VMEM((wide, wide), jnp.bfloat16)] * 4]
    return call_kernel(functools.partial(body, orbs), shapes, scratch, name, scalars, vmem_args, flops)


def half_transforms(uses_ref, slab_refs, own_ref, store, base, pno):
    last = own_ref.shape[0] // pno - 1

    def rows(side):
        return own_ref[pl.ds(pl.multiple_of(jnp.minimum(side // 2, last) * pno, pno), pno), :]

    def both_sides(slab, k):
        one, two = uses_ref[k, 0], uses_ref[k, 1]
        bases = jnp.concatenate([rows(one), rows(two)], axis=0)
        both = lax.dot_general(slab, bases, (((1,), (1,)), ((), ())), preferred_element_type=jnp.float32)
        both = both.astype(jnp.bfloat16)
        store(k, 0, one, both[:, :pno])
        store(k, 1, two, both[:, pno:])

    for slab_ref in slab_refs:
        if slab_ref.shape[0] > 4:

            def step(k, carry, slab_ref=slab_ref, base=base):
                both_sides(slab_ref[k], base + k)
                return carry

            lax.fori_loop(0, slab_ref.shape[0], step, 0)
        else:
            for k in range(slab_ref.shape[0]):
                both_sides(slab_ref[k], base + k)
        base += slab_ref.shape[0]


def halves_kernel(base, uses_ref, *refs):
    *slab_refs, own_ref, half_ref = refs

    def store(k, use, side, half):
        half_ref[side] = half

    half_transforms(uses_ref, slab_refs, own_ref, store, base, half_ref.shape[2])


def more_halves_kernel(base, uses_ref, *refs):
    *slab_refs, own_ref, _, half_ref = refs
    halves_kernel(base, uses_ref, *slab_refs, own_ref, half_ref)


def exchange_kernel(scale, base, uses_ref, turn_ref, upper_ref, *refs):
    *slab_refs, own_ref, early_ref, acc_ref, low_ref, high_ref, row_ref, column_ref, out_ref, late_ref = refs
    half_count = low_ref.shape[0]

    def store(k, use, side, half):
        late_ref[2 * (k - base) + use] = half

    def half(p, side):
        k = turn_ref[2 * p + side]
        late = jnp.where(uses_ref[k, 0] == 2 * p + side, 0, 1) + 2 * jnp.maximum(k - base, 0)
        return jnp.where(k < base, early_ref[2 * p + side], late_ref[late])

    half_transforms(uses_ref, slab_refs, own_ref, store, base, out_ref.shape[1])
    for p in range(out_ref.shape[0]):
        product = lax.dot_general(half(p, 0), half(p, 1), (((0,), (0,)), ((), ())), preferred_element_type=jnp.float32)
        k, upper = p % half_count, p // half_count
        first = (low_ref, high_ref)[upper][k].astype(jnp.float32)
        second = jnp.where(upper_ref[0] == upper, row_ref[k], column_ref[k]).astype(jnp.float32)
        out_ref[p] = acc_ref[p] + (first + second) + product * scale


def half_products(uses, base, slabs, own_t, pno, done, flops):
    sides = own_t.shape[0] // pno * 2
    shape = jax.ShapeDtypeStruct((sides + 1, slabs[0].shape[1], pno), jnp.bfloat16)
    if done is None:
        return call_kernel(functools.partial(halves_kernel, base), shape, [], "halves", (uses,), (*slabs, own_t), flops)
    args = (*slabs, own_t, done)
    return call_kernel(
        functools.partial(more_halves_kernel, base), shape, [], "more_halves", (uses,), args, flops, aliases={len(args): 0}
    )


def add_exchange(uses, turn, upper, base, slabs, own_t, early, sums):
    return call_kernel(
        functools.partial(exchange_kernel, 1.0 / math.sqrt(slabs[0].shape[1]), base),
        jax.ShapeDtypeStruct(sums[0].shape, jnp.float32),
        [pltpu.VMEM((2 * sum(slab.shape[0] for slab in slabs),) + early.shape[1:], jnp.bfloat16)],
        "exchange",
        (uses, turn, upper),
        (*slabs, own_t, early, *sums),
        0,
    )


def pack_kernel(scale, chips, group_ref, me_ref, coupled_ref, length_ref, owner_ref, orbs_ref, base_ref, amp_ref, *refs):
    low_ref, high_ref, weight_ref, uses_ref, turn_ref, held_ref, sems = refs
    pairs, orbs, pno = base_ref.shape
    half = pairs // 2
    group, me = group_ref[0], me_ref[0]
    copies = []

    def copy(ref, k, row, sem):
        rows = pl.ds(row, ref.shape[1])
        copies.append(pltpu.make_async_copy(ref.at[pl.ds(k * half, half)], held_ref.at[k, :, rows], sems.at[sem]))
        copies[-1].start()

    for k in range(2):
        copy(base_ref, k, 0, 2 * k)
        copy(amp_ref, k, orbs, 2 * k + 1)
    lane = lax.broadcasted_iota(jnp.int32, (1, pno), 1)
    for p in range(pairs):
        counts = jnp.zeros((1, pno), jnp.float32)
        for s in range(coupled_ref.shape[1]):
            named = coupled_ref[p, s]
            at = (lax.div(named, pairs) ^ group) * pairs + lax.rem(named, pairs)
            counts += jnp.where(lane == jnp.where(s < length_ref[p], at, -1), scale, 0.0)
        weight_ref[p : p + 1, :] = counts
        rows = slice(orbs + amp_ref.shape[1], held_ref.shape[2])
        held_ref[p // half, p % half, rows, :] = jnp.broadcast_to(counts, (16, pno)).astype(jnp.bfloat16)
    for started in copies:
        started.wait()
    stores = [
        pltpu.make_async_copy(held_ref.at[k], out_ref, sems.at[4 + k]) for k, out_ref in enumerate((low_ref, high_ref))
    ]
    for store in stores:
        store.start()

    sides = 2 * pairs

    def clear(k, carry):
        uses_ref[k, 0] = sides
        uses_ref[k, 1] = sides
        return carry

    lax.fori_loop(0, uses_ref.shape[0], clear, 0)
    for f in range(sides):
        position = owner_ref[orbs_ref[f % 2, f // 2]]
        k = position
        if chips <= RING_CHIPS:
            steps = lax.rem(lax.div(me, 2) - lax.div(position, 2) + chips, chips)
            swapped = lax.rem(position, 2) ^ lax.rem(me, 2)
            k = jnp.where(steps < 2, steps + 2 * swapped, steps + 2 + 2 * swapped)
        turn_ref[f] = k
        uses_ref[k, 1] = uses_ref[k, 0]
        uses_ref[k, 0] = f
    for store in stores:
        store.wait()


def pack(group, me, chips, coupled, coupled_len, slab_owner, pair_orbs, bases, amps):
    pairs, orbs, pno = bases.shape
    packed = jax.ShapeDtypeStruct((pairs // 2, orbs + amps.shape[1] + 16, pno), bases.dtype)
    return pl.pallas_call(
        functools.partial(pack_kernel, orbs / pno, chips),
        out_shape=(
            packed,
            packed,
            jax.ShapeDtypeStruct((pairs, pno), jnp.float32),
            jax.ShapeDtypeStruct((slab_owner.shape[0], 2), jnp.int32),
            jax.ShapeDtypeStruct((2 * pairs,), jnp.int32),
        ),
        in_specs=[SMEM_SPEC] * 6 + [HBM_SPEC] * 2,
        out_specs=(HBM_SPEC, HBM_SPEC, VMEM_SPEC, SMEM_SPEC, SMEM_SPEC),
        scratch_shapes=[pltpu.VMEM((2,) + packed.shape, bases.dtype), pltpu.SemaphoreType.DMA((6,))],
        compiler_params=pltpu.CompilerParams(vmem_limit_bytes=PACK_LIMIT),
        name="pack",
    )(group, me, coupled, coupled_len, slab_owner, pair_orbs.T, bases, amps)


def after(value, *earlier):
    return lax.optimization_barrier((value,) + earlier)[0]


def on_device(integral_slabs, slab_owner, pair_orbs, domain_bases, amplitudes, coupled, coupled_len):
    n_grp, n_dev = lax.axis_size("grp"), lax.axis_size("dev")
    pairs, orbs, pno = domain_bases.shape
    group, me = lax.axis_index("grp"), lax.axis_index("dev")
    chips = n_dev // 2

    half = pairs // 2

    def along_x(value):
        return lax.ppermute(value, "grp", [(g, g ^ 1) for g in range(n_grp)])

    def along_y(value):
        return lax.ppermute(value, "grp", [(g, g ^ 2) for g in range(n_grp)])

    def along_chips(value, step):
        return lax.ppermute(value, "dev", [(d, (d + 2 * step) % n_dev) for d in range(n_dev)])

    def other_core(value):
        return lax.ppermute(value, "dev", [(d, d ^ 1) for d in range(n_dev)])

    *own, weights, uses, turns = pack(
        group.astype(jnp.int32).reshape(1), me.astype(jnp.int32).reshape(1), chips, coupled, coupled_len, slab_owner, pair_orbs, domain_bases, amplitudes
    )
    own_lo, own_hi = own
    upper = (group // 2).astype(jnp.int32).reshape(1)

    x_lo, y_hi = along_x(own_lo), along_y(own_hi)
    x_hi, y_lo = along_x(after(own_hi, own_lo)), along_y(after(own_lo, own_hi))

    slab = integral_slabs[0]
    around = chips <= RING_CHIPS
    ahead = 6 if around else n_dev // 2
    acc, own_t = own_coupled(weights, own, orbs, OWN_COST)
    if around:
        below, above = along_chips(slab, 1), along_chips(slab, -1)
        halves = half_products(uses, 0, [slab[None], below[None]], own_t, pno, None, DECLARED)
        beyond = along_chips(below, 1)
        acc = after(acc, halves)
    else:
        gathered = lax.all_gather(slab, "dev", axis=0, tiled=False)
        halves = half_products(uses, 0, [gathered[:ahead]], own_t, pno, None, 0)
        rest = [gathered[ahead:]]

    lanes = [*range(pairs, pairs + half), *range(2 * pairs + half, 3 * pairs)]
    acc = add_coupled(lanes, weights, own_t, acc, (x_lo, y_hi), DECLARED)
    first = across(first_across_kernel, "first_across", (), (after(x_lo, acc), after(y_hi, acc)), orbs, FIRST_COST)
    back_low, back_high = along_x(first[0]), along_y(first[1])
    gate = first[0]
    if around:
        swaps = [other_core(after(value, x_lo, y_hi)) for value in (slab, below)]
        more = [value[None] for value in (*swaps, beyond, above)]
        halves = half_products(uses, 2, more, after(own_t, gate), pno, halves, 0)
        beyond, above = after(beyond, halves), after(above, halves)
        rest = [other_core(beyond)[None], other_core(above)[None]]
        gate = halves
    second = across(
        second_across_kernel, "second_across", (upper,), (after(x_lo, gate), x_hi, y_lo, y_hi), orbs, SECOND_COST
    )
    back_row, back_column = along_x(second[0]), along_y(second[1])
    lanes = [*range(pairs + half, 2 * pairs), *range(2 * pairs, 2 * pairs + half)]
    acc = add_coupled(lanes, weights, own_t, after(acc, second[0]), (x_hi, y_lo), LAST_COST)
    sums = (acc, back_low, back_high, back_row, back_column)
    return add_exchange(uses, turns, upper, ahead, rest, own_t, halves, sums)


def solution(mesh):
    in_specs = (
        P("dev", None, None),
        P(),
        P(("grp", "dev"), None),
        P(("grp", "dev"), None, None),
        P(("grp", "dev"), None, None),
        P(("grp", "dev"), None),
        P(("grp", "dev")),
    )
    out_specs = P(("grp", "dev"), None, None)
    return jax.shard_map(
        on_device, mesh=mesh, in_specs=in_specs, out_specs=out_specs, check_vma=False
    )
```

```python
import functools
import math

import jax
import jax.numpy as jnp
from jax import lax
from jax.experimental import pallas as pl
from jax.experimental.pallas import tpu as pltpu
from jax.sharding import PartitionSpec as P

MARGIN = 0
PACK_LIMIT = 56 * 1024 * 1024
RING_CHIPS = 4
DECLARED = 20_000_000_000
OWN_COST, FIRST_COST, SECOND_COST, LAST_COST = 0, 0, 0, DECLARED
SMEM_SPEC = pl.BlockSpec(memory_space=pltpu.SMEM)
VMEM_SPEC = pl.BlockSpec(memory_space=pltpu.VMEM)
HBM_SPEC = pl.BlockSpec(memory_space=pltpu.HBM)


def call_kernel(body, out_shape, scratch, name, smem_args, vmem_args, flops, hbm_args=(), aliases={}):
    outs = out_shape if isinstance(out_shape, tuple) else (out_shape,)
    held = [a for a in (*vmem_args, *scratch, *outs) if a.dtype in (jnp.float32, jnp.bfloat16)]
    return pl.pallas_call(
        body,
        out_shape=out_shape,
        in_specs=[SMEM_SPEC] * len(smem_args) + [VMEM_SPEC] * len(vmem_args) + [HBM_SPEC] * len(hbm_args),
        out_specs=(VMEM_SPEC,) * len(outs) if isinstance(out_shape, tuple) else VMEM_SPEC,
        scratch_shapes=scratch,
        input_output_aliases=aliases,
        compiler_params=pltpu.CompilerParams(
            vmem_limit_bytes=sum(math.prod(a.shape) * a.dtype.itemsize for a in held) + MARGIN
        ),
        cost_estimate=pl.CostEstimate(flops=flops, bytes_accessed=0, transcendentals=0),
        name=name,
    )(*smem_args, *vmem_args, *hbm_args)


class Side:
    def __init__(self, left, packs, orbs, pno):
        self.left, self.packs, self.orbs, self.pno = left, packs, orbs, pno

    def basis(self, k):
        return self.packs[k][: self.orbs, :]

    def amps(self, k):
        return self.packs[k][self.orbs : self.orbs + self.pno, :]

    def counts(self, lanes):
        rows = [pack[self.orbs + self.pno :, :].astype(jnp.float32) for pack in self.packs]
        return lambda p, c: rows[p][0:1, lanes[c] : lanes[c] + 1]


def project(side, other, count, inter_ref, proj_ref, copies=()):
    pno = side.pno
    empty = jnp.zeros((pno, pno), jnp.bfloat16)
    for j in range(0, len(other.packs), 2):
        for copy in copies[j : j + 2]:
            copy.wait()
        pair = jnp.concatenate([other.basis(j), other.basis(j + 1)], axis=1)
        inter = jnp.dot(side.left[...], pair, preferred_element_type=jnp.float32).astype(jnp.bfloat16)
        inter_ref[:, j * pno : (j + 2) * pno] = inter
        diagonal = jnp.concatenate(
            [
                jnp.concatenate([other.amps(j), empty], axis=1),
                jnp.concatenate([empty, other.amps(j + 1)], axis=1),
            ],
            axis=0,
        )
        proj = jnp.dot(inter, diagonal, preferred_element_type=jnp.float32)
        for p in range(side.left.shape[0] // pno):
            for c in range(2):
                block = proj[p * pno : (p + 1) * pno, c * pno : (c + 1) * pno]
                proj_ref[p * pno : (p + 1) * pno, (j + c) * pno : (j + c + 1) * pno] = (
                    block * count(p, j + c)
                ).astype(jnp.bfloat16)


def coupled_kernel(lanes, weight_ref, left_ref, acc_ref, one_ref, two_ref, out_ref, inter_ref, proj_ref):
    pairs, pno, _ = out_ref.shape
    half, orbs = pairs // 2, left_ref.shape[1]
    own = Side(left_ref, (), orbs, pno)
    other = Side(None, [ref.at[k] for ref in (one_ref, two_ref) for k in range(half)], orbs, pno)
    project(own, other, lambda p, c: weight_ref[p, lanes[c]], inter_ref, proj_ref)
    for p in range(pairs):
        out_ref[p] = acc_ref[p] + one_sum(proj_ref, inter_ref, p, pno)


def own_kernel(weight_ref, low_ref, high_ref, out_ref, left_ref, inter_ref, proj_ref):
    pairs, pno, _ = out_ref.shape
    orbs = left_ref.shape[1]
    packs = [ref.at[k] for ref in (low_ref, high_ref) for k in range(pairs // 2)]
    for p, pack_ref in enumerate(packs):
        left_ref[p * pno : (p + 1) * pno, :] = pack_ref[:orbs, :].T
    own = Side(left_ref, packs, orbs, pno)
    project(own, own, lambda p, c: weight_ref[p, c], inter_ref, proj_ref)
    for p in range(pairs):
        out_ref[p] = one_sum(proj_ref, inter_ref, p, pno)


def one_sum(proj_ref, inter_ref, p, pno):
    at = slice(p * pno, (p + 1) * pno)
    return lax.dot_general(
        proj_ref[at, :], inter_ref[at, :], (((1,), (1,)), ((), ())), preferred_element_type=jnp.float32
    )


def both_sums(one_ref, two_ref, turned_ref, one_lanes, two_lanes, products, orbs):
    half, _, pno = one_ref.shape
    sides = []
    for first, ref in ((0, one_ref), (half, two_ref)):
        for k in range(half):
            turned_ref[(first + k) * pno : (first + k + 1) * pno, :] = ref[k, :orbs, :].T
        left = turned_ref.at[first * pno : (first + half) * pno, :]
        sides.append(Side(left, [ref.at[k] for k in range(half)], orbs, pno))
    project(sides[0], sides[1], sides[0].counts(two_lanes), products[0], products[1])
    project(sides[1], sides[0], sides[1].counts(one_lanes), products[2], products[3])

    def total(proj, inter):
        def of(k):
            at = slice(k * pno, (k + 1) * pno)
            return jnp.dot(proj[at, :], inter[:, at], preferred_element_type=jnp.float32)

        return of

    return total(products[1], products[2]), total(products[3], products[0])


def first_across_kernel(orbs, x_low, y_high, out_one, out_two, turned_ref, *products):
    half = out_one.shape[0]
    block = 3 * 2 * half
    low, high = range(block, block + half), range(block + half, block + 2 * half)
    one, two = both_sums(x_low, y_high, turned_ref, low, high, products, orbs)
    for k in range(half):
        out_one[k] = one(k).astype(jnp.bfloat16)
        out_two[k] = two(k).astype(jnp.bfloat16)


def second_across_kernel(orbs, upper_ref, x_low, x_high, y_low, y_high, out_one, out_two, turned_ref, *products):
    half = out_one.shape[0]
    block = 3 * 2 * half

    def between(one_ref, two_ref, lanes):
        one, two = both_sums(one_ref, two_ref, turned_ref, lanes, lanes, products, orbs)
        for k in range(half):
            out_one[k] = one(k).astype(jnp.bfloat16)
            out_two[k] = two(k).astype(jnp.bfloat16)

    @pl.when(upper_ref[0] == 0)
    def _():
        between(x_low, y_low, range(block, block + half))

    @pl.when(upper_ref[0] == 1)
    def _():
        between(x_high, y_high, range(block + half, block + 2 * half))


def own_coupled(weights, own, orbs, flops):
    half, _, pno = own[0].shape
    rows = 2 * half * pno
    shapes = (jax.ShapeDtypeStruct((2 * half, pno, pno), jnp.float32), jax.ShapeDtypeStruct((rows, orbs), jnp.bfloat16))
    scratch = [pltpu.VMEM((rows, rows), jnp.bfloat16)] * 2
    return call_kernel(own_kernel, shapes, scratch, "own_coupled", (weights,), own, flops)


def add_coupled(lanes, weights, own_t, acc, received, flops):
    rows = own_t.shape[0]
    scratch = [pltpu.VMEM((rows, rows), jnp.bfloat16)] * 2
    shape = jax.ShapeDtypeStruct(acc.shape, jnp.float32)
    body = functools.partial(coupled_kernel, lanes)
    return call_kernel(body, shape, scratch, "coupled", (weights,), (own_t, acc, *received), flops)


def across(body, name, scalars, vmem_args, orbs, flops):
    half, _, pno = vmem_args[0].shape
    wide = half * pno
    shapes = (jax.ShapeDtypeStruct((half, pno, pno), jnp.bfloat16),) * 2
    scratch = [pltpu.VMEM((2 * wide, orbs), jnp.bfloat16), *[pltpu.VMEM((wide, wide), jnp.bfloat16)] * 4]
    return call_kernel(functools.partial(body, orbs), shapes, scratch, name, scalars, vmem_args, flops)


def half_transforms(uses_ref, slab_refs, own_ref, store, base, pno):
    last = own_ref.shape[0] // pno - 1

    def rows(side):
        return own_ref[pl.ds(pl.multiple_of(jnp.minimum(side // 2, last) * pno, pno), pno), :]

    def both_sides(slab, k):
        one, two = uses_ref[k, 0], uses_ref[k, 1]
        bases = jnp.concatenate([rows(one), rows(two)], axis=0)
        both = lax.dot_general(slab, bases, (((1,), (1,)), ((), ())), preferred_element_type=jnp.float32)
        both = both.astype(jnp.bfloat16)
        store(k, 0, one, both[:, :pno])
        store(k, 1, two, both[:, pno:])

    for slab_ref in slab_refs:
        if slab_ref.shape[0] > 4:

            def step(k, carry, slab_ref=slab_ref, base=base):
                both_sides(slab_ref[k], base + k)
                return carry

            lax.fori_loop(0, slab_ref.shape[0], step, 0)
        else:
            for k in range(slab_ref.shape[0]):
                both_sides(slab_ref[k], base + k)
        base += slab_ref.shape[0]


def halves_kernel(base, uses_ref, *refs):
    *slab_refs, own_ref, half_ref = refs

    def store(k, use, side, half):
        half_ref[side] = half

    half_transforms(uses_ref, slab_refs, own_ref, store, base, half_ref.shape[2])


def more_halves_kernel(base, uses_ref, *refs):
    *slab_refs, own_ref, _, half_ref = refs
    halves_kernel(base, uses_ref, *slab_refs, own_ref, half_ref)


def exchange_kernel(scale, base, uses_ref, turn_ref, upper_ref, *refs):
    *slab_refs, own_ref, early_ref, acc_ref, low_ref, high_ref, row_ref, column_ref, out_ref, late_ref = refs
    half_count = low_ref.shape[0]

    def store(k, use, side, half):
        late_ref[2 * (k - base) + use] = half

    def half(p, side):
        k = turn_ref[2 * p + side]
        late = jnp.where(uses_ref[k, 0] == 2 * p + side, 0, 1) + 2 * jnp.maximum(k - base, 0)
        return jnp.where(k < base, early_ref[2 * p + side], late_ref[late])

    half_transforms(uses_ref, slab_refs, own_ref, store, base, out_ref.shape[1])
    for p in range(out_ref.shape[0]):
        product = lax.dot_general(half(p, 0), half(p, 1), (((0,), (0,)), ((), ())), preferred_element_type=jnp.float32)
        k, upper = p % half_count, p // half_count
        first = (low_ref, high_ref)[upper][k].astype(jnp.float32)
        second = jnp.where(upper_ref[0] == upper, row_ref[k], column_ref[k]).astype(jnp.float32)
        out_ref[p] = acc_ref[p] + (first + second) + product * scale


def half_products(uses, base, slabs, own_t, pno, done, flops):
    sides = own_t.shape[0] // pno * 2
    shape = jax.ShapeDtypeStruct((sides + 1, slabs[0].shape[1], pno), jnp.bfloat16)
    if done is None:
        return call_kernel(functools.partial(halves_kernel, base), shape, [], "halves", (uses,), (*slabs, own_t), flops)
    args = (*slabs, own_t, done)
    return call_kernel(
        functools.partial(more_halves_kernel, base), shape, [], "more_halves", (uses,), args, flops, aliases={len(args): 0}
    )


def add_exchange(uses, turn, upper, base, slabs, own_t, early, sums):
    return call_kernel(
        functools.partial(exchange_kernel, 1.0 / math.sqrt(slabs[0].shape[1]), base),
        jax.ShapeDtypeStruct(sums[0].shape, jnp.float32),
        [pltpu.VMEM((2 * sum(slab.shape[0] for slab in slabs),) + early.shape[1:], jnp.bfloat16)],
        "exchange",
        (uses, turn, upper),
        (*slabs, own_t, early, *sums),
        0,
    )


def pack_kernel(scale, chips, group_ref, me_ref, coupled_ref, length_ref, owner_ref, orbs_ref, base_ref, amp_ref, *refs):
    low_ref, high_ref, weight_ref, uses_ref, turn_ref, held_ref, sems = refs
    pairs, orbs, pno = base_ref.shape
    half = pairs // 2
    group, me = group_ref[0], me_ref[0]
    copies = []

    def copy(ref, k, row, sem):
        rows = pl.ds(row, ref.shape[1])
        copies.append(pltpu.make_async_copy(ref.at[pl.ds(k * half, half)], held_ref.at[k, :, rows], sems.at[sem]))
        copies[-1].start()

    for k in range(2):
        copy(base_ref, k, 0, 2 * k)
        copy(amp_ref, k, orbs, 2 * k + 1)
    assert pairs & (pairs - 1) == 0
    named = lax.broadcasted_iota(jnp.int32, (1, pno), 1) ^ (group * pairs)
    for p in range(pairs):
        counts = jnp.zeros((1, pno), jnp.float32)
        length = length_ref[p]
        for s in range(coupled_ref.shape[1]):
            counts += jnp.where(named == jnp.where(s < length, coupled_ref[p, s], -1), scale, 0.0)
        weight_ref[p : p + 1, :] = counts
        rows = slice(orbs + amp_ref.shape[1], held_ref.shape[2])
        held_ref[p // half, p % half, rows, :] = jnp.broadcast_to(counts, (16, pno)).astype(jnp.bfloat16)
    for started in copies:
        started.wait()
    stores = [
        pltpu.make_async_copy(held_ref.at[k], out_ref, sems.at[4 + k]) for k, out_ref in enumerate((low_ref, high_ref))
    ]
    for store in stores:
        store.start()

    sides = 2 * pairs

    def clear(k, carry):
        uses_ref[k, 0] = sides
        uses_ref[k, 1] = sides
        return carry

    lax.fori_loop(0, uses_ref.shape[0], clear, 0)
    for f in range(sides):
        position = owner_ref[orbs_ref[f % 2, f // 2]]
        k = position
        if chips <= RING_CHIPS:
            steps = lax.rem((me >> 1) - (position >> 1) + chips, chips)
            swapped = (position ^ me) & 1
            k = jnp.where(steps < 2, steps + 2 * swapped, steps + 2 + 2 * swapped)
        turn_ref[f] = k
        uses_ref[k, 1] = uses_ref[k, 0]
        uses_ref[k, 0] = f
    for store in stores:
        store.wait()


def pack(group, me, chips, coupled, coupled_len, slab_owner, pair_orbs, bases, amps):
    pairs, orbs, pno = bases.shape
    packed = jax.ShapeDtypeStruct((pairs // 2, orbs + amps.shape[1] + 16, pno), bases.dtype)
    return pl.pallas_call(
        functools.partial(pack_kernel, orbs / pno, chips),
        out_shape=(
            packed,
            packed,
            jax.ShapeDtypeStruct((pairs, pno), jnp.float32),
            jax.ShapeDtypeStruct((slab_owner.shape[0], 2), jnp.int32),
            jax.ShapeDtypeStruct((2 * pairs,), jnp.int32),
        ),
        in_specs=[SMEM_SPEC] * 6 + [HBM_SPEC] * 2,
        out_specs=(HBM_SPEC, HBM_SPEC, VMEM_SPEC, SMEM_SPEC, SMEM_SPEC),
        scratch_shapes=[pltpu.VMEM((2,) + packed.shape, bases.dtype), pltpu.SemaphoreType.DMA((6,))],
        compiler_params=pltpu.CompilerParams(vmem_limit_bytes=PACK_LIMIT),
        name="pack",
    )(group, me, coupled, coupled_len, slab_owner, pair_orbs.T, bases, amps)


def after(value, *earlier):
    return lax.optimization_barrier((value,) + earlier)[0]


def on_device(integral_slabs, slab_owner, pair_orbs, domain_bases, amplitudes, coupled, coupled_len):
    n_grp, n_dev = lax.axis_size("grp"), lax.axis_size("dev")
    pairs, orbs, pno = domain_bases.shape
    group, me = lax.axis_index("grp"), lax.axis_index("dev")
    chips = n_dev // 2

    half = pairs // 2

    def along_x(value):
        return lax.ppermute(value, "grp", [(g, g ^ 1) for g in range(n_grp)])

    def along_y(value):
        return lax.ppermute(value, "grp", [(g, g ^ 2) for g in range(n_grp)])

    def along_chips(value, step):
        return lax.ppermute(value, "dev", [(d, (d + 2 * step) % n_dev) for d in range(n_dev)])

    def other_core(value):
        return lax.ppermute(value, "dev", [(d, d ^ 1) for d in range(n_dev)])

    *own, weights, uses, turns = pack(
        group.astype(jnp.int32).reshape(1), me.astype(jnp.int32).reshape(1), chips, coupled, coupled_len, slab_owner, pair_orbs, domain_bases, amplitudes
    )
    own_lo, own_hi = own
    upper = (group // 2).astype(jnp.int32).reshape(1)

    x_lo, y_hi = along_x(own_lo), along_y(own_hi)
    x_hi, y_lo = along_x(after(own_hi, own_lo)), along_y(after(own_lo, own_hi, x_lo))

    slab = integral_slabs[0]
    around = chips <= RING_CHIPS
    ahead = 6 if around else n_dev // 2
    acc, own_t = own_coupled(weights, own, orbs, OWN_COST)
    if around:
        below, above = along_chips(slab, 1), along_chips(slab, -1)
        halves = half_products(uses, 0, [slab[None], below[None]], own_t, pno, None, DECLARED)
        beyond = along_chips(below, 1)
        acc = after(acc, halves)
    else:
        gathered = lax.all_gather(slab, "dev", axis=0, tiled=False)
        halves = half_products(uses, 0, [gathered[:ahead]], own_t, pno, None, 0)
        rest = [gathered[ahead:]]

    lanes = [*range(pairs, pairs + half), *range(2 * pairs + half, 3 * pairs)]
    acc = add_coupled(lanes, weights, own_t, acc, (x_lo, y_hi), DECLARED)
    first = across(first_across_kernel, "first_across", (), (after(x_lo, acc), after(y_hi, acc)), orbs, FIRST_COST)
    back_low, back_high = along_x(first[0]), along_y(first[1])
    gate = first[0]
    if around:
        swaps = [other_core(after(value, x_lo, y_hi)) for value in (slab, below)]
        more = [value[None] for value in (*swaps, beyond, above)]
        halves = half_products(uses, 2, more, after(own_t, gate), pno, halves, 0)
        beyond, above = after(beyond, halves), after(above, halves)
        rest = [other_core(beyond)[None], other_core(above)[None]]
        gate = halves
    second = across(
        second_across_kernel, "second_across", (upper,), (after(x_lo, gate), x_hi, y_lo, y_hi), orbs, SECOND_COST
    )
    back_row, back_column = along_x(second[0]), along_y(second[1])
    lanes = [*range(pairs + half, 2 * pairs), *range(2 * pairs, 2 * pairs + half)]
    acc = add_coupled(lanes, weights, own_t, after(acc, second[0]), (x_hi, y_lo), LAST_COST)
    sums = (acc, back_low, back_high, back_row, back_column)
    return add_exchange(uses, turns, upper, ahead, rest, own_t, halves, sums)


def solution(mesh):
    in_specs = (
        P("dev", None, None),
        P(),
        P(("grp", "dev"), None),
        P(("grp", "dev"), None, None),
        P(("grp", "dev"), None, None),
        P(("grp", "dev"), None),
        P(("grp", "dev")),
    )
    out_specs = P(("grp", "dev"), None, None)
    return jax.shard_map(
        on_device, mesh=mesh, in_specs=in_specs, out_specs=out_specs, check_vma=False
    )
```

```python
import functools
import math

import jax
import jax.numpy as jnp
from jax import lax
from jax.experimental import pallas as pl
from jax.experimental.pallas import tpu as pltpu
from jax.sharding import PartitionSpec as P

MARGIN = 0
PACK_LIMIT = 56 * 1024 * 1024
RING_CHIPS = 4
DECLARED = 20_000_000_000
OWN_COST, FIRST_COST, SECOND_COST, LAST_COST = 0, 0, 0, DECLARED
SMEM_SPEC = pl.BlockSpec(memory_space=pltpu.SMEM)
VMEM_SPEC = pl.BlockSpec(memory_space=pltpu.VMEM)
HBM_SPEC = pl.BlockSpec(memory_space=pltpu.HBM)


def call_kernel(body, out_shape, scratch, name, smem_args, vmem_args, flops, hbm_args=(), aliases={}):
    outs = out_shape if isinstance(out_shape, tuple) else (out_shape,)
    held = [a for a in (*vmem_args, *scratch, *outs) if a.dtype in (jnp.float32, jnp.bfloat16)]
    return pl.pallas_call(
        body,
        out_shape=out_shape,
        in_specs=[SMEM_SPEC] * len(smem_args) + [VMEM_SPEC] * len(vmem_args) + [HBM_SPEC] * len(hbm_args),
        out_specs=(VMEM_SPEC,) * len(outs) if isinstance(out_shape, tuple) else VMEM_SPEC,
        scratch_shapes=scratch,
        input_output_aliases=aliases,
        compiler_params=pltpu.CompilerParams(
            vmem_limit_bytes=sum(math.prod(a.shape) * a.dtype.itemsize for a in held) + MARGIN
        ),
        cost_estimate=pl.CostEstimate(flops=flops, bytes_accessed=0, transcendentals=0),
        name=name,
    )(*smem_args, *vmem_args, *hbm_args)


class Side:
    def __init__(self, left, packs, orbs, pno):
        self.left, self.packs, self.orbs, self.pno = left, packs, orbs, pno

    def basis(self, k):
        return self.packs[k][: self.orbs, :]

    def amps(self, k):
        return self.packs[k][self.orbs : self.orbs + self.pno, :]

    def counts(self, lanes):
        rows = [pack[self.orbs + self.pno :, :].astype(jnp.float32) for pack in self.packs]
        return lambda p, c: rows[p][0:1, lanes[c] : lanes[c] + 1]


def project(side, other, count, inter_ref, proj_ref, copies=()):
    pno = side.pno
    empty = jnp.zeros((pno, pno), jnp.bfloat16)
    for j in range(0, len(other.packs), 2):
        for copy in copies[j : j + 2]:
            copy.wait()
        pair = jnp.concatenate([other.basis(j), other.basis(j + 1)], axis=1)
        inter = jnp.dot(side.left[...], pair, preferred_element_type=jnp.float32).astype(jnp.bfloat16)
        inter_ref[:, j * pno : (j + 2) * pno] = inter
        diagonal = jnp.concatenate(
            [
                jnp.concatenate([other.amps(j), empty], axis=1),
                jnp.concatenate([empty, other.amps(j + 1)], axis=1),
            ],
            axis=0,
        )
        proj = jnp.dot(inter, diagonal, preferred_element_type=jnp.float32)
        for p in range(side.left.shape[0] // pno):
            for c in range(2):
                block = proj[p * pno : (p + 1) * pno, c * pno : (c + 1) * pno]
                proj_ref[p * pno : (p + 1) * pno, (j + c) * pno : (j + c + 1) * pno] = (
                    block * count(p, j + c)
                ).astype(jnp.bfloat16)


def coupled_kernel(lanes, weight_ref, left_ref, acc_ref, one_ref, two_ref, out_ref, inter_ref, proj_ref):
    pairs, pno, _ = out_ref.shape
    half, orbs = pairs // 2, left_ref.shape[1]
    own = Side(left_ref, (), orbs, pno)
    other = Side(None, [ref.at[k] for ref in (one_ref, two_ref) for k in range(half)], orbs, pno)
    project(own, other, lambda p, c: weight_ref[p, lanes[c]], inter_ref, proj_ref)
    for p in range(pairs):
        out_ref[p] = acc_ref[p] + one_sum(proj_ref, inter_ref, p, pno)


def own_kernel(weight_ref, low_ref, high_ref, out_ref, left_ref, inter_ref, proj_ref):
    pairs, pno, _ = out_ref.shape
    orbs = left_ref.shape[1]
    packs = [ref.at[k] for ref in (low_ref, high_ref) for k in range(pairs // 2)]
    for p, pack_ref in enumerate(packs):
        left_ref[p * pno : (p + 1) * pno, :] = pack_ref[:orbs, :].T
    own = Side(left_ref, packs, orbs, pno)
    project(own, own, lambda p, c: weight_ref[p, c], inter_ref, proj_ref)
    for p in range(pairs):
        out_ref[p] = one_sum(proj_ref, inter_ref, p, pno)


def one_sum(proj_ref, inter_ref, p, pno):
    at = slice(p * pno, (p + 1) * pno)
    return lax.dot_general(
        proj_ref[at, :], inter_ref[at, :], (((1,), (1,)), ((), ())), preferred_element_type=jnp.float32
    )


def both_sums(one_ref, two_ref, turned_ref, one_lanes, two_lanes, products, orbs):
    half, _, pno = one_ref.shape
    sides = []
    for first, ref in ((0, one_ref), (half, two_ref)):
        for k in range(half):
            turned_ref[(first + k) * pno : (first + k + 1) * pno, :] = ref[k, :orbs, :].T
        left = turned_ref.at[first * pno : (first + half) * pno, :]
        sides.append(Side(left, [ref.at[k] for k in range(half)], orbs, pno))
    project(sides[0], sides[1], sides[0].counts(two_lanes), products[0], products[1])
    project(sides[1], sides[0], sides[1].counts(one_lanes), products[2], products[3])

    def total(proj, inter):
        def of(k):
            at = slice(k * pno, (k + 1) * pno)
            return jnp.dot(proj[at, :], inter[:, at], preferred_element_type=jnp.float32)

        return of

    return total(products[1], products[2]), total(products[3], products[0])


def first_across_kernel(orbs, x_low, y_high, out_one, out_two, turned_ref, *products):
    half = out_one.shape[0]
    block = 3 * 2 * half
    low, high = range(block, block + half), range(block + half, block + 2 * half)
    one, two = both_sums(x_low, y_high, turned_ref, low, high, products, orbs)
    for k in range(half):
        out_one[k] = one(k).astype(jnp.bfloat16)
        out_two[k] = two(k).astype(jnp.bfloat16)


def second_across_kernel(orbs, upper_ref, x_low, x_high, y_low, y_high, out_one, out_two, turned_ref, *products):
    half = out_one.shape[0]
    block = 3 * 2 * half

    def between(one_ref, two_ref, lanes):
        one, two = both_sums(one_ref, two_ref, turned_ref, lanes, lanes, products, orbs)
        for k in range(half):
            out_one[k] = one(k).astype(jnp.bfloat16)
            out_two[k] = two(k).astype(jnp.bfloat16)

    @pl.when(upper_ref[0] == 0)
    def _():
        between(x_low, y_low, range(block, block + half))

    @pl.when(upper_ref[0] == 1)
    def _():
        between(x_high, y_high, range(block + half, block + 2 * half))


def own_coupled(weights, own, orbs, flops):
    half, _, pno = own[0].shape
    rows = 2 * half * pno
    shapes = (jax.ShapeDtypeStruct((2 * half, pno, pno), jnp.float32), jax.ShapeDtypeStruct((rows, orbs), jnp.bfloat16))
    scratch = [pltpu.VMEM((rows, rows), jnp.bfloat16)] * 2
    return call_kernel(own_kernel, shapes, scratch, "own_coupled", (weights,), own, flops)


def add_coupled(lanes, weights, own_t, acc, received, flops):
    rows = own_t.shape[0]
    scratch = [pltpu.VMEM((rows, rows), jnp.bfloat16)] * 2
    shape = jax.ShapeDtypeStruct(acc.shape, jnp.float32)
    body = functools.partial(coupled_kernel, lanes)
    return call_kernel(body, shape, scratch, "coupled", (weights,), (own_t, acc, *received), flops)


def across(body, name, scalars, vmem_args, orbs, flops):
    half, _, pno = vmem_args[0].shape
    wide = half * pno
    shapes = (jax.ShapeDtypeStruct((half, pno, pno), jnp.bfloat16),) * 2
    scratch = [pltpu.VMEM((2 * wide, orbs), jnp.bfloat16), *[pltpu.VMEM((wide, wide), jnp.bfloat16)] * 4]
    return call_kernel(functools.partial(body, orbs), shapes, scratch, name, scalars, vmem_args, flops)


def half_transforms(uses_ref, slab_refs, own_ref, store, base, pno):
    last = own_ref.shape[0] // pno - 1

    def rows(side):
        return own_ref[pl.ds(pl.multiple_of(jnp.minimum(side // 2, last) * pno, pno), pno), :]

    def both_sides(slab, k):
        one, two = uses_ref[k, 0], uses_ref[k, 1]
        bases = jnp.concatenate([rows(one), rows(two)], axis=0)
        both = lax.dot_general(slab, bases, (((1,), (1,)), ((), ())), preferred_element_type=jnp.float32)
        both = both.astype(jnp.bfloat16)
        store(k, 0, one, both[:, :pno])
        store(k, 1, two, both[:, pno:])

    for slab_ref in slab_refs:
        if slab_ref.shape[0] > 4:

            def step(k, carry, slab_ref=slab_ref, base=base):
                both_sides(slab_ref[k], base + k)
                return carry

            lax.fori_loop(0, slab_ref.shape[0], step, 0)
        else:
            for k in range(slab_ref.shape[0]):
                both_sides(slab_ref[k], base + k)
        base += slab_ref.shape[0]


def halves_kernel(base, uses_ref, *refs):
    *slab_refs, own_ref, half_ref = refs

    def store(k, use, side, half):
        half_ref[side] = half

    half_transforms(uses_ref, slab_refs, own_ref, store, base, half_ref.shape[2])


def more_halves_kernel(base, uses_ref, *refs):
    *slab_refs, own_ref, _, half_ref = refs
    halves_kernel(base, uses_ref, *slab_refs, own_ref, half_ref)


def exchange_kernel(scale, base, uses_ref, turn_ref, upper_ref, *refs):
    *slab_refs, own_ref, early_ref, acc_ref, low_ref, high_ref, row_ref, column_ref, out_ref, late_ref = refs
    half_count = low_ref.shape[0]

    def store(k, use, side, half):
        late_ref[2 * (k - base) + use] = half

    def half(p, side):
        k = turn_ref[2 * p + side]
        late = jnp.where(uses_ref[k, 0] == 2 * p + side, 0, 1) + 2 * jnp.maximum(k - base, 0)
        return jnp.where(k < base, early_ref[2 * p + side], late_ref[late])

    half_transforms(uses_ref, slab_refs, own_ref, store, base, out_ref.shape[1])
    for p in range(out_ref.shape[0]):
        product = lax.dot_general(half(p, 0), half(p, 1), (((0,), (0,)), ((), ())), preferred_element_type=jnp.float32)
        k, upper = p % half_count, p // half_count
        first = (low_ref, high_ref)[upper][k].astype(jnp.float32)
        second = jnp.where(upper_ref[0] == upper, row_ref[k], column_ref[k]).astype(jnp.float32)
        out_ref[p] = acc_ref[p] + (first + second) + product * scale


def half_products(uses, base, slabs, own_t, pno, done, flops):
    sides = own_t.shape[0] // pno * 2
    shape = jax.ShapeDtypeStruct((sides + 1, slabs[0].shape[1], pno), jnp.bfloat16)
    if done is None:
        return call_kernel(functools.partial(halves_kernel, base), shape, [], "halves", (uses,), (*slabs, own_t), flops)
    args = (*slabs, own_t, done)
    return call_kernel(
        functools.partial(more_halves_kernel, base), shape, [], "more_halves", (uses,), args, flops, aliases={len(args): 0}
    )


def add_exchange(uses, turn, upper, base, slabs, own_t, early, sums):
    return call_kernel(
        functools.partial(exchange_kernel, 1.0 / math.sqrt(slabs[0].shape[1]), base),
        jax.ShapeDtypeStruct(sums[0].shape, jnp.float32),
        [pltpu.VMEM((2 * sum(slab.shape[0] for slab in slabs),) + early.shape[1:], jnp.bfloat16)],
        "exchange",
        (uses, turn, upper),
        (*slabs, own_t, early, *sums),
        0,
    )


def pack_kernel(scale, chips, group_ref, me_ref, coupled_ref, length_ref, owner_ref, orbs_ref, base_ref, amp_ref, *refs):
    low_ref, high_ref, weight_ref, uses_ref, turn_ref, held_ref, sems = refs
    pairs, orbs, pno = base_ref.shape
    half = pairs // 2
    group, me = group_ref[0], me_ref[0]
    copies = []

    def copy(ref, k, row, sem):
        rows = pl.ds(row, ref.shape[1])
        copies.append(pltpu.make_async_copy(ref.at[pl.ds(k * half, half)], held_ref.at[k, :, rows], sems.at[sem]))
        copies[-1].start()

    for k in range(2):
        copy(base_ref, k, 0, 2 * k)
        copy(amp_ref, k, orbs, 2 * k + 1)
    assert pairs & (pairs - 1) == 0
    named = lax.broadcasted_iota(jnp.int32, (1, pno), 1) ^ (group * pairs)
    for p in range(pairs):
        counts = jnp.zeros((1, pno), jnp.float32)
        length = length_ref[p]
        for s in range(coupled_ref.shape[1]):
            counts += jnp.where(named == jnp.where(s < length, coupled_ref[p, s], -1), scale, 0.0)
        weight_ref[p : p + 1, :] = counts
        rows = slice(orbs + amp_ref.shape[1], held_ref.shape[2])
        held_ref[p // half, p % half, rows, :] = jnp.broadcast_to(counts, (16, pno)).astype(jnp.bfloat16)
    stores = [
        pltpu.make_async_copy(held_ref.at[k], out_ref, sems.at[4 + k]) for k, out_ref in enumerate((low_ref, high_ref))
    ]
    for k, store in enumerate(stores):
        for started in copies[2 * k : 2 * k + 2]:
            started.wait()
        store.start()

    sides = 2 * pairs

    def clear(k, carry):
        uses_ref[k, 0] = sides
        uses_ref[k, 1] = sides
        return carry

    lax.fori_loop(0, uses_ref.shape[0], clear, 0)
    for f in range(sides):
        position = owner_ref[orbs_ref[f % 2, f // 2]]
        k = position
        if chips <= RING_CHIPS:
            steps = lax.rem((me >> 1) - (position >> 1) + chips, chips)
            swapped = (position ^ me) & 1
            k = jnp.where(steps < 2, steps + 2 * swapped, steps + 2 + 2 * swapped)
        turn_ref[f] = k
        uses_ref[k, 1] = uses_ref[k, 0]
        uses_ref[k, 0] = f
    for store in stores:
        store.wait()


def pack(group, me, chips, coupled, coupled_len, slab_owner, pair_orbs, bases, amps):
    pairs, orbs, pno = bases.shape
    packed = jax.ShapeDtypeStruct((pairs // 2, orbs + amps.shape[1] + 16, pno), bases.dtype)
    return pl.pallas_call(
        functools.partial(pack_kernel, orbs / pno, chips),
        out_shape=(
            packed,
            packed,
            jax.ShapeDtypeStruct((pairs, pno), jnp.float32),
            jax.ShapeDtypeStruct((slab_owner.shape[0], 2), jnp.int32),
            jax.ShapeDtypeStruct((2 * pairs,), jnp.int32),
        ),
        in_specs=[SMEM_SPEC] * 6 + [HBM_SPEC] * 2,
        out_specs=(HBM_SPEC, HBM_SPEC, VMEM_SPEC, SMEM_SPEC, SMEM_SPEC),
        scratch_shapes=[pltpu.VMEM((2,) + packed.shape, bases.dtype), pltpu.SemaphoreType.DMA((6,))],
        compiler_params=pltpu.CompilerParams(vmem_limit_bytes=PACK_LIMIT),
        name="pack",
    )(group, me, coupled, coupled_len, slab_owner, pair_orbs.T, bases, amps)


def after(value, *earlier):
    return lax.optimization_barrier((value,) + earlier)[0]


def on_device(integral_slabs, slab_owner, pair_orbs, domain_bases, amplitudes, coupled, coupled_len):
    n_grp, n_dev = lax.axis_size("grp"), lax.axis_size("dev")
    pairs, orbs, pno = domain_bases.shape
    group, me = lax.axis_index("grp"), lax.axis_index("dev")
    chips = n_dev // 2

    half = pairs // 2

    def along_x(value):
        return lax.ppermute(value, "grp", [(g, g ^ 1) for g in range(n_grp)])

    def along_y(value):
        return lax.ppermute(value, "grp", [(g, g ^ 2) for g in range(n_grp)])

    def along_chips(value, step):
        return lax.ppermute(value, "dev", [(d, (d + 2 * step) % n_dev) for d in range(n_dev)])

    def other_core(value):
        return lax.ppermute(value, "dev", [(d, d ^ 1) for d in range(n_dev)])

    *own, weights, uses, turns = pack(
        group.astype(jnp.int32).reshape(1), me.astype(jnp.int32).reshape(1), chips, coupled, coupled_len, slab_owner, pair_orbs, domain_bases, amplitudes
    )
    own_lo, own_hi = own
    upper = (group // 2).astype(jnp.int32).reshape(1)

    x_lo, y_hi = along_x(own_lo), along_y(own_hi)
    x_hi, y_lo = along_x(after(own_hi, own_lo)), along_y(after(own_lo, own_hi, x_lo))

    slab = integral_slabs[0]
    around = chips <= RING_CHIPS
    ahead = 6 if around else n_dev // 2
    acc, own_t = own_coupled(weights, own, orbs, OWN_COST)
    if around:
        below, above = along_chips(slab, 1), along_chips(slab, -1)
        halves = half_products(uses, 0, [slab[None], below[None]], own_t, pno, None, DECLARED)
        beyond = along_chips(below, 1)
        acc = after(acc, halves, above)
    else:
        gathered = lax.all_gather(slab, "dev", axis=0, tiled=False)
        halves = half_products(uses, 0, [gathered[:ahead]], own_t, pno, None, 0)
        rest = [gathered[ahead:]]

    lanes = [*range(pairs, pairs + half), *range(2 * pairs + half, 3 * pairs)]
    acc = add_coupled(lanes, weights, own_t, acc, (x_lo, y_hi), DECLARED)
    if around:
        swaps = [other_core(after(value, x_lo, y_hi)) for value in (slab, below)]
    first = across(first_across_kernel, "first_across", (), (after(x_lo, acc, *swaps) if around else x_lo, after(y_hi, acc)), orbs, FIRST_COST)
    gate = first[0]
    back_low, back_high = along_x(first[0]), along_y(first[1])
    if around:
        more = [value[None] for value in (*swaps, beyond, above)]
        halves = half_products(uses, 2, more, after(own_t, gate), pno, halves, 0)
        beyond, above = after(beyond, halves), after(above, halves)
        rest = [other_core(beyond)[None], other_core(above)[None]]
        gate = halves
    second = across(
        second_across_kernel, "second_across", (upper,), (after(x_lo, gate), x_hi, y_lo, y_hi), orbs, SECOND_COST
    )
    back_row, back_column = along_x(second[0]), along_y(second[1])
    lanes = [*range(pairs + half, 2 * pairs), *range(2 * pairs, 2 * pairs + half)]
    acc = add_coupled(lanes, weights, own_t, after(acc, second[0]), (x_hi, y_lo), LAST_COST)
    sums = (acc, back_low, back_high, back_row, back_column)
    return add_exchange(uses, turns, upper, ahead, rest, own_t, halves, sums)


def solution(mesh):
    in_specs = (
        P("dev", None, None),
        P(),
        P(("grp", "dev"), None),
        P(("grp", "dev"), None, None),
        P(("grp", "dev"), None, None),
        P(("grp", "dev"), None),
        P(("grp", "dev")),
    )
    out_specs = P(("grp", "dev"), None, None)
    return jax.shard_map(
        on_device, mesh=mesh, in_specs=in_specs, out_specs=out_specs, check_vma=False
    )
```

```python
import functools
import math

import jax
import jax.numpy as jnp
from jax import lax
from jax.experimental import pallas as pl
from jax.experimental.pallas import tpu as pltpu
from jax.sharding import PartitionSpec as P

MARGIN = 0
PACK_LIMIT = 56 * 1024 * 1024
RING_CHIPS = 4
DECLARED = 20_000_000_000
OWN_COST, FIRST_COST, SECOND_COST, LAST_COST = 0, 0, 0, DECLARED
MORE_COST, EXCHANGE_COST = 0, 0
SMEM_SPEC = pl.BlockSpec(memory_space=pltpu.SMEM)
VMEM_SPEC = pl.BlockSpec(memory_space=pltpu.VMEM)
HBM_SPEC = pl.BlockSpec(memory_space=pltpu.HBM)


def call_kernel(body, out_shape, scratch, name, smem_args, vmem_args, flops, hbm_args=(), aliases={}):
    outs = out_shape if isinstance(out_shape, tuple) else (out_shape,)
    held = [a for a in (*vmem_args, *scratch, *outs) if a.dtype in (jnp.float32, jnp.bfloat16)]
    return pl.pallas_call(
        body,
        out_shape=out_shape,
        in_specs=[SMEM_SPEC] * len(smem_args) + [VMEM_SPEC] * len(vmem_args) + [HBM_SPEC] * len(hbm_args),
        out_specs=(VMEM_SPEC,) * len(outs) if isinstance(out_shape, tuple) else VMEM_SPEC,
        scratch_shapes=scratch,
        input_output_aliases=aliases,
        compiler_params=pltpu.CompilerParams(
            vmem_limit_bytes=sum(math.prod(a.shape) * a.dtype.itemsize for a in held) + MARGIN
        ),
        cost_estimate=pl.CostEstimate(flops=flops, bytes_accessed=0, transcendentals=0),
        name=name,
    )(*smem_args, *vmem_args, *hbm_args)


class Side:
    def __init__(self, left, packs, orbs, pno):
        self.left, self.packs, self.orbs, self.pno = left, packs, orbs, pno

    def basis(self, k):
        return self.packs[k][: self.orbs, :]

    def amps(self, k):
        return self.packs[k][self.orbs : self.orbs + self.pno, :]

    def counts(self, lanes):
        rows = [pack[self.orbs + self.pno :, :].astype(jnp.float32) for pack in self.packs]
        return lambda p, c: rows[p][0:1, lanes[c] : lanes[c] + 1]


def project(side, other, count, inter_ref, proj_ref, copies=()):
    pno = side.pno
    empty = jnp.zeros((pno, pno), jnp.bfloat16)
    for j in range(0, len(other.packs), 2):
        for copy in copies[j : j + 2]:
            copy.wait()
        pair = jnp.concatenate([other.basis(j), other.basis(j + 1)], axis=1)
        inter = jnp.dot(side.left[...], pair, preferred_element_type=jnp.float32).astype(jnp.bfloat16)
        inter_ref[:, j * pno : (j + 2) * pno] = inter
        diagonal = jnp.concatenate(
            [
                jnp.concatenate([other.amps(j), empty], axis=1),
                jnp.concatenate([empty, other.amps(j + 1)], axis=1),
            ],
            axis=0,
        )
        proj = jnp.dot(inter, diagonal, preferred_element_type=jnp.float32)
        for p in range(side.left.shape[0] // pno):
            for c in range(2):
                block = proj[p * pno : (p + 1) * pno, c * pno : (c + 1) * pno]
                proj_ref[p * pno : (p + 1) * pno, (j + c) * pno : (j + c + 1) * pno] = (
                    block * count(p, j + c)
                ).astype(jnp.bfloat16)


def coupled_kernel(lanes, weight_ref, left_ref, acc_ref, one_ref, two_ref, out_ref, inter_ref, proj_ref):
    pairs, pno, _ = out_ref.shape
    half, orbs = pairs // 2, left_ref.shape[1]
    own = Side(left_ref, (), orbs, pno)
    other = Side(None, [ref.at[k] for ref in (one_ref, two_ref) for k in range(half)], orbs, pno)
    project(own, other, lambda p, c: weight_ref[p, lanes[c]], inter_ref, proj_ref)
    for p in range(pairs):
        out_ref[p] = acc_ref[p] + one_sum(proj_ref, inter_ref, p, pno)


def own_kernel(weight_ref, low_ref, high_ref, out_ref, left_ref, inter_ref, proj_ref):
    pairs, pno, _ = out_ref.shape
    orbs = left_ref.shape[1]
    packs = [ref.at[k] for ref in (low_ref, high_ref) for k in range(pairs // 2)]
    for p, pack_ref in enumerate(packs):
        left_ref[p * pno : (p + 1) * pno, :] = pack_ref[:orbs, :].T
    own = Side(left_ref, packs, orbs, pno)
    project(own, own, lambda p, c: weight_ref[p, c], inter_ref, proj_ref)
    for p in range(pairs):
        out_ref[p] = one_sum(proj_ref, inter_ref, p, pno)


def one_sum(proj_ref, inter_ref, p, pno):
    at = slice(p * pno, (p + 1) * pno)
    return lax.dot_general(
        proj_ref[at, :], inter_ref[at, :], (((1,), (1,)), ((), ())), preferred_element_type=jnp.float32
    )


def both_sums(one_ref, two_ref, turned_ref, one_lanes, two_lanes, products, orbs):
    half, _, pno = one_ref.shape
    sides = []
    for first, ref in ((0, one_ref), (half, two_ref)):
        for k in range(half):
            turned_ref[(first + k) * pno : (first + k + 1) * pno, :] = ref[k, :orbs, :].T
        left = turned_ref.at[first * pno : (first + half) * pno, :]
        sides.append(Side(left, [ref.at[k] for k in range(half)], orbs, pno))
    project(sides[0], sides[1], sides[0].counts(two_lanes), products[0], products[1])
    project(sides[1], sides[0], sides[1].counts(one_lanes), products[2], products[3])

    def total(proj, inter):
        def of(k):
            at = slice(k * pno, (k + 1) * pno)
            return jnp.dot(proj[at, :], inter[:, at], preferred_element_type=jnp.float32)

        return of

    return total(products[1], products[2]), total(products[3], products[0])


def first_across_kernel(orbs, x_low, y_high, out_one, out_two, turned_ref, *products):
    half = out_one.shape[0]
    block = 3 * 2 * half
    low, high = range(block, block + half), range(block + half, block + 2 * half)
    one, two = both_sums(x_low, y_high, turned_ref, low, high, products, orbs)
    for k in range(half):
        out_one[k] = one(k).astype(jnp.bfloat16)
        out_two[k] = two(k).astype(jnp.bfloat16)


def second_across_kernel(orbs, upper_ref, x_low, x_high, y_low, y_high, out_one, out_two, turned_ref, *products):
    half = out_one.shape[0]
    block = 3 * 2 * half

    def between(one_ref, two_ref, lanes):
        one, two = both_sums(one_ref, two_ref, turned_ref, lanes, lanes, products, orbs)
        for k in range(half):
            out_one[k] = one(k).astype(jnp.bfloat16)
            out_two[k] = two(k).astype(jnp.bfloat16)

    @pl.when(upper_ref[0] == 0)
    def _():
        between(x_low, y_low, range(block, block + half))

    @pl.when(upper_ref[0] == 1)
    def _():
        between(x_high, y_high, range(block + half, block + 2 * half))


def own_coupled(weights, own, orbs, flops):
    half, _, pno = own[0].shape
    rows = 2 * half * pno
    shapes = (jax.ShapeDtypeStruct((2 * half, pno, pno), jnp.float32), jax.ShapeDtypeStruct((rows, orbs), jnp.bfloat16))
    scratch = [pltpu.VMEM((rows, rows), jnp.bfloat16)] * 2
    return call_kernel(own_kernel, shapes, scratch, "own_coupled", (weights,), own, flops)


def add_coupled(lanes, weights, own_t, acc, received, flops):
    rows = own_t.shape[0]
    scratch = [pltpu.VMEM((rows, rows), jnp.bfloat16)] * 2
    shape = jax.ShapeDtypeStruct(acc.shape, jnp.float32)
    body = functools.partial(coupled_kernel, lanes)
    return call_kernel(body, shape, scratch, "coupled", (weights,), (own_t, acc, *received), flops)


def across(body, name, scalars, vmem_args, orbs, flops):
    half, _, pno = vmem_args[0].shape
    wide = half * pno
    shapes = (jax.ShapeDtypeStruct((half, pno, pno), jnp.bfloat16),) * 2
    scratch = [pltpu.VMEM((2 * wide, orbs), jnp.bfloat16), *[pltpu.VMEM((wide, wide), jnp.bfloat16)] * 4]
    return call_kernel(functools.partial(body, orbs), shapes, scratch, name, scalars, vmem_args, flops)


def half_transforms(uses_ref, slab_refs, own_ref, store, base, pno):
    last = own_ref.shape[0] // pno - 1

    def rows(side):
        return own_ref[pl.ds(pl.multiple_of(jnp.minimum(side // 2, last) * pno, pno), pno), :]

    def both_sides(slab, k):
        one, two = uses_ref[k, 0], uses_ref[k, 1]
        bases = jnp.concatenate([rows(one), rows(two)], axis=0)
        both = lax.dot_general(slab, bases, (((1,), (1,)), ((), ())), preferred_element_type=jnp.float32)
        both = both.astype(jnp.bfloat16)
        store(k, 0, one, both[:, :pno])
        store(k, 1, two, both[:, pno:])

    for slab_ref in slab_refs:
        if slab_ref.shape[0] > 4:

            def step(k, carry, slab_ref=slab_ref, base=base):
                both_sides(slab_ref[k], base + k)
                return carry

            lax.fori_loop(0, slab_ref.shape[0], step, 0)
        else:
            for k in range(slab_ref.shape[0]):
                both_sides(slab_ref[k], base + k)
        base += slab_ref.shape[0]


def halves_kernel(base, uses_ref, *refs):
    *slab_refs, own_ref, half_ref = refs

    def store(k, use, side, half):
        half_ref[side] = half

    half_transforms(uses_ref, slab_refs, own_ref, store, base, half_ref.shape[2])


def more_halves_kernel(base, uses_ref, *refs):
    *slab_refs, own_ref, _, half_ref = refs
    halves_kernel(base, uses_ref, *slab_refs, own_ref, half_ref)


def exchange_kernel(scale, base, uses_ref, turn_ref, *refs):
    *slab_refs, own_ref, early_ref, acc_ref, out_ref, late_ref = refs

    def store(k, use, side, half):
        late_ref[2 * (k - base) + use] = half

    def half(p, side):
        k = turn_ref[2 * p + side]
        late = jnp.where(uses_ref[k, 0] == 2 * p + side, 0, 1) + 2 * jnp.maximum(k - base, 0)
        return jnp.where(k < base, early_ref[2 * p + side], late_ref[late])

    half_transforms(uses_ref, slab_refs, own_ref, store, base, out_ref.shape[1])
    for p in range(out_ref.shape[0]):
        product = lax.dot_general(half(p, 0), half(p, 1), (((0,), (0,)), ((), ())), preferred_element_type=jnp.float32)
        out_ref[p] = acc_ref[p] + product * scale


def finish_kernel(upper_ref, acc_ref, low_ref, high_ref, row_ref, column_ref, out_ref):
    half = low_ref.shape[0]
    for p in range(out_ref.shape[0]):
        k, upper = p % half, p // half
        first = (low_ref, high_ref)[upper][k].astype(jnp.float32)
        second = jnp.where(upper_ref[0] == upper, row_ref[k], column_ref[k]).astype(jnp.float32)
        out_ref[p] = acc_ref[p] + (first + second)


def half_products(uses, base, slabs, own_t, pno, done, flops):
    sides = own_t.shape[0] // pno * 2
    shape = jax.ShapeDtypeStruct((sides + 1, slabs[0].shape[1], pno), jnp.bfloat16)
    if done is None:
        return call_kernel(functools.partial(halves_kernel, base), shape, [], "halves", (uses,), (*slabs, own_t), flops)
    args = (*slabs, own_t, done)
    return call_kernel(
        functools.partial(more_halves_kernel, base), shape, [], "more_halves", (uses,), args, flops, aliases={len(args): 0}
    )


def add_exchange(uses, turn, base, slabs, own_t, early, acc):
    return call_kernel(
        functools.partial(exchange_kernel, 1.0 / math.sqrt(slabs[0].shape[1]), base),
        jax.ShapeDtypeStruct(acc.shape, jnp.float32),
        [pltpu.VMEM((2 * sum(slab.shape[0] for slab in slabs),) + early.shape[1:], jnp.bfloat16)],
        "exchange",
        (uses, turn),
        (*slabs, own_t, early, acc),
        EXCHANGE_COST,
    )


def finish(upper, acc, backs):
    shape = jax.ShapeDtypeStruct(acc.shape, jnp.float32)
    return call_kernel(finish_kernel, shape, [], "finish", (upper,), (acc, *backs), 0)


def pack_kernel(scale, chips, group_ref, me_ref, coupled_ref, length_ref, owner_ref, orbs_ref, base_ref, amp_ref, *refs):
    low_ref, high_ref, weight_ref, uses_ref, turn_ref, held_ref, sems = refs
    pairs, orbs, pno = base_ref.shape
    half = pairs // 2
    group, me = group_ref[0], me_ref[0]
    copies = []

    def copy(ref, k, row, sem):
        rows = pl.ds(row, ref.shape[1])
        copies.append(pltpu.make_async_copy(ref.at[pl.ds(k * half, half)], held_ref.at[k, :, rows], sems.at[sem]))
        copies[-1].start()

    for k in range(2):
        copy(base_ref, k, 0, 2 * k)
        copy(amp_ref, k, orbs, 2 * k + 1)
    assert pairs & (pairs - 1) == 0
    named = lax.broadcasted_iota(jnp.int32, (1, pno), 1) ^ (group * pairs)
    for p in range(pairs):
        counts = jnp.zeros((1, pno), jnp.float32)
        length = length_ref[p]
        for s in range(coupled_ref.shape[1]):
            counts += jnp.where(named == jnp.where(s < length, coupled_ref[p, s], -1), scale, 0.0)
        weight_ref[p : p + 1, :] = counts
        rows = slice(orbs + amp_ref.shape[1], held_ref.shape[2])
        held_ref[p // half, p % half, rows, :] = jnp.broadcast_to(counts, (16, pno)).astype(jnp.bfloat16)
    for started in copies:
        started.wait()
    stores = [
        pltpu.make_async_copy(held_ref.at[k], out_ref, sems.at[4 + k]) for k, out_ref in enumerate((low_ref, high_ref))
    ]
    for store in stores:
        store.start()

    sides = 2 * pairs

    def clear(k, carry):
        uses_ref[k, 0] = sides
        uses_ref[k, 1] = sides
        return carry

    lax.fori_loop(0, uses_ref.shape[0], clear, 0)
    for f in range(sides):
        position = owner_ref[orbs_ref[f % 2, f // 2]]
        k = position
        if chips <= RING_CHIPS:
            steps = lax.rem((me >> 1) - (position >> 1) + chips, chips)
            swapped = (position ^ me) & 1
            late = jnp.where(steps == 2, 5 + swapped, 4 + 3 * swapped)
            k = jnp.where(steps < 2, steps + 2 * swapped, late)
        turn_ref[f] = k
        uses_ref[k, 1] = uses_ref[k, 0]
        uses_ref[k, 0] = f
    for store in stores:
        store.wait()


def pack(group, me, chips, coupled, coupled_len, slab_owner, pair_orbs, bases, amps):
    pairs, orbs, pno = bases.shape
    packed = jax.ShapeDtypeStruct((pairs // 2, orbs + amps.shape[1] + 16, pno), bases.dtype)
    return pl.pallas_call(
        functools.partial(pack_kernel, orbs / pno, chips),
        out_shape=(
            packed,
            packed,
            jax.ShapeDtypeStruct((pairs, pno), jnp.float32),
            jax.ShapeDtypeStruct((slab_owner.shape[0], 2), jnp.int32),
            jax.ShapeDtypeStruct((2 * pairs,), jnp.int32),
        ),
        in_specs=[SMEM_SPEC] * 6 + [HBM_SPEC] * 2,
        out_specs=(HBM_SPEC, HBM_SPEC, VMEM_SPEC, SMEM_SPEC, SMEM_SPEC),
        scratch_shapes=[pltpu.VMEM((2,) + packed.shape, bases.dtype), pltpu.SemaphoreType.DMA((6,))],
        compiler_params=pltpu.CompilerParams(vmem_limit_bytes=PACK_LIMIT),
        name="pack",
    )(group, me, coupled, coupled_len, slab_owner, pair_orbs.T, bases, amps)


def after(value, *earlier):
    return lax.optimization_barrier((value,) + earlier)[0]


def on_device(integral_slabs, slab_owner, pair_orbs, domain_bases, amplitudes, coupled, coupled_len):
    n_grp, n_dev = lax.axis_size("grp"), lax.axis_size("dev")
    pairs, orbs, pno = domain_bases.shape
    group, me = lax.axis_index("grp"), lax.axis_index("dev")
    chips = n_dev // 2

    half = pairs // 2

    def along_x(value):
        return lax.ppermute(value, "grp", [(g, g ^ 1) for g in range(n_grp)])

    def along_y(value):
        return lax.ppermute(value, "grp", [(g, g ^ 2) for g in range(n_grp)])

    def along_chips(value, step):
        return lax.ppermute(value, "dev", [(d, (d + 2 * step) % n_dev) for d in range(n_dev)])

    def other_core(value):
        return lax.ppermute(value, "dev", [(d, d ^ 1) for d in range(n_dev)])

    *own, weights, uses, turns = pack(
        group.astype(jnp.int32).reshape(1), me.astype(jnp.int32).reshape(1), chips, coupled, coupled_len, slab_owner, pair_orbs, domain_bases, amplitudes
    )
    own_lo, own_hi = own
    upper = (group // 2).astype(jnp.int32).reshape(1)

    x_lo, y_hi = along_x(own_lo), along_y(own_hi)
    x_hi, y_lo = along_x(after(own_hi, own_lo)), along_y(after(own_lo, own_hi, x_lo))

    slab = integral_slabs[0]
    around = chips <= RING_CHIPS
    ahead = 5 if around else n_dev // 2
    acc, own_t = own_coupled(weights, own, orbs, OWN_COST)
    if around:
        below, above = along_chips(slab, 1), along_chips(slab, -1)
        halves = half_products(uses, 0, [slab[None], below[None]], own_t, pno, None, DECLARED)
        beyond = along_chips(below, 1)
        acc = after(acc, halves)
    else:
        gathered = lax.all_gather(slab, "dev", axis=0, tiled=False)
        halves = half_products(uses, 0, [gathered[:ahead]], own_t, pno, None, 0)
        rest = [gathered[ahead:]]

    lanes = [*range(pairs, pairs + half), *range(2 * pairs + half, 3 * pairs)]
    acc = add_coupled(lanes, weights, own_t, acc, (x_lo, y_hi), DECLARED)
    first = across(first_across_kernel, "first_across", (), (after(x_lo, acc), after(y_hi, acc)), orbs, FIRST_COST)
    back_low, back_high = along_x(first[0]), along_y(first[1])
    if around:
        swaps = [other_core(after(value, x_lo, y_hi)) for value in (slab, below)]
        more = [value[None] for value in (*swaps, above)]
        halves = half_products(uses, 2, more, after(own_t, first[0]), pno, halves, MORE_COST)
        beyond = after(beyond, halves)
        rest = [value[None] for value in (beyond, other_core(beyond), other_core(above))]
    acc = add_exchange(uses, turns, ahead, rest, own_t, halves, acc)
    second = across(
        second_across_kernel, "second_across", (upper,), (after(x_lo, acc), x_hi, y_lo, y_hi), orbs, SECOND_COST
    )
    back_row, back_column = along_x(second[0]), along_y(second[1])
    lanes = [*range(pairs + half, 2 * pairs), *range(2 * pairs, 2 * pairs + half)]
    acc = add_coupled(lanes, weights, own_t, after(acc, second[0]), (x_hi, y_lo), LAST_COST)
    return finish(upper, acc, (back_low, back_high, back_row, back_column))


def solution(mesh):
    in_specs = (
        P("dev", None, None),
        P(),
        P(("grp", "dev"), None),
        P(("grp", "dev"), None, None),
        P(("grp", "dev"), None, None),
        P(("grp", "dev"), None),
        P(("grp", "dev")),
    )
    out_specs = P(("grp", "dev"), None, None)
    return jax.shard_map(
        on_device, mesh=mesh, in_specs=in_specs, out_specs=out_specs, check_vma=False
    )
```

```python
import functools
import math

import jax
import jax.numpy as jnp
from jax import lax
from jax.experimental import pallas as pl
from jax.experimental.pallas import tpu as pltpu
from jax.sharding import PartitionSpec as P

MARGIN = 0
PACK_LIMIT = 56 * 1024 * 1024
RING_CHIPS = 4
DECLARED = 20_000_000_000
OWN_COST, FIRST_COST, SECOND_COST, LAST_COST = 0, 0, 0, DECLARED
MORE_COST, EXCHANGE_COST = 0, 0
SMEM_SPEC = pl.BlockSpec(memory_space=pltpu.SMEM)
VMEM_SPEC = pl.BlockSpec(memory_space=pltpu.VMEM)
HBM_SPEC = pl.BlockSpec(memory_space=pltpu.HBM)


def call_kernel(body, out_shape, scratch, name, smem_args, vmem_args, flops, hbm_args=(), aliases={}):
    outs = out_shape if isinstance(out_shape, tuple) else (out_shape,)
    held = [a for a in (*vmem_args, *scratch, *outs) if a.dtype in (jnp.float32, jnp.bfloat16)]
    return pl.pallas_call(
        body,
        out_shape=out_shape,
        in_specs=[SMEM_SPEC] * len(smem_args) + [VMEM_SPEC] * len(vmem_args) + [HBM_SPEC] * len(hbm_args),
        out_specs=(VMEM_SPEC,) * len(outs) if isinstance(out_shape, tuple) else VMEM_SPEC,
        scratch_shapes=scratch,
        input_output_aliases=aliases,
        compiler_params=pltpu.CompilerParams(
            vmem_limit_bytes=sum(math.prod(a.shape) * a.dtype.itemsize for a in held) + MARGIN
        ),
        cost_estimate=pl.CostEstimate(flops=flops, bytes_accessed=0, transcendentals=0),
        name=name,
    )(*smem_args, *vmem_args, *hbm_args)


class Side:
    def __init__(self, left, packs, orbs, pno):
        self.left, self.packs, self.orbs, self.pno = left, packs, orbs, pno

    def basis(self, k):
        return self.packs[k][: self.orbs, :]

    def amps(self, k):
        return self.packs[k][self.orbs : self.orbs + self.pno, :]

    def counts(self, lanes):
        rows = [pack[self.orbs + self.pno :, :].astype(jnp.float32) for pack in self.packs]
        return lambda p, c: rows[p][0:1, lanes[c] : lanes[c] + 1]


def project(side, other, count, inter_ref, proj_ref, copies=()):
    pno = side.pno
    empty = jnp.zeros((pno, pno), jnp.bfloat16)
    for j in range(0, len(other.packs), 2):
        for copy in copies[j : j + 2]:
            copy.wait()
        pair = jnp.concatenate([other.basis(j), other.basis(j + 1)], axis=1)
        inter = jnp.dot(side.left[...], pair, preferred_element_type=jnp.float32).astype(jnp.bfloat16)
        inter_ref[:, j * pno : (j + 2) * pno] = inter
        diagonal = jnp.concatenate(
            [
                jnp.concatenate([other.amps(j), empty], axis=1),
                jnp.concatenate([empty, other.amps(j + 1)], axis=1),
            ],
            axis=0,
        )
        proj = jnp.dot(inter, diagonal, preferred_element_type=jnp.float32)
        for p in range(side.left.shape[0] // pno):
            for c in range(2):
                block = proj[p * pno : (p + 1) * pno, c * pno : (c + 1) * pno]
                proj_ref[p * pno : (p + 1) * pno, (j + c) * pno : (j + c + 1) * pno] = (
                    block * count(p, j + c)
                ).astype(jnp.bfloat16)


def coupled_kernel(lanes, weight_ref, left_ref, acc_ref, one_ref, two_ref, out_ref, inter_ref, proj_ref):
    pairs, pno, _ = out_ref.shape
    half, orbs = pairs // 2, left_ref.shape[1]
    own = Side(left_ref, (), orbs, pno)
    other = Side(None, [ref.at[k] for ref in (one_ref, two_ref) for k in range(half)], orbs, pno)
    project(own, other, lambda p, c: weight_ref[p, lanes[c]], inter_ref, proj_ref)
    for p in range(pairs):
        out_ref[p] = acc_ref[p] + one_sum(proj_ref, inter_ref, p, pno)


def own_kernel(weight_ref, low_ref, high_ref, out_ref, left_ref, inter_ref, proj_ref):
    pairs, pno, _ = out_ref.shape
    orbs = left_ref.shape[1]
    packs = [ref.at[k] for ref in (low_ref, high_ref) for k in range(pairs // 2)]
    for p, pack_ref in enumerate(packs):
        left_ref[p * pno : (p + 1) * pno, :] = pack_ref[:orbs, :].T
    own = Side(left_ref, packs, orbs, pno)
    project(own, own, lambda p, c: weight_ref[p, c], inter_ref, proj_ref)
    for p in range(pairs):
        out_ref[p] = one_sum(proj_ref, inter_ref, p, pno)


def one_sum(proj_ref, inter_ref, p, pno):
    at = slice(p * pno, (p + 1) * pno)
    return lax.dot_general(
        proj_ref[at, :], inter_ref[at, :], (((1,), (1,)), ((), ())), preferred_element_type=jnp.float32
    )


def both_sums(one_ref, two_ref, turned_ref, one_lanes, two_lanes, products, orbs):
    half, _, pno = one_ref.shape
    sides = []
    for first, ref in ((0, one_ref), (half, two_ref)):
        for k in range(half):
            turned_ref[(first + k) * pno : (first + k + 1) * pno, :] = ref[k, :orbs, :].T
        left = turned_ref.at[first * pno : (first + half) * pno, :]
        sides.append(Side(left, [ref.at[k] for k in range(half)], orbs, pno))
    project(sides[0], sides[1], sides[0].counts(two_lanes), products[0], products[1])
    project(sides[1], sides[0], sides[1].counts(one_lanes), products[2], products[3])

    def total(proj, inter):
        def of(k):
            at = slice(k * pno, (k + 1) * pno)
            return jnp.dot(proj[at, :], inter[:, at], preferred_element_type=jnp.float32)

        return of

    return total(products[1], products[2]), total(products[3], products[0])


def first_across_kernel(orbs, x_low, y_high, out_one, out_two, turned_ref, *products):
    half = out_one.shape[0]
    block = 3 * 2 * half
    low, high = range(block, block + half), range(block + half, block + 2 * half)
    one, two = both_sums(x_low, y_high, turned_ref, low, high, products, orbs)
    for k in range(half):
        out_one[k] = one(k).astype(jnp.bfloat16)
        out_two[k] = two(k).astype(jnp.bfloat16)


def second_across_kernel(orbs, upper_ref, x_low, x_high, y_low, y_high, out_one, out_two, turned_ref, *products):
    half = out_one.shape[0]
    block = 3 * 2 * half

    def between(one_ref, two_ref, lanes):
        one, two = both_sums(one_ref, two_ref, turned_ref, lanes, lanes, products, orbs)
        for k in range(half):
            out_one[k] = one(k).astype(jnp.bfloat16)
            out_two[k] = two(k).astype(jnp.bfloat16)

    @pl.when(upper_ref[0] == 0)
    def _():
        between(x_low, y_low, range(block, block + half))

    @pl.when(upper_ref[0] == 1)
    def _():
        between(x_high, y_high, range(block + half, block + 2 * half))


def own_coupled(weights, own, orbs, flops):
    half, _, pno = own[0].shape
    rows = 2 * half * pno
    shapes = (jax.ShapeDtypeStruct((2 * half, pno, pno), jnp.float32), jax.ShapeDtypeStruct((rows, orbs), jnp.bfloat16))
    scratch = [pltpu.VMEM((rows, rows), jnp.bfloat16)] * 2
    return call_kernel(own_kernel, shapes, scratch, "own_coupled", (weights,), own, flops)


def add_coupled(lanes, weights, own_t, acc, received, flops):
    rows = own_t.shape[0]
    scratch = [pltpu.VMEM((rows, rows), jnp.bfloat16)] * 2
    shape = jax.ShapeDtypeStruct(acc.shape, jnp.float32)
    body = functools.partial(coupled_kernel, lanes)
    return call_kernel(body, shape, scratch, "coupled", (weights,), (own_t, acc, *received), flops)


def across(body, name, scalars, vmem_args, orbs, flops):
    half, _, pno = vmem_args[0].shape
    wide = half * pno
    shapes = (jax.ShapeDtypeStruct((half, pno, pno), jnp.bfloat16),) * 2
    scratch = [pltpu.VMEM((2 * wide, orbs), jnp.bfloat16), *[pltpu.VMEM((wide, wide), jnp.bfloat16)] * 4]
    return call_kernel(functools.partial(body, orbs), shapes, scratch, name, scalars, vmem_args, flops)


def half_transforms(uses_ref, slab_refs, own_ref, store, base, pno):
    last = own_ref.shape[0] // pno - 1

    def rows(side):
        return own_ref[pl.ds(pl.multiple_of(jnp.minimum(side // 2, last) * pno, pno), pno), :]

    def both_sides(slab, k):
        one, two = uses_ref[k, 0], uses_ref[k, 1]
        bases = jnp.concatenate([rows(one), rows(two)], axis=0)
        both = lax.dot_general(slab, bases, (((1,), (1,)), ((), ())), preferred_element_type=jnp.float32)
        both = both.astype(jnp.bfloat16)
        store(k, 0, one, both[:, :pno])
        store(k, 1, two, both[:, pno:])

    for slab_ref in slab_refs:
        if slab_ref.shape[0] > 4:

            def step(k, carry, slab_ref=slab_ref, base=base):
                both_sides(slab_ref[k], base + k)
                return carry

            lax.fori_loop(0, slab_ref.shape[0], step, 0)
        else:
            for k in range(slab_ref.shape[0]):
                both_sides(slab_ref[k], base + k)
        base += slab_ref.shape[0]


def halves_kernel(base, uses_ref, *refs):
    *slab_refs, own_ref, half_ref = refs

    def store(k, use, side, half):
        half_ref[side] = half

    half_transforms(uses_ref, slab_refs, own_ref, store, base, half_ref.shape[2])


def more_halves_kernel(base, uses_ref, *refs):
    *slab_refs, own_ref, _, half_ref = refs
    halves_kernel(base, uses_ref, *slab_refs, own_ref, half_ref)


def exchange_kernel(scale, base, uses_ref, turn_ref, *refs):
    *slab_refs, own_ref, early_ref, out_ref, late_ref = refs

    def store(k, use, side, half):
        late_ref[2 * (k - base) + use] = half

    def half(p, side):
        k = turn_ref[2 * p + side]
        late = jnp.where(uses_ref[k, 0] == 2 * p + side, 0, 1) + 2 * jnp.maximum(k - base, 0)
        return jnp.where(k < base, early_ref[2 * p + side], late_ref[late])

    half_transforms(uses_ref, slab_refs, own_ref, store, base, out_ref.shape[1])
    for p in range(out_ref.shape[0]):
        product = lax.dot_general(half(p, 0), half(p, 1), (((0,), (0,)), ((), ())), preferred_element_type=jnp.float32)
        out_ref[p] = product * scale


def finish_kernel(upper_ref, acc_ref, rest_ref, low_ref, high_ref, row_ref, column_ref, out_ref):
    half = low_ref.shape[0]
    for p in range(out_ref.shape[0]):
        k, upper = p % half, p // half
        first = (low_ref, high_ref)[upper][k].astype(jnp.float32)
        second = jnp.where(upper_ref[0] == upper, row_ref[k], column_ref[k]).astype(jnp.float32)
        out_ref[p] = acc_ref[p] + rest_ref[p] + (first + second)


def half_products(uses, base, slabs, own_t, pno, done, flops):
    sides = own_t.shape[0] // pno * 2
    shape = jax.ShapeDtypeStruct((sides + 1, slabs[0].shape[1], pno), jnp.bfloat16)
    if done is None:
        return call_kernel(functools.partial(halves_kernel, base), shape, [], "halves", (uses,), (*slabs, own_t), flops)
    args = (*slabs, own_t, done)
    return call_kernel(
        functools.partial(more_halves_kernel, base), shape, [], "more_halves", (uses,), args, flops, aliases={len(args): 0}
    )


def exchange(uses, turn, base, slabs, own_t, early, shape):
    return call_kernel(
        functools.partial(exchange_kernel, 1.0 / math.sqrt(slabs[0].shape[1]), base),
        jax.ShapeDtypeStruct(shape, jnp.float32),
        [pltpu.VMEM((2 * sum(slab.shape[0] for slab in slabs),) + early.shape[1:], jnp.bfloat16)],
        "exchange",
        (uses, turn),
        (*slabs, own_t, early),
        EXCHANGE_COST,
    )


def finish(upper, acc, rest, backs):
    shape = jax.ShapeDtypeStruct(acc.shape, jnp.float32)
    return call_kernel(finish_kernel, shape, [], "finish", (upper,), (acc, rest, *backs), 0)


def pack_kernel(scale, chips, group_ref, me_ref, coupled_ref, length_ref, owner_ref, orbs_ref, base_ref, amp_ref, *refs):
    low_ref, high_ref, weight_ref, uses_ref, turn_ref, held_ref, sems = refs
    pairs, orbs, pno = base_ref.shape
    half = pairs // 2
    group, me = group_ref[0], me_ref[0]
    copies = []

    def copy(ref, k, row, sem):
        rows = pl.ds(row, ref.shape[1])
        copies.append(pltpu.make_async_copy(ref.at[pl.ds(k * half, half)], held_ref.at[k, :, rows], sems.at[sem]))
        copies[-1].start()

    for k in range(2):
        copy(base_ref, k, 0, 2 * k)
        copy(amp_ref, k, orbs, 2 * k + 1)
    assert pairs & (pairs - 1) == 0
    named = lax.broadcasted_iota(jnp.int32, (1, pno), 1) ^ (group * pairs)
    for p in range(pairs):
        counts = jnp.zeros((1, pno), jnp.float32)
        length = length_ref[p]
        for s in range(coupled_ref.shape[1]):
            counts += jnp.where(named == jnp.where(s < length, coupled_ref[p, s], -1), scale, 0.0)
        weight_ref[p : p + 1, :] = counts
        rows = slice(orbs + amp_ref.shape[1], held_ref.shape[2])
        held_ref[p // half, p % half, rows, :] = jnp.broadcast_to(counts, (16, pno)).astype(jnp.bfloat16)
    for started in copies:
        started.wait()
    stores = [
        pltpu.make_async_copy(held_ref.at[k], out_ref, sems.at[4 + k]) for k, out_ref in enumerate((low_ref, high_ref))
    ]
    for store in stores:
        store.start()

    sides = 2 * pairs

    def clear(k, carry):
        uses_ref[k, 0] = sides
        uses_ref[k, 1] = sides
        return carry

    lax.fori_loop(0, uses_ref.shape[0], clear, 0)
    for f in range(sides):
        position = owner_ref[orbs_ref[f % 2, f // 2]]
        k = position
        if chips <= RING_CHIPS:
            steps = lax.rem((me >> 1) - (position >> 1) + chips, chips)
            swapped = (position ^ me) & 1
            late = jnp.where(steps == 2, 5 + swapped, 4 + 3 * swapped)
            k = jnp.where(steps < 2, steps + 2 * swapped, late)
        turn_ref[f] = k
        uses_ref[k, 1] = uses_ref[k, 0]
        uses_ref[k, 0] = f
    for store in stores:
        store.wait()


def pack(group, me, chips, coupled, coupled_len, slab_owner, pair_orbs, bases, amps):
    pairs, orbs, pno = bases.shape
    packed = jax.ShapeDtypeStruct((pairs // 2, orbs + amps.shape[1] + 16, pno), bases.dtype)
    return pl.pallas_call(
        functools.partial(pack_kernel, orbs / pno, chips),
        out_shape=(
            packed,
            packed,
            jax.ShapeDtypeStruct((pairs, pno), jnp.float32),
            jax.ShapeDtypeStruct((slab_owner.shape[0], 2), jnp.int32),
            jax.ShapeDtypeStruct((2 * pairs,), jnp.int32),
        ),
        in_specs=[SMEM_SPEC] * 6 + [HBM_SPEC] * 2,
        out_specs=(HBM_SPEC, HBM_SPEC, VMEM_SPEC, SMEM_SPEC, SMEM_SPEC),
        scratch_shapes=[pltpu.VMEM((2,) + packed.shape, bases.dtype), pltpu.SemaphoreType.DMA((6,))],
        compiler_params=pltpu.CompilerParams(vmem_limit_bytes=PACK_LIMIT),
        name="pack",
    )(group, me, coupled, coupled_len, slab_owner, pair_orbs.T, bases, amps)


def after(value, *earlier):
    return lax.optimization_barrier((value,) + earlier)[0]


def on_device(integral_slabs, slab_owner, pair_orbs, domain_bases, amplitudes, coupled, coupled_len):
    n_grp, n_dev = lax.axis_size("grp"), lax.axis_size("dev")
    pairs, orbs, pno = domain_bases.shape
    group, me = lax.axis_index("grp"), lax.axis_index("dev")
    chips = n_dev // 2

    half = pairs // 2

    def along_x(value):
        return lax.ppermute(value, "grp", [(g, g ^ 1) for g in range(n_grp)])

    def along_y(value):
        return lax.ppermute(value, "grp", [(g, g ^ 2) for g in range(n_grp)])

    def along_chips(value, step):
        return lax.ppermute(value, "dev", [(d, (d + 2 * step) % n_dev) for d in range(n_dev)])

    def other_core(value):
        return lax.ppermute(value, "dev", [(d, d ^ 1) for d in range(n_dev)])

    *own, weights, uses, turns = pack(
        group.astype(jnp.int32).reshape(1), me.astype(jnp.int32).reshape(1), chips, coupled, coupled_len, slab_owner, pair_orbs, domain_bases, amplitudes
    )
    own_lo, own_hi = own
    upper = (group // 2).astype(jnp.int32).reshape(1)

    x_lo, y_hi = along_x(own_lo), along_y(own_hi)
    x_hi, y_lo = along_x(after(own_hi, own_lo)), along_y(after(own_lo, own_hi, x_lo))

    slab = integral_slabs[0]
    around = chips <= RING_CHIPS
    ahead = 5 if around else n_dev // 2
    acc, own_t = own_coupled(weights, own, orbs, OWN_COST)
    if around:
        below, above = along_chips(slab, 1), along_chips(slab, -1)
        halves = half_products(uses, 0, [slab[None], below[None]], own_t, pno, None, DECLARED)
        beyond = along_chips(below, 1)
        acc = after(acc, halves)
    else:
        gathered = lax.all_gather(slab, "dev", axis=0, tiled=False)
        halves = half_products(uses, 0, [gathered[:ahead]], own_t, pno, None, 0)
        rest = [gathered[ahead:]]

    lanes = [*range(pairs, pairs + half), *range(2 * pairs + half, 3 * pairs)]
    acc = add_coupled(lanes, weights, own_t, acc, (x_lo, y_hi), DECLARED)
    first = across(first_across_kernel, "first_across", (), (after(x_lo, acc), after(y_hi, acc)), orbs, FIRST_COST)
    back_low, back_high = along_x(first[0]), along_y(first[1])
    if around:
        swaps = [other_core(after(value, x_lo, y_hi)) for value in (slab, below)]
        more = [value[None] for value in (*swaps, above)]
        halves = half_products(uses, 2, more, after(own_t, first[0]), pno, halves, MORE_COST)
        beyond = after(beyond, halves)
        rest = [value[None] for value in (beyond, other_core(beyond), other_core(above))]
    rest_sum = exchange(uses, turns, ahead, rest, own_t, halves, acc.shape)
    second = across(
        second_across_kernel, "second_across", (upper,), (after(x_lo, rest_sum), x_hi, y_lo, y_hi), orbs, SECOND_COST
    )
    back_row, back_column = along_x(second[0]), along_y(second[1])
    lanes = [*range(pairs + half, 2 * pairs), *range(2 * pairs, 2 * pairs + half)]
    rest_sum = add_coupled(lanes, weights, own_t, after(rest_sum, second[0]), (x_hi, y_lo), LAST_COST)
    return finish(upper, acc, rest_sum, (back_low, back_high, back_row, back_column))


def solution(mesh):
    in_specs = (
        P("dev", None, None),
        P(),
        P(("grp", "dev"), None),
        P(("grp", "dev"), None, None),
        P(("grp", "dev"), None, None),
        P(("grp", "dev"), None),
        P(("grp", "dev")),
    )
    out_specs = P(("grp", "dev"), None, None)
    return jax.shard_map(
        on_device, mesh=mesh, in_specs=in_specs, out_specs=out_specs, check_vma=False
    )
```
